32 devices in a mesh: ax: 8 (over y, x, core), xs: 4 (over z).
Axes of the slice: x: 2, y: 2, z: 4, core: 2. Of those that a mesh axis runs over, the one named last changes fastest.
Arguments:
- populations: float32 [19, 32, 256, 256], P(None, 'ax', 'xs'), may hold values from 0.001 to 0.75, as said below
- fluid_mask: int32 [32, 256, 256], P('ax', 'xs'), may hold values 0 or 1
- patch_voxel: int32 [256, 512], P(('ax', 'xs')), may hold values from 0 to 65535
- patch_owner: int32 [256], P(('ax', 'xs')), may hold values from 0 to 3, as said below
- positions: float32 [256, 3, 512], P(('ax', 'xs')), may hold values from 0 to 5.5
- velocities: float32 [256, 3, 512], P(('ax', 'xs')), may hold values from -6 to 6
- pair_tiles: int32 [256, 8, 2], P(('ax', 'xs')), may hold values from 0 to 3
- pair_noise: bfloat16 [256, 8, 128, 128], P(('ax', 'xs')), may hold values from -6 to 6
Outputs:
- populations_out: float32 [19, 32, 256, 256], P(None, 'ax', 'xs')
- new_positions: float32 [256, 3, 512], P(('ax', 'xs'))
- new_velocities: float32 [256, 3, 512], P(('ax', 'xs'))
- drag_field: float32 [3, 32, 256, 256], P(None, 'ax', 'xs')
The draws below stay inside these ranges and needn't reach their ends.
Inputs may be any that keep to these rules, and one draw needn't show every extreme that they name: `patch_owner`: among the 8 patches of every device, each index along xs is named exactly 2 times. `populations`: every distribution is positive.
All inputs are finite; a program needn't handle non-finite values. No bound on the sum of `fluid_mask` on one device may be relied on, other than what follows from the above.
Results may differ from the reference program's by a relative error of at most 0.0003.
Values sent between devices are 32-bit elements; how exact they have to be, the bound alone decides.
No kernel may reach another device: no remote copies, remote signals or barrier semaphores. Data moves between devices by JAX's collectives and lax.ppermute only.
A program may use at most 128 MiB of HBM per device.

```python
import jax
import jax.numpy as jnp
from jax import lax

LX = 4
LY = 64
LZ = 256
PATCH_DEV = 8
NT = 4
PAIR_TILES = 8
TILE = 128
BEADS = 512
PER_OWNER = 2
NX = 32
NY = 256
PATCHES = 256
N_XS = 4


LATTICE_DIRS = [(0, 0, 0), (1, 0, 0), (-1, 0, 0), (0, 1, 0), (0, -1, 0), (0, 0, 1), (0, 0, -1), (1, 1, 0), (-1, -1, 0), (1, -1, 0), (-1, 1, 0), (1, 0, 1), (-1, 0, -1), (1, 0, -1), (-1, 0, 1), (0, 1, 1), (0, -1, -1), (0, 1, -1), (0, -1, 1)]


LATTICE_WEIGHTS = [1.0 / 3.0] + [1.0 / 18.0] * 6 + [1.0 / 36.0] * 12


def draw_populations(key, part):
    key_one, key_two, key_three = jax.random.split(key, 3)
    cells = (NX, NY, LZ)
    density = jax.random.uniform(key_one, cells, jnp.float32, 0.85, 1.15)
    flow = jnp.clip(0.03 * jax.random.normal(key_two, (3,) + cells, jnp.float32), -0.08, 0.08)
    rough = jax.random.uniform(key_three, (19,) + cells, jnp.float32, 0.92, 1.08)
    out = []
    for index in range(19):
        dirx, diry, dirz = LATTICE_DIRS[index]
        proj = dirx * flow[0] + diry * flow[1] + dirz * flow[2]
        out.append(LATTICE_WEIGHTS[index] * density * (1.0 + 3.0 * proj) * rough[index])
    return jnp.stack(out).astype(jnp.float32)


def draw_patch_owner(key, part):
    blocks = PATCHES // PATCH_DEV
    keys = jax.random.split(key, blocks)
    perms = jax.vmap(lambda subkey: jax.random.permutation(subkey, PATCH_DEV))(keys)
    return (perms // PER_OWNER).reshape(PATCHES).astype(jnp.int32)


def place_ends(result, key, smallest, largest):
    extent = result.shape
    spot = [jax.random.randint(jax.random.fold_in(key, axis), (), 0, extent[axis]) for axis in range(len(extent))]
    result = result.at[tuple(spot)].set(smallest)
    longest = extent.index(max(extent))
    spot[longest] = (spot[longest] + 1) % extent[longest]
    return result.at[tuple(spot)].set(largest)


def steps_of(stream_key, shape, cuts, least, largest):
    level, own = 1.0, jax.random.fold_in(stream_key, 6)
    for dim, blocks in cuts:
        heights = jnp.exp(jax.random.uniform(jax.random.fold_in(own, dim), (blocks,), jnp.float32, least / len(cuts), largest / len(cuts)))
        level = level * jnp.repeat(heights, shape[dim] // blocks).reshape([-1 if axis == dim else 1 for axis in range(len(shape))])
    return level


def scatter_about(key, extent, scale, most, cuts=(), kind=jnp.bfloat16):
    result = scale * jax.random.normal(key, extent, jnp.float32)
    if cuts:
        result = result * steps_of(key, extent, cuts, -0.22, 0.18)
    return jnp.clip(result, -most, most).astype(kind)


def setup_inputs(seed: int = 0) -> dict:
    key_list = jax.random.split(jax.random.key(seed), 9)
    populations = draw_populations(jax.random.fold_in(key_list[8], 71), 0)
    fluid_mask = place_ends((jax.random.randint(key_list[1], (NX, NY, LZ), 0, 8) < 7).astype(jnp.int32), jax.random.fold_in(key_list[1], 1), 0, 1)
    patch_voxel = place_ends(jax.random.randint(key_list[2], (PATCHES, BEADS), 0, LX * LY * LZ), jax.random.fold_in(key_list[2], 1), 0, (LX * LY * LZ) - 1).astype(jnp.int32)
    patch_owner = draw_patch_owner(jax.random.fold_in(key_list[8], 71), 0)
    positions = jnp.clip(5.5 * jax.random.uniform(key_list[4], (PATCHES, 3, BEADS), jnp.float32) ** steps_of(key_list[4], (PATCHES, 3, BEADS), ((0, 32),), -0.2, 0.2), 0.0, 5.5)
    velocities = scatter_about(key_list[5], (PATCHES, 3, BEADS), 1.0, 6.0, ((0, 32),), jnp.float32)
    pair_tiles = place_ends(jax.random.randint(key_list[6], (PATCHES, PAIR_TILES, 2), 0, NT), jax.random.fold_in(key_list[6], 1), 0, NT - 1).astype(jnp.int32)
    pair_noise = scatter_about(key_list[7], (PATCHES, PAIR_TILES, TILE, TILE), 1.0, 6.0, ((0, 32),))
    return {"populations": populations, "fluid_mask": fluid_mask, "patch_voxel": patch_voxel, "patch_owner": patch_owner, "positions": positions, "velocities": velocities, "pair_tiles": pair_tiles, "pair_noise": pair_noise}


LATTICE_DIRS = [(0, 0, 0), (1, 0, 0), (-1, 0, 0), (0, 1, 0), (0, -1, 0), (0, 0, 1), (0, 0, -1), (1, 1, 0), (-1, -1, 0), (1, -1, 0), (-1, 1, 0), (1, 0, 1), (-1, 0, -1), (1, 0, -1), (-1, 0, 1), (0, 1, 1), (0, -1, -1), (0, 1, -1), (0, -1, 1)]
LATTICE_WEIGHTS = [1.0 / 3.0] + [1.0 / 18.0] * 6 + [1.0 / 36.0] * 12
OPPOSITE_DIR = [0, 2, 1, 4, 3, 6, 5, 8, 7, 10, 9, 12, 11, 14, 13, 16, 15, 18, 17]
RELAX_TIME = 0.8
TIME_STEP = 0.04
REPULSION = 25.0
FRICTION = 4.5
NOISE_AMP = 3.0
DRAG_COEFF = 12.5
VELOCITY_SCALE = 20.0
SOFTENING = 0.01

def moments(dist):
    density = lax.optimization_barrier(jnp.sum(dist, axis=0))
    comps = []
    for axis in range(3):
        total = jnp.zeros_like(density)
        for index in range(19):
            sign = LATTICE_DIRS[index][axis]
            if sign != 0:
                total = total + sign * dist[index]
        comps.append(total / density)
    return (density, comps)

def collide(dist):
    density, comps = moments(dist)
    speed_sq = comps[0] * comps[0] + comps[1] * comps[1] + comps[2] * comps[2]
    out = []
    for index in range(19):
        dirx, diry, dirz = LATTICE_DIRS[index]
        proj = dirx * comps[0] + diry * comps[1] + dirz * comps[2]
        equil = LATTICE_WEIGHTS[index] * density * (1.0 + 3.0 * proj + 4.5 * proj * proj - 1.5 * speed_sq)
        out.append(dist[index] - (dist[index] - equil) / RELAX_TIME)
    return jnp.stack(out)

def stream_padded(padded, post):
    size_x, size_y, size_z = (post.shape[1], post.shape[2], post.shape[3])
    out = []
    for index in range(19):
        dirx, diry, dirz = LATTICE_DIRS[index]
        start_x, start_y, start_z = (1 - dirx, 1 - diry, 1 - dirz)
        source = padded[index, start_x:start_x + size_x, start_y:start_y + size_y, start_z:start_z + size_z]
        source_mask = padded[19, start_x:start_x + size_x, start_y:start_y + size_y, start_z:start_z + size_z]
        out.append(jnp.where(source_mask > 0.5, source, post[OPPOSITE_DIR[index]]))
    return jnp.stack(out)

def lattice_step(dist, fluid):
    post = collide(dist)
    stacked = jnp.concatenate([post, fluid[None]], axis=0)
    wrapped = jnp.concatenate([stacked[:, -1:], stacked, stacked[:, :1]], axis=1)
    padded = jnp.pad(wrapped, ((0, 0), (0, 0), (1, 1), (1, 1)))
    return stream_padded(padded, post)

def pair_forces(position, velocity, pair_list, noise):
    tile = noise.shape[-1]
    count = position.shape[1] // tile
    pos_tiles = position.reshape(3, count, tile)
    vel_tiles = velocity.reshape(3, count, tile)

    def one_pair(carry, item):
        pair, noise_tile = item
        pos_a = lax.dynamic_index_in_dim(pos_tiles, pair[0], 1, keepdims=False)
        pos_b = lax.dynamic_index_in_dim(pos_tiles, pair[1], 1, keepdims=False)
        vel_a = lax.dynamic_index_in_dim(vel_tiles, pair[0], 1, keepdims=False)
        vel_b = lax.dynamic_index_in_dim(vel_tiles, pair[1], 1, keepdims=False)
        delta = pos_a[:, :, None] - pos_b[:, None, :]
        distance = jnp.sqrt(lax.optimization_barrier(jnp.sum(delta * delta, axis=0)) + SOFTENING)
        weight = jnp.maximum(0.0, 1.0 - distance)
        unit = delta / distance
        along = lax.optimization_barrier(jnp.sum(unit * (vel_a[:, :, None] - vel_b[:, None, :]), axis=0))
        scalar = REPULSION * weight - FRICTION * weight * weight * along + NOISE_AMP * weight * noise_tile.astype(jnp.float32) / jnp.sqrt(TIME_STEP)
        force = lax.optimization_barrier(jnp.sum(scalar[None] * unit, axis=2))
        current = lax.dynamic_index_in_dim(carry, pair[0], 1, keepdims=False)
        carry = lax.dynamic_update_index_in_dim(carry, current + force, pair[0], 1)
        return (carry, None)
    start = jnp.zeros((3, count, tile), jnp.float32)
    total, unused = lax.scan(one_pair, start, (pair_list, noise))
    return total.reshape(3, count * tile)

def patch_step(item):
    position, velocity, flow, pair_list, noise = item
    drag = DRAG_COEFF * (flow - velocity)
    new_vel = velocity + TIME_STEP * (pair_forces(position, velocity, pair_list, noise) + drag)
    new_pos = position + TIME_STEP * new_vel
    return (new_pos, new_vel, -TIME_STEP * drag)

def reference(populations, fluid_mask, patch_voxel, patch_owner, positions, velocities, pair_tiles, pair_noise):
    fluid = fluid_mask.astype(jnp.float32)
    dist = populations
    for step in range(2):
        dist = lattice_step(dist, fluid)
    density, comps = moments(dist)
    velocity_flat = VELOCITY_SCALE * jnp.stack(comps).reshape(3, NX * NY * LZ)
    blocks = PATCHES // PATCH_DEV
    owner_rows = patch_owner.reshape(blocks, PATCH_DEV)
    onehot = (owner_rows[:, :, None] == jnp.arange(N_XS, dtype=jnp.int32)[None, None, :]).astype(jnp.int32)
    rank = lax.optimization_barrier(jnp.sum(onehot * (jnp.cumsum(onehot, axis=1) - 1), axis=2))
    block_ids = jnp.arange(blocks, dtype=jnp.int32)[:, None]
    axial_idx = block_ids // N_XS
    cross_idx = block_ids % N_XS
    dest = ((axial_idx * N_XS + owner_rows) * PATCH_DEV + cross_idx * PER_OWNER + rank).reshape(PATCHES).astype(jnp.int32)
    row_block = (jnp.arange(PATCHES, dtype=jnp.int32) // PATCH_DEV)[:, None]
    local_x = patch_voxel // (LY * LZ)
    local_y = patch_voxel // LZ % LY
    local_z = patch_voxel % LZ
    global_id = ((row_block // N_XS * LX + local_x) * NY + row_block % N_XS * LY + local_y) * LZ + local_z
    global_id = global_id.astype(jnp.int32)
    at_source = jnp.transpose(velocity_flat[:, global_id], (1, 0, 2))
    owned = jnp.zeros_like(at_source).at[dest].set(at_source)
    new_pos, new_vel, reaction = lax.map(patch_step, (positions, velocities, owned, pair_tiles, pair_noise))
    back = reaction[dest]
    flat_ids = global_id.reshape(-1)
    field = jnp.stack([jax.ops.segment_sum(back[:, comp, :].reshape(-1), flat_ids, num_segments=NX * NY * LZ) for comp in range(3)])
    return (dist, new_pos, new_vel, field.reshape(3, NX, NY, LZ))
```

```python
import functools

import jax
import jax.numpy as jnp
from jax import lax
from jax.experimental import pallas as pl
from jax.experimental.pallas import tpu as pltpu
from jax.sharding import PartitionSpec as P

DIRS = [
    (0, 0, 0),
    (1, 0, 0),
    (-1, 0, 0),
    (0, 1, 0),
    (0, -1, 0),
    (0, 0, 1),
    (0, 0, -1),
    (1, 1, 0),
    (-1, -1, 0),
    (1, -1, 0),
    (-1, 1, 0),
    (1, 0, 1),
    (-1, 0, -1),
    (1, 0, -1),
    (-1, 0, 1),
    (0, 1, 1),
    (0, -1, -1),
    (0, 1, -1),
    (0, -1, 1),
]
OPP = [0, 2, 1, 4, 3, 6, 5, 8, 7, 10, 9, 12, 11, 14, 13, 16, 15, 18, 17]
CX_PLUS = [k for k in range(19) if DIRS[k][0] == 1]
CX_MINUS = [k for k in range(19) if DIRS[k][0] == -1]
CY_PLUS = [k for k in range(19) if DIRS[k][1] == 1]
CY_MINUS = [k for k in range(19) if DIRS[k][1] == -1]
F32 = jnp.float32
BF16 = jnp.bfloat16
I32 = jnp.int32
VMEM_SPEC = pl.BlockSpec(memory_space=pltpu.VMEM)
SMEM_SPEC = pl.BlockSpec(memory_space=pltpu.SMEM)
ANY_SPEC = pl.BlockSpec(memory_space=pl.ANY)

ROWS = 64
PAD = 88
TILES = ROWS // 8


def params(mib=48):
    return pltpu.CompilerParams(vmem_limit_bytes=mib * 1024 * 1024)


def cost(flops, bytes_accessed):
    return pl.CostEstimate(flops=flops, bytes_accessed=bytes_accessed, transcendentals=0)


def velocity_of(f):
    diff = [None] + [f[k] - f[k + 1] for k in range(1, 19, 2)]
    rho = f[0]
    for k in range(1, 19):
        rho = rho + f[k]
    m1, m3, m5, m7, m9, m11, m13, m15, m17 = diff[1:]
    jx = m1 + m7 + m9 + m11 + m13
    jy = m3 + m7 - m9 + m15 + m17
    jz = m5 + m11 - m13 + m15 - m17
    inv = 1.0 / rho
    return rho, jx * inv, jy * inv, jz * inv


def collide(f):
    rho, ux, uy, uz = velocity_of(f)
    base = (1.25 * rho) * (1.0 - 1.5 * (ux * ux + uy * uy + uz * uz))
    ux, uy, uz = 1.5 * ux, 1.5 * uy, 1.5 * uz
    even1, even2 = base * (1.0 / 18.0), base * (1.0 / 36.0)
    odd1, odd2 = rho * (2.5 / 18.0), rho * (2.5 / 36.0)
    out = [None] * 19
    out[0] = base * (1.0 / 3.0) - 0.25 * f[0]
    for k in range(1, 19, 2):
        dx, dy, dz = DIRS[k]
        proj = None
        for sign, comp in ((dx, ux), (dy, uy), (dz, uz)):
            if sign == 0:
                continue
            if proj is None:
                proj = comp
            else:
                proj = proj + comp if sign > 0 else proj - comp
        even, odd = (even1, odd1) if k < 7 else (even2, odd2)
        odd = odd * proj
        even = even + odd * proj
        out[k] = (even + odd) - 0.25 * f[k]
        out[k + 1] = (even - odd) - 0.25 * f[k + 1]
    return out


def shifted(read, tile, dy, dz):
    here = read(tile)
    if dy != 0:
        sub = lax.broadcasted_iota(I32, here.shape, 0)
        if dy > 0:
            here = pltpu.roll(jnp.where(sub == 7, read(tile - 1), here), 1, 0)
        else:
            here = pltpu.roll(jnp.where(sub == 0, read(tile + 1), here), 7, 0)
    if dz != 0:
        here = pltpu.roll(here, 1 if dz > 0 else here.shape[1] - 1, 1)
    return here


def rows_of(tile):
    return pl.ds(pl.multiple_of(8 + 8 * tile, 8), 8)


def open_bits(read_mask, tile):
    bits = None
    cache = {}
    for k in range(1, 19):
        dx, dy, dz = DIRS[k]
        if (dx, dy) not in cache:
            cache[(dx, dy)] = shifted(functools.partial(read_mask, dx), tile, dy, 0)
        m = cache[(dx, dy)]
        if dz != 0:
            lane = lax.broadcasted_iota(I32, m.shape, 1)
            last = m.shape[1] - 1
            m = pltpu.roll(m, 1 if dz > 0 else last, 1)
            m = jnp.where(lane == (0 if dz > 0 else last), 0, m)
        m = m << k
        bits = m if bits is None else bits | m
    return bits


def stream(read, own, bits, tile):
    out = [own[0]]
    for k in range(1, 19):
        dx, dy, dz = DIRS[k]
        source = shifted(functools.partial(read, k, dx), tile, dy, dz)
        out.append(jnp.where((bits & (1 << k)) != 0, source, own[OPP[k]]))
    return out


def collide_kernel(n, per, pop, mask, vel, post, fwd, bwd, up, down, *others):
    x = pl.program_id(0)
    last = pl.num_programs(0) - 1

    def body(t, carry):
        rows = pl.ds(pl.multiple_of(8 * t, 8), 8)
        out = collide([pop[k, 0, rows, :] for k in range(19)])
        for k in range(19):
            post[k, 0, rows, :] = out[k]
        return carry

    lax.fori_loop(0, TILES, body, 0)
    for ref, near, beyond, dirs in ((up, ROWS - 1, ROWS - 2, CY_PLUS), (down, 0, 1, CY_MINUS)):
        for k in range(19):
            ref[x, k : k + 1, :] = post[k, 0, near : near + 1, :]
        for j, k in enumerate(dirs):
            ref[x, 19 + j : 20 + j, :] = post[k, 0, beyond : beyond + 1, :]
        ref[x, 24:25, :] = mask[0, near : near + 1, :].astype(F32)
        ref[x, 25:26, :] = mask[0, beyond : beyond + 1, :].astype(F32)

    def faces(ref, dirs):
        for j, k in enumerate(dirs):
            ref[j * ROWS : (j + 1) * ROWS, :] = post[k, 0]
        ref[5 * ROWS : 6 * ROWS, :] = mask[0].astype(F32)

    @pl.when(x == last)
    def _():
        faces(fwd, CX_PLUS)

    @pl.when(x == 0)
    def _():
        faces(bwd, CX_MINUS)
        me = lax.axis_index("xs")
        for d in range(1, n):
            target = lax.rem(me + d, n)
            for r in range(per):
                rows = vel[target * per + r]
                for c in range(3):
                    for half in range(2):
                        i = (r * 3 + c) * 2 + half
                        piece = rows[c : c + 1, half * 256 : (half + 1) * 256]
                        if d in (1, n - 1):
                            ref = up if d == 1 else down
                            ref[i // 3, 26 + i % 3 : 27 + i % 3, :] = piece
                        else:
                            others[d - 2][i : i + 1, :] = piece


def sent_velocity(refs, n, d, r, c):
    out = []
    for half in range(2):
        i = (r * 3 + c) * 2 + half
        if d in (1, n - 1):
            out.append(refs[d - 1][i // 3, 26 + i % 3 : 27 + i % 3, :])
        else:
            out.append(refs[d - 1][i : i + 1, :])
    return jnp.concatenate(out, axis=1)


def border_flags(n):
    me = lax.axis_index("xs")
    return (me > 0).astype(F32), (me < n - 1).astype(F32)


def edges_kernel(n, nx, fwd_in, bwd_in, below, above, fwd, bwd, rows, sems):
    has_below, has_above = border_flags(n)
    for i, (x, dirs, far_below, far_above) in enumerate(
        ((nx - 1, CX_PLUS, 7, 9), (0, CX_MINUS, 10, 8))
    ):
        for j, k in enumerate(dirs):
            rows[i, j : j + 1, :] = below[x, k : k + 1, :]
            rows[i, 8 + j : 9 + j, :] = above[x, k : k + 1, :]
        j = 19 + CY_PLUS.index(far_below)
        rows[i, 5:6, :] = below[x, j : j + 1, :]
        j = 19 + CY_MINUS.index(far_above)
        rows[i, 13:14, :] = above[x, j : j + 1, :]
        rows[i, 6:8, :] = below[x, 24:26, :] * has_below
        rows[i, 14:16, :] = above[x, 24:26, :] * has_above
    copies = [
        pltpu.make_async_copy(rows.at[i], ref.at[pl.ds(6 * ROWS, 16)], sems.at[i])
        for i, ref in enumerate((fwd, bwd))
    ]
    for copy in copies:
        copy.start()
    for copy in copies:
        copy.wait()


def fill_edges(pad, below, above, layers):
    for x, dirs in layers:
        for k in dirs:
            pad[k, x, 79:80, :] = below[x, k : k + 1, :]
            pad[k, x, 72:73, :] = above[x, k : k + 1, :]
            if k in CY_PLUS:
                j = 19 + CY_PLUS.index(k)
                pad[k, x, 7:8, :] = below[x, k : k + 1, :]
                pad[k, x, 78:79, :] = below[x, j : j + 1, :]
            if k in CY_MINUS:
                j = 19 + CY_MINUS.index(k)
                pad[k, x, 73:74, :] = above[x, j : j + 1, :]
                pad[k, x, 80:81, :] = pad[k, x, 8:9, :]


def fill_mask(n, nx, pad, mask, below, above):
    has_below, has_above = border_flags(n)
    for x in range(nx):
        pad[x, 8:72, :] = mask[x]
        near = (below[x, 24:25, :] * has_below).astype(I32)
        pad[x, 79:80, :] = near
        pad[x, 7:8, :] = near
        pad[x, 78:79, :] = (below[x, 25:26, :] * has_below).astype(I32)
        pad[x, 72:73, :] = (above[x, 24:25, :] * has_above).astype(I32)
        pad[x, 73:74, :] = (above[x, 25:26, :] * has_above).astype(I32)
        pad[x, 80:81, :] = mask[x, 0:1, :]


def run_copies(copies):
    for copy in copies:
        copy.start()
    for copy in copies:
        copy.wait()


def middle_kernel(n, nx, post, mask, below, above, post2, bits_out, pad, flags, sems):
    run_copies(
        [
            pltpu.make_async_copy(post.at[:, x], pad.at[:, x, pl.ds(8, ROWS)], sems.at[x])
            for x in range(nx)
        ]
    )
    fill_edges(pad, below, above, [(x, range(19)) for x in range(nx)])
    fill_mask(n, nx, flags, mask, below, above)
    for x in range(1, nx - 1):

        def body(t, carry, x=x):
            bits = open_bits(lambda dx, tile: flags[x - dx, rows_of(tile), :], t)
            own = [pad[k, x, rows_of(t), :] for k in range(19)]
            f = stream(lambda k, dx, tile: pad[k, x - dx, rows_of(tile), :], own, bits, t)
            out = collide(f)
            for k in range(19):
                post2[k, x - 1, rows_of(t), :] = out[k]
            bits_out[x - 1, pl.ds(pl.multiple_of(8 * t, 8), 8), :] = bits
            return carry

        lax.fori_loop(0, TILES + 1, body, 0)
        for k in CY_PLUS:
            post2[k, x - 1, 7:8, :] = post2[k, x - 1, 79:80, :]


def outer_kernel(
    n, nx, post, mask, below, above, before, after, post2, bits_out, fwd2, bwd2, pad, halo, flags, halo_flags, edge, sems
):
    last = nx - 1
    copies = []

    def add(src, dst):
        copies.append(pltpu.make_async_copy(src, dst, sems.at[len(copies)]))

    body_rows = pl.ds(8, ROWS)
    add(post.at[:, 0], pad.at[:, 0, body_rows])
    add(post.at[:, last], pad.at[:, last, body_rows])
    for x, dirs in ((1, CX_MINUS), (last - 1, CX_PLUS)):
        for k in dirs:
            add(post.at[k, x], pad.at[k, x, body_rows])
    for i, ref in enumerate((before, after)):
        for j in range(5):
            add(ref.at[pl.ds(j * ROWS, ROWS)], halo.at[i, j, body_rows])
        add(ref.at[pl.ds(5 * ROWS, ROWS)], halo_flags.at[i, body_rows])
        add(ref.at[pl.ds(6 * ROWS, 16)], edge.at[i])
    run_copies(copies)
    fill_edges(
        pad, below, above, [(0, range(19)), (last, range(19)), (1, CX_MINUS), (last - 1, CX_PLUS)]
    )
    fill_mask(n, nx, flags, mask, below, above)
    for i, (dirs, far_below, far_above) in enumerate(((CX_PLUS, 7, 9), (CX_MINUS, 10, 8))):
        for j, k in enumerate(dirs):
            halo[i, j, 79:80, :] = edge[i, j : j + 1, :]
            halo[i, j, 72:73, :] = edge[i, 8 + j : 9 + j, :]
            if k == far_below:
                halo[i, j, 7:8, :] = edge[i, j : j + 1, :]
                halo[i, j, 78:79, :] = edge[i, 5:6, :]
            if k == far_above:
                halo[i, j, 73:74, :] = edge[i, 13:14, :]
                halo[i, j, 80:81, :] = halo[i, j, 8:9, :]
        halo_flags[i, 79:80, :] = edge[i, 6:7, :]
        halo_flags[i, 7:8, :] = edge[i, 6:7, :]
        halo_flags[i, 78:79, :] = edge[i, 7:8, :]
        halo_flags[i, 72:73, :] = edge[i, 14:15, :]
        halo_flags[i, 73:74, :] = edge[i, 15:16, :]
        halo_flags[i, 80:81, :] = halo_flags[i, 8:9, :]
    for i, x in enumerate((0, last)):

        def read(k, dx, tile, i=i, x=x):
            if x - dx < 0:
                return halo[0, CX_PLUS.index(k), rows_of(tile), :]
            if x - dx > last:
                return halo[1, CX_MINUS.index(k), rows_of(tile), :]
            return pad[k, x - dx, rows_of(tile), :]

        def read_mask(dx, tile, i=i, x=x):
            if x - dx < 0 or x - dx > last:
                return halo_flags[0 if x - dx < 0 else 1, rows_of(tile), :].astype(I32)
            return flags[x - dx, rows_of(tile), :]

        def body(t, carry, i=i, x=x, read=read, read_mask=read_mask):
            bits = open_bits(read_mask, t)
            own = [pad[k, x, rows_of(t), :] for k in range(19)]
            out = collide(stream(read, own, bits, t))
            for k in range(19):
                post2[k, i, rows_of(t), :] = out[k]
            bits_out[i, pl.ds(pl.multiple_of(8 * t, 8), 8), :] = bits
            return carry

        lax.fori_loop(0, TILES + 1, body, 0)
        for k in CY_PLUS:
            post2[k, i, 7:8, :] = post2[k, i, 79:80, :]
    for i, ref, dirs, k_below, k_above in ((1, fwd2, CX_PLUS, 7, 9), (0, bwd2, CX_MINUS, 10, 8)):
        for j, k in enumerate(dirs):
            ref[j * ROWS : (j + 1) * ROWS, :] = post2[k, i, 8:72, :]
        ref[320:321, :] = post2[k_below, i, 79:80, :]
        ref[321:322, :] = post2[k_above, i, 72:73, :]


def store_flow(flow, i, t, f):
    rho, ux, uy, uz = velocity_of(f)
    rows = pl.ds(pl.multiple_of(8 * t, 8), 8)
    flow[0, i, rows, :] = ux
    flow[1, i, rows, :] = uy
    flow[2, i, rows, :] = uz


def final_middle_kernel(nx, post2, outer, bits, out, flow, halo, result, sems):
    copies = [
        pltpu.make_async_copy(outer.at[k, i], halo.at[i, j], sems.at[i * 5 + j])
        for i, dirs in ((0, CX_PLUS), (1, CX_MINUS))
        for j, k in enumerate(dirs)
    ]
    run_copies(copies)
    stores = []
    for x in range(1, nx - 1):

        def read(k, dx, tile, x=x):
            if x - dx == 0:
                return halo[0, CX_PLUS.index(k), rows_of(tile), :]
            if x - dx == nx - 1:
                return halo[1, CX_MINUS.index(k), rows_of(tile), :]
            return post2[k, x - dx - 1, rows_of(tile), :]

        def body(t, carry, x=x, read=read):
            rows = pl.ds(pl.multiple_of(8 * t, 8), 8)
            own = [post2[k, x - 1, rows_of(t), :] for k in range(19)]
            f = stream(read, own, bits[x - 1, rows, :], t)
            for k in range(19):
                result[k, x - 1, rows, :] = f[k]
            store_flow(flow, x - 1, t, f)
            return carry

        lax.fori_loop(0, TILES, body, 0)
        copy = pltpu.make_async_copy(result.at[:, x - 1], out.at[:, x], sems.at[10 + x])
        copy.start()
        stores.append(copy)
    for copy in stores:
        copy.wait()


def final_outer_kernel(nx, out_in, post2, middle, bits, before, after, out, flow, halo, near, result, sems):
    last = nx - 1
    copies = []

    def add(src, dst):
        copies.append(pltpu.make_async_copy(src, dst, sems.at[len(copies)]))

    for i, ref in enumerate((before, after)):
        for j in range(5):
            add(ref.at[pl.ds(j * ROWS, ROWS)], halo.at[i, j, pl.ds(8, ROWS)])
        add(ref.at[pl.ds(5 * ROWS, 8)], halo.at[i, 5, pl.ds(8, 8)])
    for i, (x, dirs) in enumerate(((1, CX_MINUS), (last - 1, CX_PLUS))):
        for j, k in enumerate(dirs):
            add(middle.at[k, x - 1], near.at[i, j])
    run_copies(copies)
    for i, (dirs, k_below, k_above) in enumerate(((CX_PLUS, 7, 9), (CX_MINUS, 10, 8))):
        halo[i, dirs.index(k_below), 7:8, :] = halo[i, 5, 8:9, :]
        halo[i, dirs.index(k_above), 72:73, :] = halo[i, 5, 9:10, :]
    stores = []
    for i, x in enumerate((0, last)):

        def read(k, dx, tile, i=i, x=x):
            if x - dx < 0:
                return halo[0, CX_PLUS.index(k), rows_of(tile), :]
            if x - dx > last:
                return halo[1, CX_MINUS.index(k), rows_of(tile), :]
            if dx == 0:
                return post2[k, i, rows_of(tile), :]
            dirs = CX_MINUS if x == 0 else CX_PLUS
            return near[i, dirs.index(k), rows_of(tile), :]

        def body(t, carry, i=i, x=x, read=read):
            rows = pl.ds(pl.multiple_of(8 * t, 8), 8)
            own = [post2[k, i, rows_of(t), :] for k in range(19)]
            f = stream(read, own, bits[i, rows, :], t)
            for k in range(19):
                result[k, i, rows, :] = f[k]
            store_flow(flow, i, t, f)
            return carry

        lax.fori_loop(0, TILES, body, 0)
        copy = pltpu.make_async_copy(result.at[:, i], out.at[:, x], sems.at[len(copies) + i])
        copy.start()
        stores.append(copy)
    for copy in stores:
        copy.wait()


def pair_kernel(pair_tiles, pos, vel, noise, base, rows, cols, acc):
    g = pl.program_id(0)
    tile = noise.shape[-1]
    count = pos.shape[-1] // tile
    pairs = noise.shape[1]
    x, v = pos[0], vel[0]
    both = jnp.concatenate([x, 4.5 * v, jnp.zeros((2, x.shape[1]), F32)], axis=0)
    turned = both.T
    for c in range(6):
        for j in range(count):
            part = turned[j * tile : (j + 1) * tile, c : c + 1]
            cols[c, j] = jnp.broadcast_to(part, (tile, tile))
            rows[c, j] = jnp.broadcast_to(both[c : c + 1, j * tile : (j + 1) * tile], (8, tile))
    acc[...] = jnp.zeros_like(acc)
    eye = lax.broadcasted_iota(I32, (tile, tile), 0) == lax.broadcasted_iota(I32, (tile, tile), 1)
    scale = jnp.where(eye, 15.0, 0.0).astype(BF16)

    def one_pair(p, carry):
        first = pair_tiles[g, p, 0]
        second = pair_tiles[g, p, 1]
        theta = lax.dot_general(
            scale, noise[0, p], (((1,), (1,)), ((), ())), preferred_element_type=F32
        )
        mine = [rows[c, first] for c in range(6)]
        total = [acc[first, c] for c in range(3)]
        for s in range(tile // 8):
            part = slice(8 * s, 8 * s + 8)
            dx, dy, dz = [mine[c] - cols[c, second, part, :] for c in range(3)]
            vx, vy, vz = [mine[c] - cols[c, second, part, :] for c in range(3, 6)]
            square = (dx * dx + 0.01) + (dy * dy + dz * dz)
            close = jnp.maximum(lax.rsqrt(square) - 1.0, 0.0)
            along = dx * vx + dy * vy + dz * vz
            force = close * ((theta[part, :] + 25.0) - close * along)
            total = [total[0] + force * dx, total[1] + force * dy, total[2] + force * dz]
        for c in range(3):
            acc[first, c] = total[c]
        return carry

    lax.fori_loop(0, pairs, one_pair, 0)
    for j in range(count):
        lanes = slice(j * tile, (j + 1) * tile)
        for c in range(3):
            force = jnp.sum(acc[j, c], axis=0, keepdims=True)
            base[0, c : c + 1, lanes] = 0.5 * v[c : c + 1, lanes] + 0.04 * force


def split(value):
    high = value.astype(BF16)
    return high, (value - high.astype(F32)).astype(BF16)


def ranks(owner, count):
    out = []
    for g in range(count):
        rank = jnp.int32(0)
        for h in range(g):
            rank = rank + (owner[h] == owner[g]).astype(I32)
        out.append(rank)
    return out


def one_hot(index, extent):
    want = index.astype(F32).astype(BF16)
    place = lax.broadcasted_iota(I32, (extent, index.shape[1]), 0).astype(F32).astype(BF16)
    return place == want


def scatter_kernel(n, per, owner, voxel, vel, *refs):
    sent, out, table = refs[: n - 1], refs[n - 1], refs[n]
    me = lax.axis_index("xs")
    beads = voxel.shape[1]
    for r in range(per):
        table[me, r, 0:3, :] = vel[me * per + r]
        for d in range(1, n):
            source = lax.rem(me + n - d, n)
            for c in range(3):
                table[source, r, c : c + 1, :] = sent_velocity(sent, n, d, r, c)
    out[...] = jnp.zeros_like(out)
    rank = ranks(owner, voxel.shape[0])
    one, zero = BF16(1), BF16(0)
    for g in range(voxel.shape[0]):
        index = voxel[g : g + 1, :]
        lanes = jnp.where(one_hot(index & 255, 256), one, zero)
        at_row = one_hot(index >> 8, out.shape[1])
        values = table[owner[g], rank[g]]
        lanes2 = jnp.concatenate([lanes, lanes], axis=1)
        for c in range(3):
            high, low = split(values[c : c + 1, :])
            left = jnp.concatenate(
                [jnp.where(at_row, high, zero), jnp.where(at_row, low, zero)], axis=1
            )
            out[c] += lax.dot_general(
                left, lanes2, (((1,), (1,)), ((), ())), preferred_element_type=F32
            )
        out[3] += lax.dot_general(
            jnp.where(at_row, one, zero), lanes, (((1,), (1,)), ((), ())), preferred_element_type=F32
        )


def gather_kernel(n, per, owner, voxel, middle, outer, *refs):
    outs, table, field = refs[:n], refs[n], refs[n + 1]
    me = lax.axis_index("xs")
    patches = voxel.shape[0]
    inner = middle.shape[1]
    rows = (inner + 2) * ROWS
    for c in range(3):
        layers = [outer[c, 0]] + [middle[c, i] for i in range(inner)] + [outer[c, 1]]
        for x, layer in enumerate(layers):
            high, low = split(layer)
            field[c, x * ROWS : (x + 1) * ROWS, 0:256] = high
            field[c, x * ROWS : (x + 1) * ROWS, 256:512] = low
    one, zero = BF16(1), BF16(0)
    for g in range(patches):
        index = voxel[g : g + 1, :]
        lanes = jnp.where(one_hot(index & 255, 256), one, zero)
        lanes2 = jnp.concatenate([lanes, lanes], axis=0)
        at_row = lax.broadcasted_iota(I32, (rows, index.shape[1]), 0) == (index >> 8)
        for c in range(3):
            found = lax.dot_general(
                field[c], lanes2, (((1,), (0,)), ((), ())), preferred_element_type=F32
            )
            table[g, c : c + 1, :] = jnp.sum(jnp.where(at_row, found, 0.0), axis=0, keepdims=True)
    rank = ranks(owner, patches)
    for d in range(n):
        target = lax.rem(me + d, n)
        for r in range(per):
            found = jnp.int32(0)
            for g in range(patches):
                found = jnp.where((owner[g] == target) & (rank[g] == r), g, found)
            outs[d][r] = table[found, 0:3, :]


def field_kernel(total, middle, outer, field):
    nx = field.shape[1]
    for x in range(nx):
        rows = slice(x * ROWS, (x + 1) * ROWS)
        number = 10.0 * total[3, rows, :]
        for c in range(3):
            if x == 0 or x == nx - 1:
                speed = outer[c, 0 if x == 0 else 1]
            else:
                speed = middle[c, x - 1]
            field[c, x] = 0.5 * total[c, rows, :] - number * speed


def final_kernel(n, per, pos, base, *refs):
    flows, new_pos, new_vel = refs[:n], refs[n], refs[n + 1]
    me = lax.axis_index("xs")
    for d in range(n):
        source = lax.rem(me + n - d, n)
        for r in range(per):
            i = source * per + r
            speed = base[i] + 10.0 * flows[d][r]
            new_vel[i] = speed
            new_pos[i] = pos[i] + 0.04 * speed


def shift(value, axis, by):
    n = lax.axis_size(axis)
    return lax.ppermute(value, axis, [(i, (i + by) % n) for i in range(n)])


def per_device(
    populations, fluid_mask, patch_voxel, patch_owner, positions, velocities, pair_tiles, pair_noise
):
    n = lax.axis_size("xs")
    patches, beads = patch_voxel.shape
    per = patches // n
    nx = populations.shape[1]
    lanes = populations.shape[3]
    sds = jax.ShapeDtypeStruct
    vmem, dma = pltpu.VMEM, pltpu.SemaphoreType.DMA

    layer = lambda x: (0, x, 0, 0)
    whole2 = lambda x: (0, 0)
    whole3 = lambda x: (0, 0, 0)
    post, fwd, bwd, *sending = pl.pallas_call(
        functools.partial(collide_kernel, n, per),
        grid=(nx,),
        in_specs=[
            pl.BlockSpec((19, 1, ROWS, lanes), layer),
            pl.BlockSpec((1, ROWS, lanes), lambda x: (x, 0, 0)),
            pl.BlockSpec((patches, 3, beads), whole3),
        ],
        out_specs=[
            pl.BlockSpec((19, 1, ROWS, lanes), layer),
            pl.BlockSpec((400, lanes), whole2),
            pl.BlockSpec((400, lanes), whole2),
            pl.BlockSpec((nx, 32, lanes), whole3),
            pl.BlockSpec((nx, 32, lanes), whole3),
        ]
        + [pl.BlockSpec((16, lanes), whole2)] * (n - 3),
        out_shape=[
            sds(populations.shape, F32),
            sds((400, lanes), F32),
            sds((400, lanes), F32),
            sds((nx, 32, lanes), F32),
            sds((nx, 32, lanes), F32),
        ]
        + [sds((16, lanes), F32)] * (n - 3),
        compiler_params=params(),
        cost_estimate=cost(12_000_000, 11_000_000),
        name="collide_first",
    )(populations, fluid_mask, velocities)
    up, down, *others = sending
    below = shift(up, "xs", 1)
    above = shift(down, "xs", -1)
    sent = [below] + [shift(other, "xs", d + 2) for d, other in enumerate(others)] + [above]

    base = pl.pallas_call(
        pair_kernel,
        grid_spec=pltpu.PrefetchScalarGridSpec(
            num_scalar_prefetch=1,
            grid=(patches,),
            in_specs=[
                pl.BlockSpec((1, 3, beads), lambda g, s: (g, 0, 0)),
                pl.BlockSpec((1, 3, beads), lambda g, s: (g, 0, 0)),
                pl.BlockSpec((1,) + pair_noise.shape[1:], lambda g, s: (g, 0, 0, 0)),
            ],
            out_specs=pl.BlockSpec((1, 3, beads), lambda g, s: (g, 0, 0)),
            scratch_shapes=[
                vmem((6, beads // 128, 8, 128), F32),
                vmem((6, beads // 128, 128, 128), F32),
                vmem((beads // 128, 3, 8, 128), F32),
            ],
        ),
        out_shape=sds(positions.shape, F32),
        compiler_params=params(),
        cost_estimate=cost(30_000_000, 2_500_000),
        name="pair_forces",
    )(pair_tiles, positions, velocities, pair_noise)

    fwd, bwd = pl.pallas_call(
        functools.partial(edges_kernel, n, nx),
        in_specs=[ANY_SPEC, ANY_SPEC, VMEM_SPEC, VMEM_SPEC],
        out_specs=[ANY_SPEC, ANY_SPEC],
        out_shape=[sds(fwd.shape, F32), sds(bwd.shape, F32)],
        input_output_aliases={0: 0, 1: 1},
        scratch_shapes=[vmem((2, 16, lanes), F32), dma((2,))],
        compiler_params=params(),
        cost_estimate=cost(1000, 100_000),
        name="face_edges",
    )(fwd, bwd, below, above)
    before = shift(fwd, "ax", 1)
    after = shift(bwd, "ax", -1)

    total = pl.pallas_call(
        functools.partial(scatter_kernel, n, per),
        in_specs=[SMEM_SPEC] + [VMEM_SPEC] * (n + 1),
        out_specs=VMEM_SPEC,
        out_shape=sds((4, nx * ROWS, lanes), F32),
        scratch_shapes=[vmem((n, per, 8, beads), F32)],
        compiler_params=params(),
        cost_estimate=cost(3_000_000_000, 1_500_000),
        name="bead_sums",
    )(patch_owner, patch_voxel, velocities, *sent)

    inner = nx - 2
    post2, bits = pl.pallas_call(
        functools.partial(middle_kernel, n, nx),
        in_specs=[ANY_SPEC, VMEM_SPEC, VMEM_SPEC, VMEM_SPEC],
        out_specs=[VMEM_SPEC, VMEM_SPEC],
        out_shape=[sds((19, inner, PAD, lanes), F32), sds((inner, 72, lanes), I32)],
        scratch_shapes=[
            vmem((19, nx, PAD, lanes), F32),
            vmem((nx, PAD, lanes), I32),
            dma((nx,)),
        ],
        compiler_params=params(),
        cost_estimate=cost(12_000_000, 9_000_000),
        name="middle_layers",
    )(post, fluid_mask, below, above)

    post2_outer, bits_outer, fwd2, bwd2 = pl.pallas_call(
        functools.partial(outer_kernel, n, nx),
        in_specs=[ANY_SPEC, VMEM_SPEC, VMEM_SPEC, VMEM_SPEC, ANY_SPEC, ANY_SPEC],
        out_specs=[VMEM_SPEC] * 4,
        out_shape=[
            sds((19, 2, PAD, lanes), F32),
            sds((2, 72, lanes), I32),
            sds((328, lanes), F32),
            sds((328, lanes), F32),
        ],
        scratch_shapes=[
            vmem((19, nx, PAD, lanes), F32),
            vmem((2, 5, PAD, lanes), F32),
            vmem((nx, PAD, lanes), I32),
            vmem((2, PAD, lanes), F32),
            vmem((2, 16, lanes), F32),
            dma((26,)),
        ],
        compiler_params=params(),
        cost_estimate=cost(12_000_000, 9_000_000),
        name="outer_layers",
    )(post, fluid_mask, below, above, before, after)
    before2 = shift(fwd2, "ax", 1)
    after2 = shift(bwd2, "ax", -1)

    out, flow = pl.pallas_call(
        functools.partial(final_middle_kernel, nx),
        in_specs=[VMEM_SPEC, ANY_SPEC, VMEM_SPEC],
        out_specs=[ANY_SPEC, VMEM_SPEC],
        out_shape=[sds(populations.shape, F32), sds((3, inner, ROWS, lanes), F32)],
        scratch_shapes=[
            vmem((2, 5, PAD, lanes), F32),
            vmem((19, inner, ROWS, lanes), F32),
            dma((10 + nx,)),
        ],
        compiler_params=params(),
        cost_estimate=cost(6_000_000, 7_000_000),
        name="final_middle",
    )(post2, post2_outer, bits)

    out, flow_outer = pl.pallas_call(
        functools.partial(final_outer_kernel, nx),
        in_specs=[ANY_SPEC, VMEM_SPEC, ANY_SPEC, VMEM_SPEC, ANY_SPEC, ANY_SPEC],
        out_specs=[ANY_SPEC, VMEM_SPEC],
        out_shape=[sds(populations.shape, F32), sds((3, 2, ROWS, lanes), F32)],
        input_output_aliases={0: 0},
        scratch_shapes=[
            vmem((2, 6, PAD, lanes), F32),
            vmem((2, 5, PAD, lanes), F32),
            vmem((19, 2, ROWS, lanes), F32),
            dma((24,)),
        ],
        compiler_params=params(),
        cost_estimate=cost(6_000_000, 7_000_000),
        name="final_outer",
    )(out, post2_outer, post2, bits_outer, before2, after2)

    flows = pl.pallas_call(
        functools.partial(gather_kernel, n, per),
        in_specs=[SMEM_SPEC] + [VMEM_SPEC] * 3,
        out_specs=[VMEM_SPEC] * n,
        out_shape=[sds((per, 3, beads), F32)] * n,
        scratch_shapes=[
            vmem((patches, 8, beads), F32),
            vmem((3, nx * ROWS, 2 * lanes), BF16),
        ],
        compiler_params=params(),
        cost_estimate=cost(3_000_000_000, 1_500_000),
        name="bead_flow",
    )(patch_owner, patch_voxel, flow, flow_outer)
    flows = [flows[0]] + [shift(flows[d], "xs", d) for d in range(1, n)]

    field = pl.pallas_call(
        field_kernel,
        in_specs=[VMEM_SPEC] * 3,
        out_specs=VMEM_SPEC,
        out_shape=sds((3, nx, ROWS, lanes), F32),
        compiler_params=params(),
        cost_estimate=cost(400_000, 2_500_000),
        name="drag_field",
    )(total, flow, flow_outer)

    new_pos, new_vel = pl.pallas_call(
        functools.partial(final_kernel, n, per),
        in_specs=[VMEM_SPEC] * (n + 2),
        out_specs=[VMEM_SPEC] * 2,
        out_shape=[sds(positions.shape, F32)] * 2,
        compiler_params=params(),
        cost_estimate=cost(50_000, 300_000),
        name="bead_update",
    )(positions, base, *flows)
    return out, new_pos, new_vel, field


def solution(mesh):
    return jax.shard_map(
        per_device,
        mesh=mesh,
        in_specs=(
            P(None, "ax", "xs", None),
            P("ax", "xs", None),
            P(("ax", "xs"), None),
            P(("ax", "xs")),
            P(("ax", "xs"), None, None),
            P(("ax", "xs"), None, None),
            P(("ax", "xs"), None, None),
            P(("ax", "xs"), None, None, None),
        ),
        out_specs=(
            P(None, "ax", "xs", None),
            P(("ax", "xs"), None, None),
            P(("ax", "xs"), None, None),
            P(None, "ax", "xs", None),
        ),
        check_vma=False,
    )
```

```python
import functools

import jax
import jax.numpy as jnp
from jax import lax
from jax.experimental import pallas as pl
from jax.experimental.pallas import tpu as pltpu
from jax.sharding import PartitionSpec as P

DIRS = [
    (0, 0, 0),
    (1, 0, 0),
    (-1, 0, 0),
    (0, 1, 0),
    (0, -1, 0),
    (0, 0, 1),
    (0, 0, -1),
    (1, 1, 0),
    (-1, -1, 0),
    (1, -1, 0),
    (-1, 1, 0),
    (1, 0, 1),
    (-1, 0, -1),
    (1, 0, -1),
    (-1, 0, 1),
    (0, 1, 1),
    (0, -1, -1),
    (0, 1, -1),
    (0, -1, 1),
]
OPP = [0, 2, 1, 4, 3, 6, 5, 8, 7, 10, 9, 12, 11, 14, 13, 16, 15, 18, 17]
CX_PLUS = [k for k in range(19) if DIRS[k][0] == 1]
CX_MINUS = [k for k in range(19) if DIRS[k][0] == -1]
CY_PLUS = [k for k in range(19) if DIRS[k][1] == 1]
CY_MINUS = [k for k in range(19) if DIRS[k][1] == -1]
F32 = jnp.float32
BF16 = jnp.bfloat16
I32 = jnp.int32
VMEM_SPEC = pl.BlockSpec(memory_space=pltpu.VMEM)
SMEM_SPEC = pl.BlockSpec(memory_space=pltpu.SMEM)
ANY_SPEC = pl.BlockSpec(memory_space=pl.ANY)
HBM_SPEC = pl.BlockSpec(memory_space=pltpu.HBM)

ROWS = 64
PAD = 88
TILES = ROWS // 8


def params(mib=16):
    return pltpu.CompilerParams(vmem_limit_bytes=mib * 1024 * 1024)


def cost(flops, bytes_accessed):
    return pl.CostEstimate(flops=flops, bytes_accessed=bytes_accessed, transcendentals=0)


def call(kernel, ins, out_shape, name, estimate, after=(), specs=None, **kwargs):
    specs = specs or {}
    count, extra = len(ins), len(after)

    def body(*refs):
        kernel(*refs[:count], *refs[count + extra :])

    return pl.pallas_call(
        body,
        in_specs=[specs.get(i, VMEM_SPEC) for i in range(count)] + [ANY_SPEC] * extra,
        out_shape=out_shape,
        cost_estimate=estimate,
        name=name,
        **{"compiler_params": params(), **kwargs},
    )(*ins, *after)


def tree(values):
    while len(values) > 1:
        values = [
            values[i] + values[i + 1] if i + 1 < len(values) else values[i]
            for i in range(0, len(values), 2)
        ]
    return values[0]


def velocity_of(f):
    diff = [None] + [f[k] - f[k + 1] for k in range(1, 19, 2)]
    rho = tree([f[k] for k in range(1, 19)] + [f[0]])
    m1, m3, m5, m7, m9, m11, m13, m15, m17 = diff[1:]
    jx = m1 + ((m7 + m9) + (m11 + m13))
    jy = m3 + ((m7 - m9) + (m15 + m17))
    jz = m5 + ((m11 - m13) + (m15 - m17))
    inv = 1.0 / rho
    return rho, jx * inv, jy * inv, jz * inv


def collide(f):
    rho, ux, uy, uz = velocity_of(f)
    base = (1.25 * rho) * (1.0 - 1.5 * (ux * ux + uy * uy + uz * uz))
    ux, uy, uz = 1.5 * ux, 1.5 * uy, 1.5 * uz
    even1, even2 = base * (1.0 / 18.0), base * (1.0 / 36.0)
    odd1, odd2 = rho * (2.5 / 18.0), rho * (2.5 / 36.0)
    out = [None] * 19
    out[0] = base * (1.0 / 3.0) - 0.25 * f[0]
    for k in range(1, 19, 2):
        dx, dy, dz = DIRS[k]
        proj = None
        for sign, comp in ((dx, ux), (dy, uy), (dz, uz)):
            if sign == 0:
                continue
            if proj is None:
                proj = comp
            else:
                proj = proj + comp if sign > 0 else proj - comp
        even, odd = (even1, odd1) if k < 7 else (even2, odd2)
        odd = odd * proj
        even = even + odd * proj
        out[k] = (even + odd) - 0.25 * f[k]
        out[k + 1] = (even - odd) - 0.25 * f[k + 1]
    return out


def shifted(read, tile, dy, dz):
    here = read(tile)
    if dy != 0:
        sub = lax.broadcasted_iota(I32, here.shape, 0)
        if dy > 0:
            here = pltpu.roll(jnp.where(sub == 7, read(tile - 1), here), 1, 0)
        else:
            here = pltpu.roll(jnp.where(sub == 0, read(tile + 1), here), 7, 0)
    if dz != 0:
        here = pltpu.roll(here, 1 if dz > 0 else here.shape[1] - 1, 1)
    return here


def rows_of(tile):
    return pl.ds(pl.multiple_of(8 + 8 * tile, 8), 8)


def open_bits(read_mask, tile):
    bits = None
    cache = {}
    for k in range(1, 19):
        dx, dy, dz = DIRS[k]
        if (dx, dy) not in cache:
            cache[(dx, dy)] = shifted(functools.partial(read_mask, dx), tile, dy, 0)
        m = cache[(dx, dy)]
        if dz != 0:
            lane = lax.broadcasted_iota(I32, m.shape, 1)
            last = m.shape[1] - 1
            m = pltpu.roll(m, 1 if dz > 0 else last, 1)
            m = jnp.where(lane == (0 if dz > 0 else last), 0, m)
        m = m << k
        bits = m if bits is None else bits | m
    return bits


def stream(read, own, bits, tile):
    out = [own[0]]
    for k in range(1, 19):
        dx, dy, dz = DIRS[k]
        source = shifted(functools.partial(read, k, dx), tile, dy, dz)
        out.append(jnp.where((bits & (1 << k)) != 0, source, own[OPP[k]]))
    return out


def tile_rows(t):
    return pl.ds(pl.multiple_of(8 * t, 8), 8)


def collide_kernel(n, per, nx, pop, mask, vel, post, fwd, bwd, up, down, *rest):
    others, (here, flags, sems) = rest[: n - 3], rest[n - 3 :]
    copies = [pltpu.make_async_copy(pop.at[:, x], here.at[x], sems.at[x]) for x in range(nx)]
    copies.append(pltpu.make_async_copy(mask, flags, sems.at[nx]))
    for copy in copies:
        copy.start()
    me = lax.axis_index("xs")
    for d in range(1, n):
        target = lax.rem(me + d, n)
        for r in range(per):
            for c in range(3):
                row = vel[c, pl.ds(target * per + r, 1), :]
                for half in range(2):
                    i = (r * 3 + c) * 2 + half
                    piece = row[:, half * 256 : (half + 1) * 256]
                    if d in (1, n - 1):
                        ref = up if d == 1 else down
                        ref[i // 3, 26 + i % 3 : 27 + i % 3, :] = piece
                    else:
                        others[d - 2][i : i + 1, :] = piece
    copies[nx].wait()
    for x in range(nx):
        copies[x].wait()

        def body(t, carry, x=x):
            rows = tile_rows(t)
            out = collide([here[x, k, rows, :] for k in range(19)])
            for k in range(19):
                post[k, x, rows_of(t), :] = out[k]
            return carry

        lax.fori_loop(0, TILES, body, 0)
        for ref, near, beyond, dirs in ((up, ROWS - 1, ROWS - 2, CY_PLUS), (down, 0, 1, CY_MINUS)):
            for k in range(19):
                ref[x, k : k + 1, :] = post[k, x, 8 + near : 9 + near, :]
            for j, k in enumerate(dirs):
                ref[x, 19 + j : 20 + j, :] = post[k, x, 8 + beyond : 9 + beyond, :]
            ref[x, 24:25, :] = flags[x, near : near + 1, :].astype(F32)
            ref[x, 25:26, :] = flags[x, beyond : beyond + 1, :].astype(F32)
    for x, ref, dirs in ((nx - 1, fwd, CX_PLUS), (0, bwd, CX_MINUS)):
        for j, k in enumerate(dirs):
            ref[j * ROWS : (j + 1) * ROWS, :] = post[k, x, 8:72, :]
        ref[5 * ROWS : 6 * ROWS, :] = flags[x].astype(F32)


def sent_velocity(refs, n, d, r, c):
    out = []
    for half in range(2):
        i = (r * 3 + c) * 2 + half
        if d in (1, n - 1):
            out.append(refs[d - 1][i // 3, 26 + i % 3 : 27 + i % 3, :])
        else:
            out.append(refs[d - 1][i : i + 1, :])
    return jnp.concatenate(out, axis=1)


def edges_kernel(n, nx, post_in, fwd_in, bwd_in, mask, below, above, post, fwd, bwd, flags):
    me = lax.axis_index("xs")
    has_below, has_above = (me > 0).astype(F32), (me < n - 1).astype(F32)
    for x in range(nx):
        for k in range(19):
            post[k, x, 79:80, :] = below[x, k : k + 1, :]
            post[k, x, 72:73, :] = above[x, k : k + 1, :]
        for j, k in enumerate(CY_PLUS):
            post[k, x, 7:8, :] = below[x, k : k + 1, :]
            post[k, x, 78:79, :] = below[x, 19 + j : 20 + j, :]
        for j, k in enumerate(CY_MINUS):
            post[k, x, 73:74, :] = above[x, 19 + j : 20 + j, :]
            post[k, x, 80:81, :] = post[k, x, 8:9, :]
        flags[x, 8:72, :] = mask[x]
        near = (below[x, 24:25, :] * has_below).astype(I32)
        flags[x, 79:80, :] = near
        flags[x, 7:8, :] = near
        flags[x, 78:79, :] = (below[x, 25:26, :] * has_below).astype(I32)
        flags[x, 72:73, :] = (above[x, 24:25, :] * has_above).astype(I32)
        flags[x, 73:74, :] = (above[x, 25:26, :] * has_above).astype(I32)
        flags[x, 80:81, :] = mask[x, 0:1, :]
    for rows, x, dirs, far_below, far_above in (
        (fwd, nx - 1, CX_PLUS, 7, 9),
        (bwd, 0, CX_MINUS, 10, 8),
    ):
        e = 6 * ROWS
        for j, k in enumerate(dirs):
            rows[e + j : e + j + 1, :] = below[x, k : k + 1, :]
            rows[e + 8 + j : e + 9 + j, :] = above[x, k : k + 1, :]
        j = 19 + CY_PLUS.index(far_below)
        rows[e + 5 : e + 6, :] = below[x, j : j + 1, :]
        j = 19 + CY_MINUS.index(far_above)
        rows[e + 13 : e + 14, :] = above[x, j : j + 1, :]
        rows[e + 6 : e + 8, :] = below[x, 24:26, :] * has_below
        rows[e + 14 : e + 16, :] = above[x, 24:26, :] * has_above


def step_layer(x, read, read_mask, post, post2, bits_out):
    def body(t, carry):
        bits = open_bits(read_mask, t)
        own = [post[k, x, rows_of(t), :] for k in range(19)]
        out = collide(stream(read, own, bits, t))
        for k in range(19):
            post2[k, x, rows_of(t), :] = out[k]
        bits_out[x, tile_rows(t), :] = bits
        return carry

    lax.fori_loop(0, TILES + 1, body, 0)
    for k in CY_PLUS:
        post2[k, x, 7:8, :] = post2[k, x, 79:80, :]


def middle_kernel(nx, post, flags, post2, bits_out):
    for x in range(1, nx - 1):
        step_layer(
            x,
            lambda k, dx, tile, x=x: post[k, x - dx, rows_of(tile), :],
            lambda dx, tile, x=x: flags[x - dx, rows_of(tile), :],
            post,
            post2,
            bits_out,
        )


def outer_kernel(
    nx, post, flags, before, after, post2_in, bits_in, post2, bits_out, fwd2, bwd2, halo, halo_flags
):
    last = nx - 1
    e = 6 * ROWS
    for i, (ref, dirs, far_below, far_above) in enumerate(
        ((before, CX_PLUS, 7, 9), (after, CX_MINUS, 10, 8))
    ):
        for j, k in enumerate(dirs):
            halo[i, j, 8:72, :] = ref[j * ROWS : (j + 1) * ROWS, :]
            halo[i, j, 79:80, :] = ref[e + j : e + j + 1, :]
            halo[i, j, 72:73, :] = ref[e + 8 + j : e + 9 + j, :]
            if k == far_below:
                halo[i, j, 7:8, :] = ref[e + j : e + j + 1, :]
                halo[i, j, 78:79, :] = ref[e + 5 : e + 6, :]
            if k == far_above:
                halo[i, j, 73:74, :] = ref[e + 13 : e + 14, :]
                halo[i, j, 80:81, :] = ref[j * ROWS : j * ROWS + 1, :]
        halo_flags[i, 8:72, :] = ref[5 * ROWS : 6 * ROWS, :].astype(I32)
        halo_flags[i, 79:80, :] = ref[e + 6 : e + 7, :].astype(I32)
        halo_flags[i, 7:8, :] = ref[e + 6 : e + 7, :].astype(I32)
        halo_flags[i, 78:79, :] = ref[e + 7 : e + 8, :].astype(I32)
        halo_flags[i, 72:73, :] = ref[e + 14 : e + 15, :].astype(I32)
        halo_flags[i, 73:74, :] = ref[e + 15 : e + 16, :].astype(I32)
        halo_flags[i, 80:81, :] = ref[5 * ROWS : 5 * ROWS + 1, :].astype(I32)
    for x in (0, last):

        def read(k, dx, tile, x=x):
            if x - dx < 0:
                return halo[0, CX_PLUS.index(k), rows_of(tile), :]
            if x - dx > last:
                return halo[1, CX_MINUS.index(k), rows_of(tile), :]
            return post[k, x - dx, rows_of(tile), :]

        def read_mask(dx, tile, x=x):
            if x - dx < 0 or x - dx > last:
                return halo_flags[0 if x - dx < 0 else 1, rows_of(tile), :]
            return flags[x - dx, rows_of(tile), :]

        step_layer(x, read, read_mask, post, post2, bits_out)
    for x, ref, dirs, k_below, k_above in ((last, fwd2, CX_PLUS, 7, 9), (0, bwd2, CX_MINUS, 10, 8)):
        for j, k in enumerate(dirs):
            ref[j * ROWS : (j + 1) * ROWS, :] = post2[k, x, 8:72, :]
        ref[320:321, :] = post2[k_below, x, 79:80, :]
        ref[321:322, :] = post2[k_above, x, 72:73, :]


def final_layer(x, read, post2, bits, result, flow, out, sem):
    def body(t, carry):
        rows = tile_rows(t)
        own = [post2[k, x, rows_of(t), :] for k in range(19)]
        f = stream(read, own, bits[x, rows, :], t)
        for k in range(19):
            result[k, rows, :] = f[k]
        rho, ux, uy, uz = velocity_of(f)
        flow[0, x, rows, :] = ux
        flow[1, x, rows, :] = uy
        flow[2, x, rows, :] = uz
        return carry

    lax.fori_loop(0, TILES, body, 0)
    copy = pltpu.make_async_copy(result, out.at[:, x], sem)
    copy.start()
    return copy


def final_middle_kernel(nx, post2, bits, out, flow, result, sems):
    copies = []
    for i, x in enumerate(range(1, nx - 1)):
        read = lambda k, dx, tile, x=x: post2[k, x - dx, rows_of(tile), :]
        copies.append(final_layer(x, read, post2, bits, result.at[i], flow, out, sems.at[i]))
    for copy in copies:
        copy.wait()


def final_outer_kernel(nx, out_in, flow_in, post2, bits, before, after, out, flow, halo, result, sems):
    last = nx - 1
    for i, (ref, dirs, k_below, k_above) in enumerate(
        ((before, CX_PLUS, 7, 9), (after, CX_MINUS, 10, 8))
    ):
        for j in range(5):
            halo[i, j, 8:72, :] = ref[j * ROWS : (j + 1) * ROWS, :]
        halo[i, dirs.index(k_below), 7:8, :] = ref[320:321, :]
        halo[i, dirs.index(k_above), 72:73, :] = ref[321:322, :]
    copies = []
    for i, x in enumerate((0, last)):

        def read(k, dx, tile, x=x):
            if x - dx < 0:
                return halo[0, CX_PLUS.index(k), rows_of(tile), :]
            if x - dx > last:
                return halo[1, CX_MINUS.index(k), rows_of(tile), :]
            return post2[k, x - dx, rows_of(tile), :]

        copies.append(final_layer(x, read, post2, bits, result.at[i], flow, out, sems.at[i]))
    for copy in copies:
        copy.wait()


def pair_kernel(first_patch, pair_tiles, pos, vel, noise, *refs):
    base, rows, cols, theta, acc = refs[-5:]
    g = pl.program_id(0) + first_patch
    tile = noise.shape[-1]
    count = pos.shape[-1] // tile
    pairs = noise.shape[1]
    both = [ref[c, pl.ds(g, 1), :] for ref in (pos, vel) for c in range(3)]
    speed = both[3:]
    both = [both[c] if c < 3 else 4.5 * both[c] for c in range(6)]
    stacked = jnp.concatenate(both + [jnp.zeros((2, both[0].shape[1]), F32)], axis=0)
    turned = stacked.T
    for c in range(6):
        for j in range(count):
            part = turned[j * tile : (j + 1) * tile, c : c + 1]
            cols[c, j] = jnp.broadcast_to(part, (tile, tile))
            rows[c, j] = jnp.broadcast_to(both[c][:, j * tile : (j + 1) * tile], (8, tile))
    acc[...] = jnp.zeros_like(acc)
    eye = lax.broadcasted_iota(I32, (tile, tile), 0) == lax.broadcasted_iota(I32, (tile, tile), 1)
    scale = jnp.where(eye, 15.0, 0.0).astype(BF16)
    for p in range(pairs):
        theta[p] = lax.dot_general(
            scale, noise[0, p], (((1,), (1,)), ((), ())), preferred_element_type=F32
        )

    def one_pair(p, carry):
        first = pair_tiles[g, 0, p]
        second = pair_tiles[g, 1, p]
        mine = [rows[c, first] for c in range(6)]
        parts = []
        for s in range(tile // 8):
            part = slice(8 * s, 8 * s + 8)
            dx, dy, dz = [mine[c] - cols[c, second, part, :] for c in range(3)]
            vx, vy, vz = [mine[c] - cols[c, second, part, :] for c in range(3, 6)]
            square = (dx * dx + 0.01) + (dy * dy + dz * dz)
            close = jnp.maximum(lax.rsqrt(square) - 1.0, 0.0)
            along = dx * vx + (dy * vy + dz * vz)
            force = close * ((theta[p, part, :] + 25.0) - close * along)
            here = [force * dx, force * dy, force * dz]
            parts = here if not parts else [a + b for a, b in zip(parts, here)]
        for c in range(3):
            acc[first, c] += parts[c]
        return carry

    lax.fori_loop(0, pairs, one_pair, 0)
    for c in range(3):
        force = jnp.concatenate(
            [jnp.sum(acc[j, c], axis=0, keepdims=True) for j in range(count)], axis=1
        )
        base[c, pl.ds(g, 1), :] = 0.5 * speed[c] + 0.04 * force


def split(value):
    high = value.astype(BF16)
    return high, (value - high.astype(F32)).astype(BF16)


def ranks(owner, count):
    out = []
    for g in range(count):
        rank = jnp.int32(0)
        for h in range(g):
            rank = rank + (owner[h] == owner[g]).astype(I32)
        out.append(rank)
    return out


def one_hot(index, extent):
    want = index.astype(F32).astype(BF16)
    place = lax.broadcasted_iota(I32, (extent, index.shape[1]), 0).astype(F32).astype(BF16)
    return place == want


def scatter_kernel(n, per, owner, voxel, vel, *refs):
    sent, out, table = refs[: n - 1], refs[n - 1], refs[n]
    me = lax.axis_index("xs")
    beads = voxel.shape[1]
    for r in range(per):
        for c in range(3):
            table[me, r, c : c + 1, :] = vel[c, pl.ds(me * per + r, 1), :]
        for d in range(1, n):
            source = lax.rem(me + n - d, n)
            for c in range(3):
                table[source, r, c : c + 1, :] = sent_velocity(sent, n, d, r, c)
    out[...] = jnp.zeros_like(out)
    rank = ranks(owner, voxel.shape[0])
    one, zero = BF16(1), BF16(0)
    for g in range(voxel.shape[0]):
        index = voxel[g : g + 1, :]
        lanes = jnp.where(one_hot(index & 255, 256), one, zero)
        at_row = one_hot(index >> 8, out.shape[1])
        values = table[owner[g], rank[g]]
        lanes2 = jnp.concatenate([lanes, lanes], axis=1)
        for c in range(3):
            high, low = split(values[c : c + 1, :])
            left = jnp.concatenate(
                [jnp.where(at_row, high, zero), jnp.where(at_row, low, zero)], axis=1
            )
            out[c] += lax.dot_general(
                left, lanes2, (((1,), (1,)), ((), ())), preferred_element_type=F32
            )
        out[3] += lax.dot_general(
            jnp.where(at_row, one, zero), lanes, (((1,), (1,)), ((), ())), preferred_element_type=F32
        )


def gather_kernel(n, per, owner, voxel, flow, *refs):
    outs, table, field = refs[:n], refs[n], refs[n + 1]
    me = lax.axis_index("xs")
    patches = voxel.shape[0]
    nx = flow.shape[1]
    rows = nx * ROWS
    for c in range(3):
        for x in range(nx):
            high, low = split(flow[c, x])
            field[c, x * ROWS : (x + 1) * ROWS, 0:256] = high
            field[c, x * ROWS : (x + 1) * ROWS, 256:512] = low
    one, zero = BF16(1), BF16(0)
    for g in range(patches):
        index = voxel[g : g + 1, :]
        lanes = jnp.where(one_hot(index & 255, 256), one, zero)
        lanes2 = jnp.concatenate([lanes, lanes], axis=0)
        at_row = lax.broadcasted_iota(I32, (rows, index.shape[1]), 0) == (index >> 8)
        for c in range(3):
            found = lax.dot_general(
                field[c], lanes2, (((1,), (0,)), ((), ())), preferred_element_type=F32
            )
            table[g, c : c + 1, :] = jnp.sum(jnp.where(at_row, found, 0.0), axis=0, keepdims=True)
    rank = ranks(owner, patches)
    for d in range(n):
        target = lax.rem(me + d, n)
        for r in range(per):
            found = jnp.int32(0)
            for g in range(patches):
                found = jnp.where((owner[g] == target) & (rank[g] == r), g, found)
            outs[d][r * 3 : r * 3 + 3, :] = table[found, 0:3, :]


def field_kernel(total, flow, field):
    for x in range(field.shape[1]):
        rows = slice(x * ROWS, (x + 1) * ROWS)
        number = 10.0 * total[3, rows, :]
        for c in range(3):
            field[c, x] = 0.5 * total[c, rows, :] - number * flow[c, x]


def final_kernel(n, per, pos, base, *refs):
    flows, new_pos, new_vel = refs[:n], refs[n], refs[n + 1]
    me = lax.axis_index("xs")
    for d in range(n):
        source = lax.rem(me + n - d, n)
        for r in range(per):
            at = pl.ds(source * per + r, 1)
            for c in range(3):
                speed = base[c, at, :] + 10.0 * flows[d][r * 3 + c : r * 3 + c + 1, :]
                new_vel[c, at, :] = speed
                new_pos[c, at, :] = pos[c, at, :] + 0.04 * speed


def shift(value, axis, by):
    n = lax.axis_size(axis)
    return lax.ppermute(value, axis, [(i, (i + by) % n) for i in range(n)])


def pair_call(first_patch, patches, pair_tiles, pos, vel, noise, given, after):
    beads = pos.shape[2]
    tile = noise.shape[-1]
    count = beads // tile
    whole = lambda g, s: (0, 0, 0)
    ins = [pos, vel, noise] + given + after
    return pl.pallas_call(
        functools.partial(pair_kernel, first_patch),
        grid_spec=pltpu.PrefetchScalarGridSpec(
            num_scalar_prefetch=1,
            grid=(patches,),
            in_specs=[
                pl.BlockSpec(pos.shape, whole),
                pl.BlockSpec(vel.shape, whole),
                pl.BlockSpec((1,) + noise.shape[1:], lambda g, s: (g + first_patch, 0, 0, 0)),
            ]
            + [pl.BlockSpec(pos.shape, whole)] * len(given)
            + [ANY_SPEC] * len(after),
            out_specs=pl.BlockSpec(pos.shape, whole),
            scratch_shapes=[
                pltpu.VMEM((6, count, 8, tile), F32),
                pltpu.VMEM((6, count, tile, tile), F32),
                pltpu.VMEM(noise.shape[1:], F32),
                pltpu.VMEM((count, 3, 8, tile), F32),
            ],
        ),
        out_shape=jax.ShapeDtypeStruct(pos.shape, F32),
        input_output_aliases={4: 0} if given else {},
        compiler_params=params(),
        cost_estimate=cost(3_000_000_000, 1_500_000),
        name="pair_forces",
    )(pair_tiles, *ins)


def per_device(
    populations, fluid_mask, patch_voxel, patch_owner, positions, velocities, pair_tiles, pair_noise
):
    n = lax.axis_size("xs")
    patches, beads = patch_voxel.shape
    per = patches // n
    nx = populations.shape[1]
    lanes = populations.shape[3]
    arr = lambda *shape: jax.ShapeDtypeStruct(shape, F32)
    ints = lambda *shape: jax.ShapeDtypeStruct(shape, I32)
    vmem, dma = pltpu.VMEM, pltpu.SemaphoreType.DMA
    positions = jnp.transpose(positions, (1, 0, 2))
    velocities = jnp.transpose(velocities, (1, 0, 2))
    pair_tiles = jnp.transpose(pair_tiles, (0, 2, 1))

    post, fwd, bwd, up, down, *others = call(
        functools.partial(collide_kernel, n, per, nx),
        [populations, fluid_mask, velocities],
        [
            arr(19, nx, PAD, lanes),
            arr(400, lanes),
            arr(400, lanes),
            arr(nx, 32, lanes),
            arr(nx, 32, lanes),
        ]
        + [arr(16, lanes)] * (n - 3),
        "collide_first",
        cost(3_000_000_000, 11_000_000),
        specs={0: HBM_SPEC, 1: HBM_SPEC},
        out_specs=[VMEM_SPEC] * (5 + n - 3),
        scratch_shapes=[vmem((nx, 19, ROWS, lanes), F32), vmem((nx, ROWS, lanes), I32), dma((nx + 1,))],
    )
    below = shift(up, "xs", 1)
    above = shift(down, "xs", -1)
    sent = [below] + [shift(other, "xs", d + 2) for d, other in enumerate(others)] + [above]

    half = patches // 2
    bead_args = (pair_tiles, positions, velocities, pair_noise)
    base = pair_call(0, half, *bead_args, [], [down])

    post, fwd, bwd, flags = call(
        functools.partial(edges_kernel, n, nx),
        [post, fwd, bwd, fluid_mask, below, above],
        [arr(*post.shape), arr(*fwd.shape), arr(*bwd.shape), ints(nx, PAD, lanes)],
        "edges",
        cost(1000, 100_000),
        after=[base],
        out_specs=[VMEM_SPEC] * 4,
        input_output_aliases={0: 0, 1: 1, 2: 2},
    )
    before = shift(fwd, "ax", 1)
    after = shift(bwd, "ax", -1)

    post2, bits = call(
        functools.partial(middle_kernel, nx),
        [post, flags],
        [arr(19, nx, PAD, lanes), ints(nx, 72, lanes)],
        "middle_layers",
        cost(3_000_000_000, 9_000_000),
        out_specs=[VMEM_SPEC] * 2,
    )
    base = pair_call(half, patches - half, *bead_args, [base], [flags])

    post2, bits, fwd2, bwd2 = call(
        functools.partial(outer_kernel, nx),
        [post, flags, before, after, post2, bits],
        [arr(*post2.shape), ints(*bits.shape), arr(328, lanes), arr(328, lanes)],
        "outer_layers",
        cost(3_000_000_000, 9_000_000),
        after=[base],
        out_specs=[VMEM_SPEC] * 4,
        input_output_aliases={4: 0, 5: 1},
        scratch_shapes=[vmem((2, 5, PAD, lanes), F32), vmem((2, PAD, lanes), I32)],
    )
    before2 = shift(fwd2, "ax", 1)
    after2 = shift(bwd2, "ax", -1)

    out, flow = call(
        functools.partial(final_middle_kernel, nx),
        [post2, bits],
        [arr(*populations.shape), arr(3, nx, ROWS, lanes)],
        "final_middle",
        cost(3_000_000_000, 7_000_000),
        out_specs=[ANY_SPEC, VMEM_SPEC],
        scratch_shapes=[vmem((nx - 2, 19, ROWS, lanes), F32), dma((nx - 2,))],
    )
    total = call(
        functools.partial(scatter_kernel, n, per),
        [patch_owner, patch_voxel, velocities] + sent,
        arr(4, nx * ROWS, lanes),
        "bead_sums",
        cost(3_000_000_000, 1_500_000),
        after=[fwd2],
        specs={0: SMEM_SPEC},
        out_specs=VMEM_SPEC,
        scratch_shapes=[vmem((n, per, 8, beads), F32)],
    )
    out, flow = call(
        functools.partial(final_outer_kernel, nx),
        [out, flow, post2, bits, before2, after2],
        [arr(*populations.shape), arr(*flow.shape)],
        "final_outer",
        cost(3_000_000_000, 7_000_000),
        after=[total],
        specs={0: ANY_SPEC},
        out_specs=[ANY_SPEC, VMEM_SPEC],
        input_output_aliases={0: 0, 1: 1},
        scratch_shapes=[vmem((2, 5, PAD, lanes), F32), vmem((2, 19, ROWS, lanes), F32), dma((2,))],
    )
    flows = call(
        functools.partial(gather_kernel, n, per),
        [patch_owner, patch_voxel, flow],
        [arr(8, beads)] * n,
        "bead_flow",
        cost(3_000_000_000, 1_500_000),
        specs={0: SMEM_SPEC},
        out_specs=[VMEM_SPEC] * n,
        scratch_shapes=[vmem((patches, 8, beads), F32), vmem((3, nx * ROWS, 2 * lanes), BF16)],
    )
    sent_flows = [flows[0]] + [shift(flows[d], "xs", d) for d in range(1, n)]
    field = call(
        field_kernel,
        [total, flow],
        arr(3, nx, ROWS, lanes),
        "drag_field",
        cost(400_000_000, 2_500_000),
        after=[flows[1]],
        out_specs=VMEM_SPEC,
    )
    new_pos, new_vel = call(
        functools.partial(final_kernel, n, per),
        [positions, base] + sent_flows,
        [arr(*positions.shape)] * 2,
        "bead_update",
        cost(50_000, 300_000),
        after=[field],
        out_specs=[VMEM_SPEC] * 2,
    )
    return out, jnp.transpose(new_pos, (1, 0, 2)), jnp.transpose(new_vel, (1, 0, 2)), field


def solution(mesh):
    return jax.shard_map(
        per_device,
        mesh=mesh,
        in_specs=(
            P(None, "ax", "xs", None),
            P("ax", "xs", None),
            P(("ax", "xs"), None),
            P(("ax", "xs")),
            P(("ax", "xs"), None, None),
            P(("ax", "xs"), None, None),
            P(("ax", "xs"), None, None),
            P(("ax", "xs"), None, None, None),
        ),
        out_specs=(
            P(None, "ax", "xs", None),
            P(("ax", "xs"), None, None),
            P(("ax", "xs"), None, None),
            P(None, "ax", "xs", None),
        ),
        check_vma=False,
    )
```

```python
import functools

import jax
import jax.numpy as jnp
from jax import lax
from jax.experimental import pallas as pl
from jax.experimental.pallas import tpu as pltpu
from jax.sharding import PartitionSpec as P

DIRS = [
    (0, 0, 0),
    (1, 0, 0),
    (-1, 0, 0),
    (0, 1, 0),
    (0, -1, 0),
    (0, 0, 1),
    (0, 0, -1),
    (1, 1, 0),
    (-1, -1, 0),
    (1, -1, 0),
    (-1, 1, 0),
    (1, 0, 1),
    (-1, 0, -1),
    (1, 0, -1),
    (-1, 0, 1),
    (0, 1, 1),
    (0, -1, -1),
    (0, 1, -1),
    (0, -1, 1),
]
OPP = [0, 2, 1, 4, 3, 6, 5, 8, 7, 10, 9, 12, 11, 14, 13, 16, 15, 18, 17]
CX_PLUS = [k for k in range(19) if DIRS[k][0] == 1]
CX_MINUS = [k for k in range(19) if DIRS[k][0] == -1]
CY_PLUS = [k for k in range(19) if DIRS[k][1] == 1]
CY_MINUS = [k for k in range(19) if DIRS[k][1] == -1]
F32 = jnp.float32
BF16 = jnp.bfloat16
I32 = jnp.int32
VMEM_SPEC = pl.BlockSpec(memory_space=pltpu.VMEM)
SMEM_SPEC = pl.BlockSpec(memory_space=pltpu.SMEM)
ANY_SPEC = pl.BlockSpec(memory_space=pl.ANY)

ROWS = 64
PAD = 88
TILES = ROWS // 8


def params(mib=16):
    return pltpu.CompilerParams(vmem_limit_bytes=mib * 1024 * 1024)


def cost(flops, bytes_accessed):
    return pl.CostEstimate(flops=flops, bytes_accessed=bytes_accessed, transcendentals=0)


def call(kernel, ins, out_shape, name, estimate, after=(), specs=None, **kwargs):
    specs = specs or {}
    count, extra = len(ins), len(after)

    def body(*refs):
        kernel(*refs[:count], *refs[count + extra :])

    return pl.pallas_call(
        body,
        in_specs=[specs.get(i, VMEM_SPEC) for i in range(count)] + [ANY_SPEC] * extra,
        out_shape=out_shape,
        cost_estimate=estimate,
        name=name,
        **{"compiler_params": params(), **kwargs},
    )(*ins, *after)


def in_hbm(value):
    return pltpu.with_memory_space_constraint(value, pltpu.HBM)


def tree(values):
    while len(values) > 1:
        values = [
            values[i] + values[i + 1] if i + 1 < len(values) else values[i]
            for i in range(0, len(values), 2)
        ]
    return values[0]


def velocity_of(f):
    diff = [None] + [f[k] - f[k + 1] for k in range(1, 19, 2)]
    rho = tree([f[k] for k in range(1, 19)] + [f[0]])
    m1, m3, m5, m7, m9, m11, m13, m15, m17 = diff[1:]
    jx = m1 + ((m7 + m9) + (m11 + m13))
    jy = m3 + ((m7 - m9) + (m15 + m17))
    jz = m5 + ((m11 - m13) + (m15 - m17))
    inv = 1.0 / rho
    return rho, jx * inv, jy * inv, jz * inv


def collide(f):
    rho, ux, uy, uz = velocity_of(f)
    base = (1.25 * rho) * (1.0 - 1.5 * (ux * ux + uy * uy + uz * uz))
    ux, uy, uz = 1.5 * ux, 1.5 * uy, 1.5 * uz
    even1, even2 = base * (1.0 / 18.0), base * (1.0 / 36.0)
    odd1, odd2 = rho * (2.5 / 18.0), rho * (2.5 / 36.0)
    out = [None] * 19
    out[0] = base * (1.0 / 3.0) - 0.25 * f[0]
    for k in range(1, 19, 2):
        dx, dy, dz = DIRS[k]
        proj = None
        for sign, comp in ((dx, ux), (dy, uy), (dz, uz)):
            if sign == 0:
                continue
            if proj is None:
                proj = comp
            else:
                proj = proj + comp if sign > 0 else proj - comp
        even, odd = (even1, odd1) if k < 7 else (even2, odd2)
        odd = odd * proj
        even = even + odd * proj
        out[k] = (even + odd) - 0.25 * f[k]
        out[k + 1] = (even - odd) - 0.25 * f[k + 1]
    return out


def shifted(read, tile, dy, dz):
    here = read(tile)
    if dy != 0:
        sub = lax.broadcasted_iota(I32, here.shape, 0)
        if dy > 0:
            here = pltpu.roll(jnp.where(sub == 7, read(tile - 1), here), 1, 0)
        else:
            here = pltpu.roll(jnp.where(sub == 0, read(tile + 1), here), 7, 0)
    if dz != 0:
        here = pltpu.roll(here, 1 if dz > 0 else here.shape[1] - 1, 1)
    return here


def rows_of(tile):
    return pl.ds(pl.multiple_of(8 + 8 * tile, 8), 8)


def open_bits(read_mask, tile):
    bits = None
    cache = {}
    for k in range(1, 19):
        dx, dy, dz = DIRS[k]
        if (dx, dy) not in cache:
            cache[(dx, dy)] = shifted(functools.partial(read_mask, dx), tile, dy, 0)
        m = cache[(dx, dy)]
        if dz != 0:
            lane = lax.broadcasted_iota(I32, m.shape, 1)
            last = m.shape[1] - 1
            m = pltpu.roll(m, 1 if dz > 0 else last, 1)
            m = jnp.where(lane == (0 if dz > 0 else last), 0, m)
        m = m << k
        bits = m if bits is None else bits | m
    return bits


def stream(read, own, bits, tile):
    out = [own[0]]
    for k in range(1, 19):
        dx, dy, dz = DIRS[k]
        source = shifted(functools.partial(read, k, dx), tile, dy, dz)
        out.append(jnp.where((bits & (1 << k)) != 0, source, own[OPP[k]]))
    return out


def tile_rows(t):
    return pl.ds(pl.multiple_of(8 * t, 8), 8)


def collide_kernel(n, per, nx, pop, mask, vel, post, fwd, bwd, up, down, *rest):
    others, (here, flags, speeds, sems) = rest[: n - 3], rest[n - 3 :]
    copies = [pltpu.make_async_copy(pop.at[:, x], here.at[x], sems.at[x]) for x in range(nx)]
    copies.append(pltpu.make_async_copy(vel, speeds, sems.at[nx]))
    copies.append(pltpu.make_async_copy(mask, flags, sems.at[nx + 1]))
    for copy in copies[nx:] + copies[:nx]:
        copy.start()
    me = lax.axis_index("xs")
    copies[nx].wait()
    for d in range(1, n):
        target = lax.rem(me + d, n)
        for r in range(per):
            for c in range(3):
                row = speeds[c, pl.ds(target * per + r, 1), :]
                for half in range(2):
                    i = (r * 3 + c) * 2 + half
                    piece = row[:, half * 256 : (half + 1) * 256]
                    if d in (1, n - 1):
                        ref = up if d == 1 else down
                        ref[i // 3, 26 + i % 3 : 27 + i % 3, :] = piece
                    else:
                        others[d - 2][i : i + 1, :] = piece
    copies[nx + 1].wait()
    for x in range(nx):
        copies[x].wait()

        def body(t, carry, x=x):
            rows = tile_rows(t)
            out = collide([here[x, k, rows, :] for k in range(19)])
            for k in range(19):
                post[k, x, rows_of(t), :] = out[k]
            return carry

        lax.fori_loop(0, TILES, body, 0)
        for ref, near, beyond, dirs in ((up, ROWS - 1, ROWS - 2, CY_PLUS), (down, 0, 1, CY_MINUS)):
            for k in range(19):
                ref[x, k : k + 1, :] = post[k, x, 8 + near : 9 + near, :]
            for j, k in enumerate(dirs):
                ref[x, 19 + j : 20 + j, :] = post[k, x, 8 + beyond : 9 + beyond, :]
            ref[x, 24:25, :] = flags[x, near : near + 1, :].astype(F32)
            ref[x, 25:26, :] = flags[x, beyond : beyond + 1, :].astype(F32)
    for x, ref, dirs in ((nx - 1, fwd, CX_PLUS), (0, bwd, CX_MINUS)):
        for j, k in enumerate(dirs):
            ref[j * ROWS : (j + 1) * ROWS, :] = post[k, x, 8:72, :]
        ref[5 * ROWS : 6 * ROWS, :] = flags[x].astype(F32)


def sent_velocity(refs, n, d, r, c):
    out = []
    for half in range(2):
        i = (r * 3 + c) * 2 + half
        if d in (1, n - 1):
            out.append(refs[d - 1][i // 3, 26 + i % 3 : 27 + i % 3, :])
        else:
            out.append(refs[d - 1][i : i + 1, :])
    return jnp.concatenate(out, axis=1)


def edges_kernel(n, nx, post_in, fwd_in, bwd_in, mask, below, above, post, fwd, bwd, flags):
    me = lax.axis_index("xs")
    has_below, has_above = (me > 0).astype(F32), (me < n - 1).astype(F32)
    for x in range(nx):
        for k in range(19):
            post[k, x, 79:80, :] = below[x, k : k + 1, :]
            post[k, x, 72:73, :] = above[x, k : k + 1, :]
        for j, k in enumerate(CY_PLUS):
            post[k, x, 7:8, :] = below[x, k : k + 1, :]
            post[k, x, 78:79, :] = below[x, 19 + j : 20 + j, :]
        for j, k in enumerate(CY_MINUS):
            post[k, x, 73:74, :] = above[x, 19 + j : 20 + j, :]
            post[k, x, 80:81, :] = post[k, x, 8:9, :]
        flags[x, 8:72, :] = mask[x]
        near = (below[x, 24:25, :] * has_below).astype(I32)
        flags[x, 79:80, :] = near
        flags[x, 7:8, :] = near
        flags[x, 78:79, :] = (below[x, 25:26, :] * has_below).astype(I32)
        flags[x, 72:73, :] = (above[x, 24:25, :] * has_above).astype(I32)
        flags[x, 73:74, :] = (above[x, 25:26, :] * has_above).astype(I32)
        flags[x, 80:81, :] = mask[x, 0:1, :]
    for rows, x, dirs, far_below, far_above in (
        (fwd, nx - 1, CX_PLUS, 7, 9),
        (bwd, 0, CX_MINUS, 10, 8),
    ):
        e = 6 * ROWS
        for j, k in enumerate(dirs):
            rows[e + j : e + j + 1, :] = below[x, k : k + 1, :]
            rows[e + 8 + j : e + 9 + j, :] = above[x, k : k + 1, :]
        j = 19 + CY_PLUS.index(far_below)
        rows[e + 5 : e + 6, :] = below[x, j : j + 1, :]
        j = 19 + CY_MINUS.index(far_above)
        rows[e + 13 : e + 14, :] = above[x, j : j + 1, :]
        rows[e + 6 : e + 8, :] = below[x, 24:26, :] * has_below
        rows[e + 14 : e + 16, :] = above[x, 24:26, :] * has_above


def step_layer(x, read, read_mask, post, post2, bits_out):
    def body(t, carry):
        bits = open_bits(read_mask, t)
        own = [post[k, x, rows_of(t), :] for k in range(19)]
        out = collide(stream(read, own, bits, t))
        for k in range(19):
            post2[k, x, rows_of(t), :] = out[k]
        bits_out[x, tile_rows(t), :] = bits
        return carry

    lax.fori_loop(0, TILES + 1, body, 0)
    for k in CY_PLUS:
        post2[k, x, 7:8, :] = post2[k, x, 79:80, :]


def middle_kernel(nx, post, flags, post2, bits_out):
    for x in range(1, nx - 1):
        step_layer(
            x,
            lambda k, dx, tile, x=x: post[k, x - dx, rows_of(tile), :],
            lambda dx, tile, x=x: flags[x - dx, rows_of(tile), :],
            post,
            post2,
            bits_out,
        )


def outer_kernel(nx, first, post, flags, face, post2_in, bits_in, post2, bits_out, send, halo, halo_flags):
    x, near = (0, -1) if first else (nx - 1, nx)
    dirs, k_below, k_above = (CX_PLUS, 7, 9) if first else (CX_MINUS, 10, 8)
    e = 6 * ROWS
    for j, k in enumerate(dirs):
        halo[j, 8:72, :] = face[j * ROWS : (j + 1) * ROWS, :]
        halo[j, 79:80, :] = face[e + j : e + j + 1, :]
        halo[j, 72:73, :] = face[e + 8 + j : e + 9 + j, :]
        if k == k_below:
            halo[j, 7:8, :] = face[e + j : e + j + 1, :]
            halo[j, 78:79, :] = face[e + 5 : e + 6, :]
        if k == k_above:
            halo[j, 73:74, :] = face[e + 13 : e + 14, :]
            halo[j, 80:81, :] = face[j * ROWS : j * ROWS + 1, :]
    halo_flags[8:72, :] = face[5 * ROWS : 6 * ROWS, :].astype(I32)
    halo_flags[79:80, :] = face[e + 6 : e + 7, :].astype(I32)
    halo_flags[7:8, :] = face[e + 6 : e + 7, :].astype(I32)
    halo_flags[78:79, :] = face[e + 7 : e + 8, :].astype(I32)
    halo_flags[72:73, :] = face[e + 14 : e + 15, :].astype(I32)
    halo_flags[73:74, :] = face[e + 15 : e + 16, :].astype(I32)
    halo_flags[80:81, :] = face[5 * ROWS : 5 * ROWS + 1, :].astype(I32)

    def read(k, dx, tile):
        if x - dx == near:
            return halo[dirs.index(k), rows_of(tile), :]
        return post[k, x - dx, rows_of(tile), :]

    def read_mask(dx, tile):
        if x - dx == near:
            return halo_flags[rows_of(tile), :]
        return flags[x - dx, rows_of(tile), :]

    step_layer(x, read, read_mask, post, post2, bits_out)
    dirs, k_below, k_above = (CX_MINUS, 10, 8) if first else (CX_PLUS, 7, 9)
    for j, k in enumerate(dirs):
        send[j * ROWS : (j + 1) * ROWS, :] = post2[k, x, 8:72, :]
    send[320:321, :] = post2[k_below, x, 79:80, :]
    send[321:322, :] = post2[k_above, x, 72:73, :]


def final_layer(x, read, post2, bits, result, flow, out, sem):
    def body(t, carry):
        rows = tile_rows(t)
        own = [post2[k, x, rows_of(t), :] for k in range(19)]
        f = stream(read, own, bits[x, rows, :], t)
        for k in range(19):
            result[k, rows, :] = f[k]
        rho, ux, uy, uz = velocity_of(f)
        flow[0, x, rows, :] = ux
        flow[1, x, rows, :] = uy
        flow[2, x, rows, :] = uz
        return carry

    lax.fori_loop(0, TILES, body, 0)
    copy = pltpu.make_async_copy(result, out.at[:, x], sem)
    copy.start()
    return copy


def final_middle_kernel(nx, post2, bits, out, flow, result, sems):
    copies = []
    for i, x in enumerate(range(1, nx - 1)):
        read = lambda k, dx, tile, x=x: post2[k, x - dx, rows_of(tile), :]
        copies.append(final_layer(x, read, post2, bits, result.at[i], flow, out, sems.at[i]))
    for copy in copies:
        copy.wait()


def final_outer_kernel(nx, first, out_in, flow_in, post2, bits, face, out, flow, halo, result, sems):
    x, near = (0, -1) if first else (nx - 1, nx)
    dirs, k_below, k_above = (CX_PLUS, 7, 9) if first else (CX_MINUS, 10, 8)
    for j in range(5):
        halo[j, 8:72, :] = face[j * ROWS : (j + 1) * ROWS, :]
    halo[dirs.index(k_below), 7:8, :] = face[320:321, :]
    halo[dirs.index(k_above), 72:73, :] = face[321:322, :]

    def read(k, dx, tile):
        if x - dx == near:
            return halo[dirs.index(k), rows_of(tile), :]
        return post2[k, x - dx, rows_of(tile), :]

    final_layer(x, read, post2, bits, result, flow, out, sems.at[0]).wait()


def pair_kernel(first_patch, pair_tiles, pos, vel, noise, *refs):
    base, rows, cols, theta, acc = refs[-5:]
    g = pl.program_id(0) + first_patch
    tile = noise.shape[-1]
    count = pos.shape[-1] // tile
    pairs = noise.shape[1]
    both = [ref[c, pl.ds(g, 1), :] for ref in (pos, vel) for c in range(3)]
    speed = both[3:]
    both = [both[c] if c < 3 else 4.5 * both[c] for c in range(6)]
    stacked = jnp.concatenate(both + [jnp.zeros((2, both[0].shape[1]), F32)], axis=0)
    turned = stacked.T
    for c in range(6):
        for j in range(count):
            part = turned[j * tile : (j + 1) * tile, c : c + 1]
            cols[c, j] = jnp.broadcast_to(part, (tile, tile))
            rows[c, j] = jnp.broadcast_to(both[c][:, j * tile : (j + 1) * tile], (8, tile))
    acc[...] = jnp.zeros_like(acc)
    eye = lax.broadcasted_iota(I32, (tile, tile), 0) == lax.broadcasted_iota(I32, (tile, tile), 1)
    scale = jnp.where(eye, 15.0, 0.0).astype(BF16)
    for p in range(pairs):
        theta[p] = lax.dot_general(
            scale, noise[0, p], (((1,), (1,)), ((), ())), preferred_element_type=F32
        )

    def one_pair(p, carry):
        first = pair_tiles[g, 0, p]
        second = pair_tiles[g, 1, p]
        mine = [rows[c, first] for c in range(6)]
        parts = []
        for s in range(tile // 8):
            part = slice(8 * s, 8 * s + 8)
            dx, dy, dz = [mine[c] - cols[c, second, part, :] for c in range(3)]
            vx, vy, vz = [mine[c] - cols[c, second, part, :] for c in range(3, 6)]
            square = (dx * dx + 0.01) + (dy * dy + dz * dz)
            close = jnp.maximum(lax.rsqrt(square) - 1.0, 0.0)
            along = dx * vx + (dy * vy + dz * vz)
            force = close * ((theta[p, part, :] + 25.0) - close * along)
            here = [force * dx, force * dy, force * dz]
            parts = here if not parts else [a + b for a, b in zip(parts, here)]
        for c in range(3):
            acc[first, c] += parts[c]
        return carry

    lax.fori_loop(0, pairs, one_pair, 0)
    for c in range(3):
        force = jnp.concatenate(
            [jnp.sum(acc[j, c], axis=0, keepdims=True) for j in range(count)], axis=1
        )
        base[c, pl.ds(g, 1), :] = 0.5 * speed[c] + 0.04 * force


def split(value):
    high = value.astype(BF16)
    return high, (value - high.astype(F32)).astype(BF16)


def ranks(owner, count):
    out = []
    for g in range(count):
        rank = jnp.int32(0)
        for h in range(g):
            rank = rank + (owner[h] == owner[g]).astype(I32)
        out.append(rank)
    return out


def one_hot(index, extent):
    want = index.astype(F32).astype(BF16)
    place = lax.broadcasted_iota(I32, (extent, index.shape[1]), 0).astype(F32).astype(BF16)
    return place == want


def scatter_kernel(n, per, owner, voxel, vel, *refs):
    sent, out, table = refs[: n - 1], refs[n - 1], refs[n]
    me = lax.axis_index("xs")
    beads = voxel.shape[1]
    for r in range(per):
        for c in range(3):
            table[me, r, c : c + 1, :] = vel[c, pl.ds(me * per + r, 1), :]
        for d in range(1, n):
            source = lax.rem(me + n - d, n)
            for c in range(3):
                table[source, r, c : c + 1, :] = sent_velocity(sent, n, d, r, c)
    out[...] = jnp.zeros_like(out)
    rank = ranks(owner, voxel.shape[0])
    one, zero = BF16(1), BF16(0)
    for g in range(voxel.shape[0]):
        index = voxel[g : g + 1, :]
        lanes = jnp.where(one_hot(index & 255, 256), one, zero)
        at_row = one_hot(index >> 8, out.shape[1])
        values = table[owner[g], rank[g]]
        lanes2 = jnp.concatenate([lanes, lanes], axis=1)
        for c in range(3):
            high, low = split(values[c : c + 1, :])
            left = jnp.concatenate(
                [jnp.where(at_row, high, zero), jnp.where(at_row, low, zero)], axis=1
            )
            out[c] += lax.dot_general(
                left, lanes2, (((1,), (1,)), ((), ())), preferred_element_type=F32
            )
        out[3] += lax.dot_general(
            jnp.where(at_row, one, zero), lanes, (((1,), (1,)), ((), ())), preferred_element_type=F32
        )


def found_flow(voxel, flow, layers, field, store):
    patches, beads = voxel.shape
    rows = len(layers) * ROWS
    for c in range(3):
        for i, x in enumerate(layers):
            high, low = split(flow[c, x])
            field[c, i * ROWS : (i + 1) * ROWS, 0:256] = high
            field[c, i * ROWS : (i + 1) * ROWS, 256:512] = low
    place = lax.broadcasted_iota(I32, (rows, beads), 0)
    step = (layers[1] - layers[0] - 1) * ROWS
    place = place + layers[0] * ROWS + jnp.where(place >= ROWS, step, 0)
    one, zero = BF16(1), BF16(0)
    for g in range(patches):
        index = voxel[g : g + 1, :]
        lanes = jnp.where(one_hot(index & 255, 256), one, zero)
        lanes2 = jnp.concatenate([lanes, lanes], axis=0)
        at_row = place == (index >> 8)
        for c in range(3):
            found = lax.dot_general(
                field[c], lanes2, (((1,), (0,)), ((), ())), preferred_element_type=F32
            )
            store(g, c, jnp.sum(jnp.where(at_row, found, 0.0), axis=0, keepdims=True))


def gather_middle_kernel(layers, voxel, flow, table, field):
    def store(g, c, row):
        table[g, c : c + 1, :] = row

    found_flow(voxel, flow, layers, field, store)


def gather_outer_kernel(n, per, layers, owner, voxel, flow, part, *refs):
    outs, table, field = refs[:n], refs[n], refs[n + 1]
    patches = voxel.shape[0]

    def store(g, c, row):
        table[g, c : c + 1, :] = part[g, c : c + 1, :] + row

    found_flow(voxel, flow, layers, field, store)
    me = lax.axis_index("xs")
    rank = ranks(owner, patches)
    for d in range(n):
        target = me ^ d
        for r in range(per):
            found = jnp.int32(0)
            for g in range(patches):
                found = jnp.where((owner[g] == target) & (rank[g] == r), g, found)
            outs[d][r * 3 : r * 3 + 3, :] = table[found, 0:3, :]


def field_kernel(total, flow, field):
    for x in range(field.shape[1]):
        rows = slice(x * ROWS, (x + 1) * ROWS)
        number = 10.0 * total[3, rows, :]
        for c in range(3):
            field[c, x] = 0.5 * total[c, rows, :] - number * flow[c, x]


def final_kernel(n, per, pos, base, *refs):
    flows, new_pos, new_vel = refs[:n], refs[n], refs[n + 1]
    me = lax.axis_index("xs")
    for d in range(n):
        source = me ^ d
        for r in range(per):
            at = pl.ds(source * per + r, 1)
            for c in range(3):
                speed = base[c, at, :] + 10.0 * flows[d][r * 3 + c : r * 3 + c + 1, :]
                new_vel[c, at, :] = speed
                new_pos[c, at, :] = pos[c, at, :] + 0.04 * speed


def shift(value, axis, by):
    n = lax.axis_size(axis)
    return lax.ppermute(value, axis, [(i, (i + by) % n) for i in range(n)])


def swap(value, axis, by):
    n = lax.axis_size(axis)
    return lax.ppermute(value, axis, [(i, i ^ by) for i in range(n)])


def pair_call(first_patch, patches, pair_tiles, pos, vel, noise, given, after):
    beads = pos.shape[2]
    tile = noise.shape[-1]
    count = beads // tile
    whole = lambda g, s: (0, 0, 0)
    ins = [pos, vel, noise] + given + after
    return pl.pallas_call(
        functools.partial(pair_kernel, first_patch),
        grid_spec=pltpu.PrefetchScalarGridSpec(
            num_scalar_prefetch=1,
            grid=(patches,),
            in_specs=[
                pl.BlockSpec(pos.shape, whole),
                pl.BlockSpec(vel.shape, whole),
                pl.BlockSpec((1,) + noise.shape[1:], lambda g, s: (g + first_patch, 0, 0, 0)),
            ]
            + [pl.BlockSpec(pos.shape, whole)] * len(given)
            + [ANY_SPEC] * len(after),
            out_specs=pl.BlockSpec(pos.shape, whole),
            scratch_shapes=[
                pltpu.VMEM((6, count, 8, tile), F32),
                pltpu.VMEM((6, count, tile, tile), F32),
                pltpu.VMEM(noise.shape[1:], F32),
                pltpu.VMEM((count, 3, 8, tile), F32),
            ],
        ),
        out_shape=jax.ShapeDtypeStruct(pos.shape, F32),
        input_output_aliases={4: 0} if given else {},
        compiler_params=params(),
        cost_estimate=cost(3_000_000_000, 1_500_000),
        name="pair_forces",
    )(pair_tiles, *ins)


def per_device(
    populations, fluid_mask, patch_voxel, patch_owner, positions, velocities, pair_tiles, pair_noise
):
    n = lax.axis_size("xs")
    patches, beads = patch_voxel.shape
    per = patches // n
    nx = populations.shape[1]
    lanes = populations.shape[3]
    arr = lambda *shape: jax.ShapeDtypeStruct(shape, F32)
    ints = lambda *shape: jax.ShapeDtypeStruct(shape, I32)
    vmem, dma = pltpu.VMEM, pltpu.SemaphoreType.DMA
    positions = jnp.transpose(positions, (1, 0, 2))
    velocities = jnp.transpose(velocities, (1, 0, 2))
    pair_tiles = jnp.transpose(pair_tiles, (0, 2, 1))

    post, fwd, bwd, up, down, *others = call(
        functools.partial(collide_kernel, n, per, nx),
        [in_hbm(populations), in_hbm(fluid_mask), in_hbm(velocities)],
        [
            arr(19, nx, PAD, lanes),
            arr(400, lanes),
            arr(400, lanes),
            arr(nx, 32, lanes),
            arr(nx, 32, lanes),
        ]
        + [arr(16, lanes)] * (n - 3),
        "collide_first",
        cost(3_000_000_000, 11_000_000),
        specs={0: ANY_SPEC, 1: ANY_SPEC, 2: ANY_SPEC},
        out_specs=[VMEM_SPEC] * (5 + n - 3),
        scratch_shapes=[vmem((nx, 19, ROWS, lanes), F32), vmem((nx, ROWS, lanes), I32), vmem(velocities.shape, F32), dma((nx + 2,))],
    )
    below = shift(up, "xs", 1)
    above = shift(down, "xs", -1)
    sent = [below] + [shift(other, "xs", d + 2) for d, other in enumerate(others)] + [above]

    half = patches // 2
    bead_args = (pair_tiles, positions, velocities, pair_noise)
    base = pair_call(0, half, *bead_args, [], [down])

    post, fwd, bwd, flags = call(
        functools.partial(edges_kernel, n, nx),
        [post, fwd, bwd, fluid_mask, below, above],
        [arr(*post.shape), arr(*fwd.shape), arr(*bwd.shape), ints(nx, PAD, lanes)],
        "edges",
        cost(1000, 100_000),
        after=[base],
        out_specs=[VMEM_SPEC] * 4,
        input_output_aliases={0: 0, 1: 1, 2: 2},
    )
    before = shift(fwd, "ax", 1)
    after = shift(bwd, "ax", -1)

    post2, bits = call(
        functools.partial(middle_kernel, nx),
        [post, flags],
        [arr(19, nx, PAD, lanes), ints(nx, 72, lanes)],
        "middle_layers",
        cost(3_000_000_000, 9_000_000),
        out_specs=[VMEM_SPEC] * 2,
    )
    base = pair_call(half, patches - half, *bead_args, [base], [flags])

    def outer(first, face, post2, bits, after):
        return call(
            functools.partial(outer_kernel, nx, first),
            [post, flags, face, post2, bits],
            [arr(*post2.shape), ints(*bits.shape), arr(328, lanes)],
            "first_layer" if first else "last_layer",
            cost(1_500_000_000, 5_000_000),
            after=after,
            out_specs=[VMEM_SPEC] * 3,
            input_output_aliases={3: 0, 4: 1},
            scratch_shapes=[vmem((5, PAD, lanes), F32), vmem((PAD, lanes), I32)],
        )

    post2, bits, bwd2 = outer(True, before, post2, bits, [base])
    after2 = shift(bwd2, "ax", -1)
    post2, bits, fwd2 = outer(False, after, post2, bits, [])
    before2 = shift(fwd2, "ax", 1)

    out, flow = call(
        functools.partial(final_middle_kernel, nx),
        [post2, bits],
        [arr(*populations.shape), arr(3, nx, ROWS, lanes)],
        "final_middle",
        cost(3_000_000_000, 7_000_000),
        out_specs=[ANY_SPEC, VMEM_SPEC],
        scratch_shapes=[vmem((nx - 2, 19, ROWS, lanes), F32), dma((nx - 2,))],
    )
    total = call(
        functools.partial(scatter_kernel, n, per),
        [patch_owner, patch_voxel, velocities] + sent,
        arr(4, nx * ROWS, lanes),
        "bead_sums",
        cost(3_000_000_000, 1_500_000),
        after=[fwd2],
        specs={0: SMEM_SPEC},
        out_specs=VMEM_SPEC,
        scratch_shapes=[vmem((n, per, 8, beads), F32)],
    )
    part = call(
        functools.partial(gather_middle_kernel, list(range(1, nx - 1))),
        [patch_voxel, flow],
        arr(patches, 8, beads),
        "flow_middle",
        cost(3_000_000_000, 1_500_000),
        out_specs=VMEM_SPEC,
        scratch_shapes=[vmem((3, (nx - 2) * ROWS, 2 * lanes), BF16)],
    )

    def final_outer(first, face, out, flow, after):
        return call(
            functools.partial(final_outer_kernel, nx, first),
            [out, flow, post2, bits, face],
            [arr(*populations.shape), arr(*flow.shape)],
            "final_first" if first else "final_last",
            cost(1_500_000_000, 4_000_000),
            after=after,
            specs={0: ANY_SPEC},
            out_specs=[ANY_SPEC, VMEM_SPEC],
            input_output_aliases={0: 0, 1: 1},
            scratch_shapes=[vmem((5, PAD, lanes), F32), vmem((19, ROWS, lanes), F32), dma((1,))],
        )

    out, flow = final_outer(False, after2, out, flow, [total, part])
    out, flow = final_outer(True, before2, out, flow, [])
    flows = call(
        functools.partial(gather_outer_kernel, n, per, [0, nx - 1]),
        [patch_owner, patch_voxel, flow, part],
        [arr(8, beads)] * n,
        "flow_outer",
        cost(3_000_000_000, 1_500_000),
        specs={0: SMEM_SPEC},
        out_specs=[VMEM_SPEC] * n,
        scratch_shapes=[vmem((patches, 8, beads), F32), vmem((3, 2 * ROWS, 2 * lanes), BF16)],
    )
    sent_flows = [flows[0]] + [swap(flows[d], "xs", d) for d in range(1, n)]
    field = call(
        field_kernel,
        [total, flow],
        arr(3, nx, ROWS, lanes),
        "drag_field",
        cost(400_000_000, 2_500_000),
        after=[flows[1]],
        out_specs=VMEM_SPEC,
    )
    new_pos, new_vel = call(
        functools.partial(final_kernel, n, per),
        [positions, base] + sent_flows,
        [arr(*positions.shape)] * 2,
        "bead_update",
        cost(50_000, 300_000),
        out_specs=[VMEM_SPEC] * 2,
    )
    return out, jnp.transpose(new_pos, (1, 0, 2)), jnp.transpose(new_vel, (1, 0, 2)), field


def solution(mesh):
    return jax.shard_map(
        per_device,
        mesh=mesh,
        in_specs=(
            P(None, "ax", "xs", None),
            P("ax", "xs", None),
            P(("ax", "xs"), None),
            P(("ax", "xs")),
            P(("ax", "xs"), None, None),
            P(("ax", "xs"), None, None),
            P(("ax", "xs"), None, None),
            P(("ax", "xs"), None, None, None),
        ),
        out_specs=(
            P(None, "ax", "xs", None),
            P(("ax", "xs"), None, None),
            P(("ax", "xs"), None, None),
            P(None, "ax", "xs", None),
        ),
        check_vma=False,
    )
```

```python
import functools

import jax
import jax.numpy as jnp
from jax import lax
from jax.experimental import pallas as pl
from jax.experimental.pallas import tpu as pltpu
from jax.sharding import PartitionSpec as P

DIRS = [
    (0, 0, 0),
    (1, 0, 0),
    (-1, 0, 0),
    (0, 1, 0),
    (0, -1, 0),
    (0, 0, 1),
    (0, 0, -1),
    (1, 1, 0),
    (-1, -1, 0),
    (1, -1, 0),
    (-1, 1, 0),
    (1, 0, 1),
    (-1, 0, -1),
    (1, 0, -1),
    (-1, 0, 1),
    (0, 1, 1),
    (0, -1, -1),
    (0, 1, -1),
    (0, -1, 1),
]
OPP = [0, 2, 1, 4, 3, 6, 5, 8, 7, 10, 9, 12, 11, 14, 13, 16, 15, 18, 17]
CX_PLUS = [k for k in range(19) if DIRS[k][0] == 1]
CX_MINUS = [k for k in range(19) if DIRS[k][0] == -1]
CY_PLUS = [k for k in range(19) if DIRS[k][1] == 1]
CY_MINUS = [k for k in range(19) if DIRS[k][1] == -1]
F32 = jnp.float32
BF16 = jnp.bfloat16
I32 = jnp.int32
VMEM_SPEC = pl.BlockSpec(memory_space=pltpu.VMEM)
SMEM_SPEC = pl.BlockSpec(memory_space=pltpu.SMEM)
ANY_SPEC = pl.BlockSpec(memory_space=pl.ANY)

ROWS = 64
PAD = 88
TILES = ROWS // 8


def params(mib=16):
    return pltpu.CompilerParams(vmem_limit_bytes=mib * 1024 * 1024)


def cost(flops, bytes_accessed):
    return pl.CostEstimate(flops=flops, bytes_accessed=bytes_accessed, transcendentals=0)


def call(kernel, ins, out_shape, name, estimate, after=(), specs=None, **kwargs):
    specs = specs or {}
    count, extra = len(ins), len(after)

    def body(*refs):
        kernel(*refs[:count], *refs[count + extra :])

    return pl.pallas_call(
        body,
        in_specs=[specs.get(i, VMEM_SPEC) for i in range(count)] + [ANY_SPEC] * extra,
        out_shape=out_shape,
        cost_estimate=estimate,
        name=name,
        **{"compiler_params": params(), **kwargs},
    )(*ins, *after)


def in_hbm(value):
    return pltpu.with_memory_space_constraint(value, pltpu.HBM)


def tree(values):
    while len(values) > 1:
        values = [
            values[i] + values[i + 1] if i + 1 < len(values) else values[i]
            for i in range(0, len(values), 2)
        ]
    return values[0]


def velocity_of(f):
    diff = [None] + [f[k] - f[k + 1] for k in range(1, 19, 2)]
    rho = tree([f[k] for k in range(1, 19)] + [f[0]])
    m1, m3, m5, m7, m9, m11, m13, m15, m17 = diff[1:]
    jx = m1 + ((m7 + m9) + (m11 + m13))
    jy = m3 + ((m7 - m9) + (m15 + m17))
    jz = m5 + ((m11 - m13) + (m15 - m17))
    inv = 1.0 / rho
    return rho, jx * inv, jy * inv, jz * inv


def collide(f):
    rho, ux, uy, uz = velocity_of(f)
    base = (1.25 * rho) * (1.0 - 1.5 * (ux * ux + uy * uy + uz * uz))
    ux, uy, uz = 1.5 * ux, 1.5 * uy, 1.5 * uz
    even1, even2 = base * (1.0 / 18.0), base * (1.0 / 36.0)
    odd1, odd2 = rho * (2.5 / 18.0), rho * (2.5 / 36.0)
    out = [None] * 19
    out[0] = base * (1.0 / 3.0) - 0.25 * f[0]
    for k in range(1, 19, 2):
        dx, dy, dz = DIRS[k]
        proj = None
        for sign, comp in ((dx, ux), (dy, uy), (dz, uz)):
            if sign == 0:
                continue
            if proj is None:
                proj = comp
            else:
                proj = proj + comp if sign > 0 else proj - comp
        even, odd = (even1, odd1) if k < 7 else (even2, odd2)
        odd = odd * proj
        even = even + odd * proj
        out[k] = (even + odd) - 0.25 * f[k]
        out[k + 1] = (even - odd) - 0.25 * f[k + 1]
    return out


def shifted(read, tile, dy, dz):
    here = read(tile)
    if dy != 0:
        sub = lax.broadcasted_iota(I32, here.shape, 0)
        if dy > 0:
            here = pltpu.roll(jnp.where(sub == 7, read(tile - 1), here), 1, 0)
        else:
            here = pltpu.roll(jnp.where(sub == 0, read(tile + 1), here), 7, 0)
    if dz != 0:
        here = pltpu.roll(here, 1 if dz > 0 else here.shape[1] - 1, 1)
    return here


def rows_of(tile):
    return pl.ds(pl.multiple_of(8 + 8 * tile, 8), 8)


def open_bits(read_mask, tile):
    bits = None
    cache = {}
    for k in range(1, 19):
        dx, dy, dz = DIRS[k]
        if (dx, dy) not in cache:
            cache[(dx, dy)] = shifted(functools.partial(read_mask, dx), tile, dy, 0)
        m = cache[(dx, dy)]
        if dz != 0:
            lane = lax.broadcasted_iota(I32, m.shape, 1)
            last = m.shape[1] - 1
            m = pltpu.roll(m, 1 if dz > 0 else last, 1)
            m = jnp.where(lane == (0 if dz > 0 else last), 0, m)
        m = m << k
        bits = m if bits is None else bits | m
    return bits


def stream(read, own, bits, tile):
    out = [own[0]]
    for k in range(1, 19):
        dx, dy, dz = DIRS[k]
        source = shifted(functools.partial(read, k, dx), tile, dy, dz)
        out.append(jnp.where((bits & (1 << k)) != 0, source, own[OPP[k]]))
    return out


def tile_rows(t):
    return pl.ds(pl.multiple_of(8 * t, 8), 8)


def collide_kernel(n, per, nx, pop, mask, vel, post, fwd, bwd, up, down, *rest):
    others, (here, flags, speeds, sems, small) = rest[: n - 3], rest[n - 3 :]
    order = [(x, h) for x in [0, nx - 1] + list(range(1, nx - 1)) for h in range(1)]
    span = ROWS // 1
    copies = [
        pltpu.make_async_copy(
            pop.at[:, x, pl.ds(h * span, span)], here.at[x, :, pl.ds(h * span, span)], sems.at[i]
        )
        for i, (x, h) in enumerate(order)
    ]
    extra = [
        pltpu.make_async_copy(vel, speeds, small.at[0]),
        pltpu.make_async_copy(mask, flags, small.at[1]),
    ]
    ahead = 3
    for copy in copies[:ahead] + extra:
        copy.start()
    me = lax.axis_index("xs")
    extra[0].wait()
    for d in range(1, n):
        target = lax.rem(me + d, n)
        for r in range(per):
            for c in range(3):
                row = speeds[c, pl.ds(target * per + r, 1), :]
                for half in range(2):
                    i = (r * 3 + c) * 2 + half
                    piece = row[:, half * 256 : (half + 1) * 256]
                    if d in (1, n - 1):
                        ref = up if d == 1 else down
                        ref[i // 3, 26 + i % 3 : 27 + i % 3, :] = piece
                    else:
                        others[d - 2][i : i + 1, :] = piece
    extra[1].wait()
    for i, (x, h) in enumerate(order):
        copies[i].wait()
        if i + ahead < len(copies):
            copies[i + ahead].start()

        def body(t, carry, x=x, h=h):
            t = t + h * (TILES // 1)
            out = collide([here[x, k, tile_rows(t), :] for k in range(19)])
            for k in range(19):
                post[k, x, rows_of(t), :] = out[k]
            return carry

        lax.fori_loop(0, TILES // 1, body, 0, unroll=TILES // 1)
        for ref, near, beyond, dirs in ((down, 0, 1, CY_MINUS), (up, ROWS - 1, ROWS - 2, CY_PLUS)):
            for k in range(19):
                ref[x, k : k + 1, :] = post[k, x, 8 + near : 9 + near, :]
            for j, k in enumerate(dirs):
                ref[x, 19 + j : 20 + j, :] = post[k, x, 8 + beyond : 9 + beyond, :]
            ref[x, 24:25, :] = flags[x, near : near + 1, :].astype(F32)
            ref[x, 25:26, :] = flags[x, beyond : beyond + 1, :].astype(F32)
    for x, ref, dirs in ((nx - 1, fwd, CX_PLUS), (0, bwd, CX_MINUS)):
        for j, k in enumerate(dirs):
            ref[j * ROWS : (j + 1) * ROWS, :] = post[k, x, 8:72, :]
        ref[5 * ROWS : 6 * ROWS, :] = flags[x].astype(F32)


def sent_velocity(refs, n, d, r, c):
    out = []
    for half in range(2):
        i = (r * 3 + c) * 2 + half
        if d in (1, n - 1):
            out.append(refs[d - 1][i // 3, 26 + i % 3 : 27 + i % 3, :])
        else:
            out.append(refs[d - 1][i : i + 1, :])
    return jnp.concatenate(out, axis=1)


def edges_kernel(n, nx, post_in, mask, below, above, post, fwd, bwd, flags):
    me = lax.axis_index("xs")
    has_below, has_above = (me > 0).astype(F32), (me < n - 1).astype(F32)
    for x in range(nx):
        for k in range(19):
            post[k, x, 79:80, :] = below[x, k : k + 1, :]
            post[k, x, 72:73, :] = above[x, k : k + 1, :]
        for j, k in enumerate(CY_PLUS):
            post[k, x, 7:8, :] = below[x, k : k + 1, :]
            post[k, x, 78:79, :] = below[x, 19 + j : 20 + j, :]
        for j, k in enumerate(CY_MINUS):
            post[k, x, 73:74, :] = above[x, 19 + j : 20 + j, :]
            post[k, x, 80:81, :] = post[k, x, 8:9, :]
        flags[x, 8:72, :] = mask[x]
        near = (below[x, 24:25, :] * has_below).astype(I32)
        flags[x, 79:80, :] = near
        flags[x, 7:8, :] = near
        flags[x, 78:79, :] = (below[x, 25:26, :] * has_below).astype(I32)
        flags[x, 72:73, :] = (above[x, 24:25, :] * has_above).astype(I32)
        flags[x, 73:74, :] = (above[x, 25:26, :] * has_above).astype(I32)
        flags[x, 80:81, :] = mask[x, 0:1, :]
    for rows, x, dirs, far_below, far_above in (
        (fwd, nx - 1, CX_PLUS, 7, 9),
        (bwd, 0, CX_MINUS, 10, 8),
    ):
        for j, k in enumerate(dirs):
            rows[j : j + 1, :] = below[x, k : k + 1, :]
            rows[8 + j : 9 + j, :] = above[x, k : k + 1, :]
        j = 19 + CY_PLUS.index(far_below)
        rows[5:6, :] = below[x, j : j + 1, :]
        j = 19 + CY_MINUS.index(far_above)
        rows[13:14, :] = above[x, j : j + 1, :]
        rows[6:8, :] = below[x, 24:26, :] * has_below
        rows[14:16, :] = above[x, 24:26, :] * has_above


def step_layer(x, read, read_mask, post, post2, bits_out):
    def body(t, carry):
        bits = open_bits(read_mask, t)
        own = [post[k, x, rows_of(t), :] for k in range(19)]
        out = collide(stream(read, own, bits, t))
        for k in range(19):
            post2[k, x, rows_of(t), :] = out[k]
        bits_out[x, tile_rows(t), :] = bits
        return carry

    lax.fori_loop(0, TILES + 1, body, 0, unroll=TILES + 1)
    for k in CY_PLUS:
        post2[k, x, 7:8, :] = post2[k, x, 79:80, :]


def middle_kernel(nx, post, flags, post2, bits_out):
    for x in range(1, nx - 1):
        step_layer(
            x,
            lambda k, dx, tile, x=x: post[k, x - dx, rows_of(tile), :],
            lambda dx, tile, x=x: flags[x - dx, rows_of(tile), :],
            post,
            post2,
            bits_out,
        )


def outer_kernel(
    nx, first, post, flags, face, edge, post2_in, bits_in, post2, bits_out, send, halo, halo_flags
):
    x, near = (0, -1) if first else (nx - 1, nx)
    dirs, k_below, k_above = (CX_PLUS, 7, 9) if first else (CX_MINUS, 10, 8)
    for j, k in enumerate(dirs):
        halo[j, 8:72, :] = face[j * ROWS : (j + 1) * ROWS, :]
        halo[j, 79:80, :] = edge[j : j + 1, :]
        halo[j, 72:73, :] = edge[8 + j : 9 + j, :]
        if k == k_below:
            halo[j, 7:8, :] = edge[j : j + 1, :]
            halo[j, 78:79, :] = edge[5:6, :]
        if k == k_above:
            halo[j, 73:74, :] = edge[13:14, :]
            halo[j, 80:81, :] = face[j * ROWS : j * ROWS + 1, :]
    halo_flags[8:72, :] = face[5 * ROWS : 6 * ROWS, :].astype(I32)
    halo_flags[79:80, :] = edge[6:7, :].astype(I32)
    halo_flags[7:8, :] = edge[6:7, :].astype(I32)
    halo_flags[78:79, :] = edge[7:8, :].astype(I32)
    halo_flags[72:73, :] = edge[14:15, :].astype(I32)
    halo_flags[73:74, :] = edge[15:16, :].astype(I32)
    halo_flags[80:81, :] = face[5 * ROWS : 5 * ROWS + 1, :].astype(I32)

    def read(k, dx, tile):
        if x - dx == near:
            return halo[dirs.index(k), rows_of(tile), :]
        return post[k, x - dx, rows_of(tile), :]

    def read_mask(dx, tile):
        if x - dx == near:
            return halo_flags[rows_of(tile), :]
        return flags[x - dx, rows_of(tile), :]

    step_layer(x, read, read_mask, post, post2, bits_out)
    dirs, k_below, k_above = (CX_MINUS, 10, 8) if first else (CX_PLUS, 7, 9)
    for j, k in enumerate(dirs):
        send[j * ROWS : (j + 1) * ROWS, :] = post2[k, x, 8:72, :]
    send[320:321, :] = post2[k_below, x, 79:80, :]
    send[321:322, :] = post2[k_above, x, 72:73, :]


def final_layer(x, read, post2, bits, result, flow, out, sem):
    def body(t, carry):
        rows = tile_rows(t)
        own = [post2[k, x, rows_of(t), :] for k in range(19)]
        f = stream(read, own, bits[x, rows, :], t)
        for k in range(19):
            result[k, rows, :] = f[k]
        rho, ux, uy, uz = velocity_of(f)
        flow[0, x, rows, :] = ux
        flow[1, x, rows, :] = uy
        flow[2, x, rows, :] = uz
        return carry

    lax.fori_loop(0, TILES, body, 0, unroll=TILES)
    copy = pltpu.make_async_copy(result, out.at[:, x], sem)
    copy.start()
    return copy


def final_middle_kernel(nx, post2, bits, voxel, out, flow, table, result, field, sems):
    copies = []
    for i, x in enumerate(range(1, nx - 1)):
        read = lambda k, dx, tile, x=x: post2[k, x - dx, rows_of(tile), :]
        copies.append(final_layer(x, read, post2, bits, result.at[i], flow, out, sems.at[i]))

    def store(g, c, row):
        table[g, c : c + 1, :] = row

    found_flow(voxel, flow, list(range(1, nx - 1)), field, store)
    for copy in copies:
        copy.wait()


def final_outer_kernel(
    n, per, nx, out_in, flow_in, post2, bits, after, before, voxel, owner, part, out, flow, *refs
):
    outs, (halo, result, table, field, sems) = refs[:n], refs[n:]
    copies = []
    for i, (face, first) in enumerate(((after, False), (before, True))):
        x, near = (0, -1) if first else (nx - 1, nx)
        dirs, k_below, k_above = (CX_PLUS, 7, 9) if first else (CX_MINUS, 10, 8)
        for j in range(5):
            halo[i, j, 8:72, :] = face[j * ROWS : (j + 1) * ROWS, :]
        halo[i, dirs.index(k_below), 7:8, :] = face[320:321, :]
        halo[i, dirs.index(k_above), 72:73, :] = face[321:322, :]

        def read(k, dx, tile, i=i, x=x, near=near, dirs=dirs):
            if x - dx == near:
                return halo[i, dirs.index(k), rows_of(tile), :]
            return post2[k, x - dx, rows_of(tile), :]

        copies.append(final_layer(x, read, post2, bits, result.at[i], flow, out, sems.at[i]))

    def store(g, c, row):
        table[g, c : c + 1, :] = part[g, c : c + 1, :] + row

    found_flow(voxel, flow, [0, nx - 1], field, store)
    patches = voxel.shape[0]
    me = lax.axis_index("xs")
    rank = ranks(owner, patches)
    for d in range(n):
        target = me ^ d
        for r in range(per):
            found = jnp.int32(0)
            for g in range(patches):
                found = jnp.where((owner[g] == target) & (rank[g] == r), g, found)
            outs[d][r * 3 : r * 3 + 3, :] = table[found, 0:3, :]
    for copy in copies:
        copy.wait()


def pair_kernel(begin, end, pair_tiles, pos, vel, noise, *refs):
    base, rows, cols, theta, acc = refs[-5:]
    tile = noise.shape[-1]
    count = pos.shape[-1] // tile
    pairs = noise.shape[1]
    patches = end - begin
    spread = (lax.broadcasted_iota(I32, (24, 6 * tile), 0) & 7) == (
        lax.broadcasted_iota(I32, (24, 6 * tile), 1) // tile
    )
    spread = jnp.where(spread, 1.0, 0.0).astype(BF16)
    eye = lax.broadcasted_iota(I32, (tile, tile), 0) == lax.broadcasted_iota(I32, (tile, tile), 1)
    scale = jnp.where(eye, 15.0, 0.0).astype(BF16)
    empty = jnp.zeros((2, pos.shape[-1]), F32)
    parts, speeds = [], []
    for g in range(patches):
        both = [ref[c, begin + g : begin + g + 1, :] for ref in (pos, vel) for c in range(3)]
        speeds.append(both[3:])
        both = [both[c] if c < 3 else 4.5 * both[c] for c in range(6)]
        for c in range(6):
            for j in range(count):
                rows[g, c, j] = jnp.broadcast_to(both[c][:, j * tile : (j + 1) * tile], (8, tile))
        stacked = jnp.concatenate(both + [empty], axis=0)
        high, rest = stacked.astype(BF16), stacked - stacked.astype(BF16).astype(F32)
        mid, low = rest.astype(BF16), rest - rest.astype(BF16).astype(F32)
        parts += [high.astype(F32), mid.astype(F32), low]
    used = 24 * patches
    parts.append(jnp.zeros((-used % 128, pos.shape[-1]), F32))
    parts = jnp.concatenate(parts, axis=0).T.astype(BF16)
    acc[...] = jnp.zeros_like(acc)
    for g in range(patches):
        for j in range(count):
            left = parts[j * tile : (j + 1) * tile, 24 * g : 24 * (g + 1)]
            wide = jnp.dot(left, spread, preferred_element_type=F32)
            for c in range(6):
                cols[g, c, j] = wide[:, c * tile : (c + 1) * tile]
        for p in range(pairs):
            theta[g * pairs + p] = lax.dot_general(
                scale, noise[begin + g, p], (((1,), (1,)), ((), ())), preferred_element_type=F32
            )

    def one_pair(i, carry):
        g, p = i // pairs, i % pairs
        first = pair_tiles[begin + g, 0, p]
        second = pair_tiles[begin + g, 1, p]
        mine = [rows[g, c, first] for c in range(6)]
        total = []
        for s in range(tile // 8):
            part = slice(8 * s, 8 * s + 8)
            dx, dy, dz = [mine[c] - cols[g, c, second, part, :] for c in range(3)]
            vx, vy, vz = [mine[c] - cols[g, c, second, part, :] for c in range(3, 6)]
            square = (dx * dx + 0.01) + (dy * dy + dz * dz)
            close = jnp.maximum(lax.rsqrt(square) - 1.0, 0.0)
            along = dx * vx + (dy * vy + dz * vz)
            force = close * ((theta[i, part, :] + 25.0) - close * along)
            here = [force * dx, force * dy, force * dz]
            total = here if not total else [a + b for a, b in zip(total, here)]
        for c in range(3):
            acc[g, first, c] += total[c]
        return carry

    lax.fori_loop(0, patches * pairs, one_pair, 0, unroll=4)
    for g in range(patches):
        for c in range(3):
            force = jnp.concatenate(
                [jnp.sum(acc[g, j, c], axis=0, keepdims=True) for j in range(count)], axis=1
            )
            base[c, begin + g : begin + g + 1, :] = 0.5 * speeds[g][c] + 0.04 * force


def split(value):
    high = value.astype(BF16)
    return high, (value - high.astype(F32)).astype(BF16)


def ranks(owner, count):
    out = []
    for g in range(count):
        rank = jnp.int32(0)
        for h in range(g):
            rank = rank + (owner[h] == owner[g]).astype(I32)
        out.append(rank)
    return out


def one_hot(index, extent):
    want = index.astype(F32).astype(BF16)
    place = lax.broadcasted_iota(I32, (extent, index.shape[1]), 0).astype(F32).astype(BF16)
    return place == want


def scatter_kernel(n, per, owner, voxel, vel, *refs):
    sent, out, table = refs[: n - 1], refs[n - 1], refs[n]
    me = lax.axis_index("xs")
    beads = voxel.shape[1]
    for r in range(per):
        for c in range(3):
            table[me, r, c : c + 1, :] = vel[c, pl.ds(me * per + r, 1), :]
        for d in range(1, n):
            source = lax.rem(me + n - d, n)
            for c in range(3):
                table[source, r, c : c + 1, :] = sent_velocity(sent, n, d, r, c)
    out[...] = jnp.zeros_like(out)
    rank = ranks(owner, voxel.shape[0])
    one, zero = BF16(1), BF16(0)
    for g in range(voxel.shape[0]):
        index = voxel[g : g + 1, :]
        lanes = jnp.where(one_hot(index & 255, 256), one, zero)
        at_row = one_hot(index >> 8, out.shape[1])
        values = table[owner[g], rank[g]]
        lanes2 = jnp.concatenate([lanes, lanes], axis=1)
        for c in range(3):
            high, low = split(values[c : c + 1, :])
            left = jnp.concatenate(
                [jnp.where(at_row, high, zero), jnp.where(at_row, low, zero)], axis=1
            )
            out[c] += lax.dot_general(
                left, lanes2, (((1,), (1,)), ((), ())), preferred_element_type=F32
            )
        out[3] += lax.dot_general(
            jnp.where(at_row, one, zero), lanes, (((1,), (1,)), ((), ())), preferred_element_type=F32
        )


def found_flow(voxel, flow, layers, field, store):
    patches, beads = voxel.shape
    rows = len(layers) * ROWS
    for c in range(3):
        for i, x in enumerate(layers):
            high, low = split(flow[c, x])
            field[c, i * ROWS : (i + 1) * ROWS, 0:256] = high
            field[c, i * ROWS : (i + 1) * ROWS, 256:512] = low
    place = lax.broadcasted_iota(I32, (rows, beads), 0)
    step = (layers[1] - layers[0] - 1) * ROWS
    place = place + layers[0] * ROWS + jnp.where(place >= ROWS, step, 0)
    one, zero = BF16(1), BF16(0)
    for g in range(patches):
        index = voxel[g : g + 1, :]
        lanes = jnp.where(one_hot(index & 255, 256), one, zero)
        lanes2 = jnp.concatenate([lanes, lanes], axis=0)
        at_row = place == (index >> 8)
        for c in range(3):
            found = lax.dot_general(
                field[c], lanes2, (((1,), (0,)), ((), ())), preferred_element_type=F32
            )
            store(g, c, jnp.sum(jnp.where(at_row, found, 0.0), axis=0, keepdims=True))


def field_kernel(total, flow, field):
    for x in range(field.shape[1]):
        rows = slice(x * ROWS, (x + 1) * ROWS)
        number = 10.0 * total[3, rows, :]
        for c in range(3):
            field[c, x] = 0.5 * total[c, rows, :] - number * flow[c, x]


def final_kernel(n, per, pos, base, *refs):
    flows, new_pos, new_vel = refs[:n], refs[n], refs[n + 1]
    me = lax.axis_index("xs")
    for d in range(n):
        source = me ^ d
        for r in range(per):
            at = pl.ds(source * per + r, 1)
            for c in range(3):
                speed = base[c, at, :] + 10.0 * flows[d][r * 3 + c : r * 3 + c + 1, :]
                new_vel[c, at, :] = speed
                new_pos[c, at, :] = pos[c, at, :] + 0.04 * speed


def shift(value, axis, by):
    n = lax.axis_size(axis)
    return lax.ppermute(value, axis, [(i, (i + by) % n) for i in range(n)])


def swap(value, axis, by):
    n = lax.axis_size(axis)
    return lax.ppermute(value, axis, [(i, i ^ by) for i in range(n)])


def pair_call(begin, end, pair_tiles, pos, vel, noise, given, after):
    tile = noise.shape[-1]
    count = pos.shape[2] // tile
    return call(
        functools.partial(pair_kernel, begin, end),
        [pair_tiles, pos, vel, noise] + given,
        jax.ShapeDtypeStruct(pos.shape, F32),
        "pair_forces",
        cost(1000, 1000),
        after=after,
        specs={0: SMEM_SPEC},
        out_specs=VMEM_SPEC,
        input_output_aliases={4: 0} if given else {},
        scratch_shapes=[
            pltpu.VMEM((end - begin, 6, count, 8, tile), F32),
            pltpu.VMEM((end - begin, 6, count, tile, tile), F32),
            pltpu.VMEM(((end - begin) * noise.shape[1], tile, tile), F32),
            pltpu.VMEM((end - begin, count, 3, 8, tile), F32),
        ],
    )


def per_device(
    populations, fluid_mask, patch_voxel, patch_owner, positions, velocities, pair_tiles, pair_noise
):
    n = lax.axis_size("xs")
    patches, beads = patch_voxel.shape
    per = patches // n
    nx = populations.shape[1]
    lanes = populations.shape[3]
    arr = lambda *shape: jax.ShapeDtypeStruct(shape, F32)
    ints = lambda *shape: jax.ShapeDtypeStruct(shape, I32)
    vmem, dma = pltpu.VMEM, pltpu.SemaphoreType.DMA
    positions = jnp.transpose(positions, (1, 0, 2))
    velocities = jnp.transpose(velocities, (1, 0, 2))
    pair_tiles = jnp.transpose(pair_tiles, (0, 2, 1))

    post, fwd, bwd, up, down, *others = call(
        functools.partial(collide_kernel, n, per, nx),
        [in_hbm(populations), in_hbm(fluid_mask), in_hbm(velocities)],
        [arr(19, nx, PAD, lanes), arr(384, lanes), arr(384, lanes)]
        + [arr(nx, 32, lanes)] * 2
        + [arr(16, lanes)] * (n - 3),
        "collide_first",
        cost(3_000_000_000, 11_000_000),
        specs={0: ANY_SPEC, 1: ANY_SPEC, 2: ANY_SPEC},
        out_specs=[VMEM_SPEC] * (n + 2),
        scratch_shapes=[
            vmem((nx, 19, ROWS, lanes), F32),
            vmem((nx, ROWS, lanes), I32),
            vmem(velocities.shape, F32),
            dma((2 * nx,)),
            dma((2,)),
        ],
    )
    before = shift(fwd, "ax", 1)
    after = shift(bwd, "ax", -1)
    below = shift(up, "xs", 1)
    above = shift(down, "xs", -1)
    sent = [below] + [shift(other, "xs", d + 2) for d, other in enumerate(others)] + [above]

    half = patches // 2
    bead_args = (pair_tiles, positions, velocities, pair_noise)
    base = pair_call(0, half, *bead_args, [], [down])

    post, edge_fwd, edge_bwd, flags = call(
        functools.partial(edges_kernel, n, nx),
        [post, fluid_mask, below, above],
        [arr(*post.shape), arr(16, lanes), arr(16, lanes), ints(nx, PAD, lanes)],
        "edges",
        cost(1000, 1000),
        after=[base] + sent[1:-1],
        out_specs=[VMEM_SPEC] * 4,
        input_output_aliases={0: 0},
    )
    edge_before = shift(edge_fwd, "ax", 1)
    edge_after = shift(edge_bwd, "ax", -1)

    post2, bits = call(
        functools.partial(middle_kernel, nx),
        [post, flags],
        [arr(19, nx, PAD, lanes), ints(nx, 72, lanes)],
        "middle_layers",
        cost(1000, 1000),
        out_specs=[VMEM_SPEC] * 2,
    )
    base = pair_call(half, patches, *bead_args, [base], [flags])

    def outer(first, face, edge, post2, bits, after):
        return call(
            functools.partial(outer_kernel, nx, first),
            [post, flags, face, edge, post2, bits],
            [arr(*post2.shape), ints(*bits.shape), arr(328, lanes)],
            "first_layer" if first else "last_layer",
            cost(1000, 1000),
            after=after,
            out_specs=[VMEM_SPEC] * 3,
            input_output_aliases={4: 0, 5: 1},
            scratch_shapes=[vmem((5, PAD, lanes), F32), vmem((PAD, lanes), I32)],
        )

    post2, bits, bwd2 = outer(True, before, edge_before, post2, bits, [base, after, edge_after])
    after2 = shift(bwd2, "ax", -1)
    post2, bits, fwd2 = outer(False, after, edge_after, post2, bits, [])
    before2 = shift(fwd2, "ax", 1)

    out, flow, part = call(
        functools.partial(final_middle_kernel, nx),
        [post2, bits, patch_voxel],
        [arr(*populations.shape), arr(3, nx, ROWS, lanes), arr(patches, 8, beads)],
        "final_middle",
        cost(1000, 1000),
        after=[fwd2],
        out_specs=[ANY_SPEC, VMEM_SPEC, VMEM_SPEC],
        scratch_shapes=[
            vmem((nx - 2, 19, ROWS, lanes), F32),
            vmem((3, (nx - 2) * ROWS, 2 * lanes), BF16),
            dma((nx - 2,)),
        ],
    )
    total = call(
        functools.partial(scatter_kernel, n, per),
        [patch_owner, patch_voxel, velocities] + sent,
        arr(4, nx * ROWS, lanes),
        "bead_sums",
        cost(1000, 1000),
        after=[fwd2],
        specs={0: SMEM_SPEC},
        out_specs=VMEM_SPEC,
        scratch_shapes=[vmem((n, per, 8, beads), F32)],
    )
    out, flow, *flows = call(
        functools.partial(final_outer_kernel, n, per, nx),
        [out, flow, post2, bits, after2, before2, patch_voxel, patch_owner, part],
        [arr(*populations.shape), arr(*flow.shape)] + [arr(8, beads)] * n,
        "final_outer",
        cost(1000, 1000),
        after=[total],
        specs={0: ANY_SPEC, 7: SMEM_SPEC},
        out_specs=[ANY_SPEC] + [VMEM_SPEC] * (n + 1),
        input_output_aliases={0: 0, 1: 1},
        scratch_shapes=[
            vmem((2, 5, PAD, lanes), F32),
            vmem((2, 19, ROWS, lanes), F32),
            vmem((patches, 8, beads), F32),
            vmem((3, 2 * ROWS, 2 * lanes), BF16),
            dma((2,)),
        ],
    )
    sent_flows = [flows[0]] + [swap(flows[d], "xs", d) for d in range(1, n)]
    field = call(
        field_kernel,
        [total, flow],
        arr(3, nx, ROWS, lanes),
        "drag_field",
        cost(1000, 1000),
        after=[flows[1]],
        out_specs=VMEM_SPEC,
    )
    new_pos, new_vel = call(
        functools.partial(final_kernel, n, per),
        [positions, base] + sent_flows,
        [arr(*positions.shape)] * 2,
        "bead_update",
        cost(1000, 1000),
        out_specs=[VMEM_SPEC] * 2,
    )
    return out, jnp.transpose(new_pos, (1, 0, 2)), jnp.transpose(new_vel, (1, 0, 2)), field


def solution(mesh):
    return jax.shard_map(
        per_device,
        mesh=mesh,
        in_specs=(
            P(None, "ax", "xs", None),
            P("ax", "xs", None),
            P(("ax", "xs"), None),
            P(("ax", "xs")),
            P(("ax", "xs"), None, None),
            P(("ax", "xs"), None, None),
            P(("ax", "xs"), None, None),
            P(("ax", "xs"), None, None, None),
        ),
        out_specs=(
            P(None, "ax", "xs", None),
            P(("ax", "xs"), None, None),
            P(("ax", "xs"), None, None),
            P(None, "ax", "xs", None),
        ),
        check_vma=False,
    )
```

```python
import functools

import jax
import jax.numpy as jnp
from jax import lax
from jax.experimental import pallas as pl
from jax.experimental.pallas import tpu as pltpu
from jax.sharding import PartitionSpec as P

DIRS = [
    (0, 0, 0),
    (1, 0, 0),
    (-1, 0, 0),
    (0, 1, 0),
    (0, -1, 0),
    (0, 0, 1),
    (0, 0, -1),
    (1, 1, 0),
    (-1, -1, 0),
    (1, -1, 0),
    (-1, 1, 0),
    (1, 0, 1),
    (-1, 0, -1),
    (1, 0, -1),
    (-1, 0, 1),
    (0, 1, 1),
    (0, -1, -1),
    (0, 1, -1),
    (0, -1, 1),
]
OPP = [0, 2, 1, 4, 3, 6, 5, 8, 7, 10, 9, 12, 11, 14, 13, 16, 15, 18, 17]
CX_PLUS = [k for k in range(19) if DIRS[k][0] == 1]
CX_MINUS = [k for k in range(19) if DIRS[k][0] == -1]
CY_PLUS = [k for k in range(19) if DIRS[k][1] == 1]
CY_MINUS = [k for k in range(19) if DIRS[k][1] == -1]
F32 = jnp.float32
BF16 = jnp.bfloat16
I32 = jnp.int32
VMEM_SPEC = pl.BlockSpec(memory_space=pltpu.VMEM)
SMEM_SPEC = pl.BlockSpec(memory_space=pltpu.SMEM)
ANY_SPEC = pl.BlockSpec(memory_space=pl.ANY)

ROWS = 64
PAD = 88
TILES = ROWS // 8


def params(mib=16):
    return pltpu.CompilerParams(vmem_limit_bytes=mib * 1024 * 1024)


def cost(flops, bytes_accessed):
    return pl.CostEstimate(flops=flops, bytes_accessed=bytes_accessed, transcendentals=0)


def call(kernel, ins, out_shape, name, estimate, after=(), specs=None, **kwargs):
    specs = specs or {}
    count, extra = len(ins), len(after)

    def body(*refs):
        kernel(*refs[:count], *refs[count + extra :])

    return pl.pallas_call(
        body,
        in_specs=[specs.get(i, VMEM_SPEC) for i in range(count)] + [ANY_SPEC] * extra,
        out_shape=out_shape,
        cost_estimate=estimate,
        name=name,
        **{"compiler_params": params(), **kwargs},
    )(*ins, *after)


def in_hbm(value):
    return pltpu.with_memory_space_constraint(value, pltpu.HBM)


def tree(values):
    while len(values) > 1:
        values = [
            values[i] + values[i + 1] if i + 1 < len(values) else values[i]
            for i in range(0, len(values), 2)
        ]
    return values[0]


def velocity_of(f):
    diff = [None] + [f[k] - f[k + 1] for k in range(1, 19, 2)]
    rho = tree([f[k] for k in range(1, 19)] + [f[0]])
    m1, m3, m5, m7, m9, m11, m13, m15, m17 = diff[1:]
    jx = m1 + ((m7 + m9) + (m11 + m13))
    jy = m3 + ((m7 - m9) + (m15 + m17))
    jz = m5 + ((m11 - m13) + (m15 - m17))
    inv = 1.0 / rho
    return rho, jx * inv, jy * inv, jz * inv


def collide(f):
    rho, ux, uy, uz = velocity_of(f)
    base = (1.25 * rho) * (1.0 - 1.5 * (ux * ux + uy * uy + uz * uz))
    ux, uy, uz = 1.5 * ux, 1.5 * uy, 1.5 * uz
    even1, even2 = base * (1.0 / 18.0), base * (1.0 / 36.0)
    odd1, odd2 = rho * (2.5 / 18.0), rho * (2.5 / 36.0)
    out = [None] * 19
    out[0] = base * (1.0 / 3.0) - 0.25 * f[0]
    for k in range(1, 19, 2):
        dx, dy, dz = DIRS[k]
        proj = None
        for sign, comp in ((dx, ux), (dy, uy), (dz, uz)):
            if sign == 0:
                continue
            if proj is None:
                proj = comp
            else:
                proj = proj + comp if sign > 0 else proj - comp
        even, odd = (even1, odd1) if k < 7 else (even2, odd2)
        odd = odd * proj
        even = even + odd * proj
        out[k] = (even + odd) - 0.25 * f[k]
        out[k + 1] = (even - odd) - 0.25 * f[k + 1]
    return out


def shifted(read, tile, dy, dz):
    here = read(tile)
    if dy != 0:
        sub = lax.broadcasted_iota(I32, here.shape, 0)
        if dy > 0:
            here = pltpu.roll(jnp.where(sub == 7, read(tile - 1), here), 1, 0)
        else:
            here = pltpu.roll(jnp.where(sub == 0, read(tile + 1), here), 7, 0)
    if dz != 0:
        here = pltpu.roll(here, 1 if dz > 0 else here.shape[1] - 1, 1)
    return here


def rows_of(tile):
    return pl.ds(pl.multiple_of(8 + 8 * tile, 8), 8)


def open_bits(read_mask, tile):
    bits = None
    cache = {}
    for k in range(1, 19):
        dx, dy, dz = DIRS[k]
        if (dx, dy) not in cache:
            cache[(dx, dy)] = shifted(functools.partial(read_mask, dx), tile, dy, 0)
        m = cache[(dx, dy)]
        if dz != 0:
            lane = lax.broadcasted_iota(I32, m.shape, 1)
            last = m.shape[1] - 1
            m = pltpu.roll(m, 1 if dz > 0 else last, 1)
            m = jnp.where(lane == (0 if dz > 0 else last), 0, m)
        m = m << k
        bits = m if bits is None else bits | m
    return bits


def stream(read, own, bits, tile):
    out = [own[0]]
    for k in range(1, 19):
        dx, dy, dz = DIRS[k]
        source = shifted(functools.partial(read, k, dx), tile, dy, dz)
        out.append(jnp.where((bits & (1 << k)) != 0, source, own[OPP[k]]))
    return out


def tile_rows(t):
    return pl.ds(pl.multiple_of(8 * t, 8), 8)


def three(value):
    high, rest = value.astype(BF16), value - value.astype(BF16).astype(F32)
    mid = rest.astype(BF16)
    return high.astype(F32), mid.astype(F32), (rest - mid.astype(F32)).astype(BF16).astype(F32)


def spread_beads(spots, speeds, rows, cols, left, right):
    patches, beads = spots.shape[1:]
    tile = cols.shape[-1]
    count = beads // tile
    place = lax.broadcasted_iota(I32, (48, 3 * tile), 0)
    comp = lax.broadcasted_iota(I32, (48, 3 * tile), 1) // tile
    part = ((place >> 3) == 0) | ((place >> 3) == 2) | ((place >> 3) == 5)
    spread = jnp.where(part & ((place & 7) == comp + 2), -1.0, 0.0).astype(BF16)
    stacks = []
    for g in range(patches):
        x = [spots[c, g : g + 1, :] for c in range(3)]
        w = [4.5 * speeds[c, g : g + 1, :] for c in range(3)]
        for c in range(3):
            for j in range(count):
                rows[g, c, j] = jnp.broadcast_to(x[c][:, j * tile : (j + 1) * tile], (8, tile))
        dot = x[0] * w[0] + (x[1] * w[1] + x[2] * w[2])
        one = jnp.ones_like(dot)
        high, mid, low = three(jnp.concatenate([dot, one] + w + x, axis=0))
        found = jnp.concatenate([high, mid, high, low, mid, high], axis=0).astype(BF16)
        for j in range(count):
            right[g, j] = found[:, j * tile : (j + 1) * tile]
        high, mid, low = three(jnp.concatenate([one, dot] + [-v for v in x + w], axis=0))
        stacks += [high, high, mid, high, mid, low]
    if -48 * patches % 128:
        stacks.append(jnp.zeros((-48 * patches % 128, beads), F32))
    turned = jnp.concatenate(stacks, axis=0).T.astype(BF16)
    for g in range(patches):
        for j in range(count):
            here = turned[j * tile : (j + 1) * tile, 48 * g : 48 * (g + 1)]
            left[g, j] = here
            wide = jnp.dot(here, spread, preferred_element_type=F32)
            for c in range(3):
                cols[g, c, j] = wide[:, c * tile : (c + 1) * tile]


def collide_kernel(n, per, nx, pop, mask, pos, vel, post, fwd, bwd, up, down, rows, cols, left, right, *rest):
    others, (here, flags, spots, speeds, sems, small) = rest[: n - 3], rest[n - 3 :]
    order = [(x, h) for x in [0, nx - 1] + list(range(1, nx - 1)) for h in range(1)]
    span = ROWS // 1
    copies = [
        pltpu.make_async_copy(
            pop.at[:, x, pl.ds(h * span, span)], here.at[x, :, pl.ds(h * span, span)], sems.at[i]
        )
        for i, (x, h) in enumerate(order)
    ]
    extra = [
        pltpu.make_async_copy(vel, speeds, small.at[0]),
        pltpu.make_async_copy(pos, spots, small.at[1]),
        pltpu.make_async_copy(mask, flags, small.at[2]),
    ]
    ahead = 3
    for copy in extra[:2] + copies[:ahead] + extra[2:]:
        copy.start()
    me = lax.axis_index("xs")
    extra[0].wait()
    for d in range(1, n):
        target = lax.rem(me + d, n)
        for r in range(per):
            for c in range(3):
                row = speeds[c, pl.ds(target * per + r, 1), :]
                for half in range(2):
                    i = (r * 3 + c) * 2 + half
                    piece = row[:, half * 256 : (half + 1) * 256]
                    if d in (1, n - 1):
                        ref = up if d == 1 else down
                        ref[i // 3, 26 + i % 3 : 27 + i % 3, :] = piece
                    else:
                        others[d - 2][i : i + 1, :] = piece
    extra[1].wait()
    spread_beads(spots, speeds, rows, cols, left, right)
    extra[2].wait()
    for i, (x, h) in enumerate(order):
        copies[i].wait()
        if i + ahead < len(copies):
            copies[i + ahead].start()

        def body(t, carry, x=x, h=h):
            t = t + h * (TILES // 1)
            out = collide([here[x, k, tile_rows(t), :] for k in range(19)])
            for k in range(19):
                post[k, x, rows_of(t), :] = out[k]
            return carry

        lax.fori_loop(0, TILES // 1, body, 0, unroll=TILES // 1)
        for ref, near, beyond, dirs in ((down, 0, 1, CY_MINUS), (up, ROWS - 1, ROWS - 2, CY_PLUS)):
            for k in range(19):
                ref[x, k : k + 1, :] = post[k, x, 8 + near : 9 + near, :]
            for j, k in enumerate(dirs):
                ref[x, 19 + j : 20 + j, :] = post[k, x, 8 + beyond : 9 + beyond, :]
            ref[x, 24:25, :] = flags[x, near : near + 1, :].astype(F32)
            ref[x, 25:26, :] = flags[x, beyond : beyond + 1, :].astype(F32)
    for x, ref, dirs in ((nx - 1, fwd, CX_PLUS), (0, bwd, CX_MINUS)):
        for j, k in enumerate(dirs):
            ref[j * ROWS : (j + 1) * ROWS, :] = post[k, x, 8:72, :]
        ref[5 * ROWS : 6 * ROWS, :] = flags[x].astype(F32)


def sent_velocity(refs, n, d, r, c):
    out = []
    for half in range(2):
        i = (r * 3 + c) * 2 + half
        if d in (1, n - 1):
            out.append(refs[d - 1][i // 3, 26 + i % 3 : 27 + i % 3, :])
        else:
            out.append(refs[d - 1][i : i + 1, :])
    return jnp.concatenate(out, axis=1)


def edges_kernel(n, nx, post_in, mask, below, above, post, fwd, bwd, flags):
    me = lax.axis_index("xs")
    has_below, has_above = (me > 0).astype(F32), (me < n - 1).astype(F32)
    for x in range(nx):
        for k in range(19):
            post[k, x, 79:80, :] = below[x, k : k + 1, :]
            post[k, x, 72:73, :] = above[x, k : k + 1, :]
        for j, k in enumerate(CY_PLUS):
            post[k, x, 7:8, :] = below[x, k : k + 1, :]
            post[k, x, 78:79, :] = below[x, 19 + j : 20 + j, :]
        for j, k in enumerate(CY_MINUS):
            post[k, x, 73:74, :] = above[x, 19 + j : 20 + j, :]
            post[k, x, 80:81, :] = post[k, x, 8:9, :]
        flags[x, 8:72, :] = mask[x]
        near = (below[x, 24:25, :] * has_below).astype(I32)
        flags[x, 79:80, :] = near
        flags[x, 7:8, :] = near
        flags[x, 78:79, :] = (below[x, 25:26, :] * has_below).astype(I32)
        flags[x, 72:73, :] = (above[x, 24:25, :] * has_above).astype(I32)
        flags[x, 73:74, :] = (above[x, 25:26, :] * has_above).astype(I32)
        flags[x, 80:81, :] = mask[x, 0:1, :]
    for rows, x, dirs, far_below, far_above in (
        (fwd, nx - 1, CX_PLUS, 7, 9),
        (bwd, 0, CX_MINUS, 10, 8),
    ):
        for j, k in enumerate(dirs):
            rows[j : j + 1, :] = below[x, k : k + 1, :]
            rows[8 + j : 9 + j, :] = above[x, k : k + 1, :]
        j = 19 + CY_PLUS.index(far_below)
        rows[5:6, :] = below[x, j : j + 1, :]
        j = 19 + CY_MINUS.index(far_above)
        rows[13:14, :] = above[x, j : j + 1, :]
        rows[6:8, :] = below[x, 24:26, :] * has_below
        rows[14:16, :] = above[x, 24:26, :] * has_above


def step_layer(x, read, read_mask, post, post2, bits_out):
    def body(t, carry):
        bits = open_bits(read_mask, t)
        own = [post[k, x, rows_of(t), :] for k in range(19)]
        out = collide(stream(read, own, bits, t))
        for k in range(19):
            post2[k, x, rows_of(t), :] = out[k]
        bits_out[x, tile_rows(t), :] = bits
        return carry

    lax.fori_loop(0, TILES + 1, body, 0, unroll=TILES + 1)
    for k in CY_PLUS:
        post2[k, x, 7:8, :] = post2[k, x, 79:80, :]


def middle_kernel(nx, post, flags, post2, bits_out):
    for x in range(1, nx - 1):
        step_layer(
            x,
            lambda k, dx, tile, x=x: post[k, x - dx, rows_of(tile), :],
            lambda dx, tile, x=x: flags[x - dx, rows_of(tile), :],
            post,
            post2,
            bits_out,
        )


def outer_kernel(
    nx, first, post, flags, face, edge, post2_in, bits_in, post2, bits_out, send, halo, halo_flags
):
    x, near = (0, -1) if first else (nx - 1, nx)
    dirs, k_below, k_above = (CX_PLUS, 7, 9) if first else (CX_MINUS, 10, 8)
    for j, k in enumerate(dirs):
        halo[j, 8:72, :] = face[j * ROWS : (j + 1) * ROWS, :]
        halo[j, 79:80, :] = edge[j : j + 1, :]
        halo[j, 72:73, :] = edge[8 + j : 9 + j, :]
        if k == k_below:
            halo[j, 7:8, :] = edge[j : j + 1, :]
            halo[j, 78:79, :] = edge[5:6, :]
        if k == k_above:
            halo[j, 73:74, :] = edge[13:14, :]
            halo[j, 80:81, :] = face[j * ROWS : j * ROWS + 1, :]
    halo_flags[8:72, :] = face[5 * ROWS : 6 * ROWS, :].astype(I32)
    halo_flags[79:80, :] = edge[6:7, :].astype(I32)
    halo_flags[7:8, :] = edge[6:7, :].astype(I32)
    halo_flags[78:79, :] = edge[7:8, :].astype(I32)
    halo_flags[72:73, :] = edge[14:15, :].astype(I32)
    halo_flags[73:74, :] = edge[15:16, :].astype(I32)
    halo_flags[80:81, :] = face[5 * ROWS : 5 * ROWS + 1, :].astype(I32)

    def read(k, dx, tile):
        if x - dx == near:
            return halo[dirs.index(k), rows_of(tile), :]
        return post[k, x - dx, rows_of(tile), :]

    def read_mask(dx, tile):
        if x - dx == near:
            return halo_flags[rows_of(tile), :]
        return flags[x - dx, rows_of(tile), :]

    step_layer(x, read, read_mask, post, post2, bits_out)
    dirs, k_below, k_above = (CX_MINUS, 10, 8) if first else (CX_PLUS, 7, 9)
    for j, k in enumerate(dirs):
        send[j * ROWS : (j + 1) * ROWS, :] = post2[k, x, 8:72, :]
    send[320:321, :] = post2[k_below, x, 79:80, :]
    send[321:322, :] = post2[k_above, x, 72:73, :]


def final_layer(x, read, post2, bits, result, flow, out, sem):
    def body(t, carry):
        rows = tile_rows(t)
        own = [post2[k, x, rows_of(t), :] for k in range(19)]
        f = stream(read, own, bits[x, rows, :], t)
        for k in range(19):
            result[k, rows, :] = f[k]
        rho, ux, uy, uz = velocity_of(f)
        flow[0, x, rows, :] = ux
        flow[1, x, rows, :] = uy
        flow[2, x, rows, :] = uz
        return carry

    lax.fori_loop(0, TILES, body, 0, unroll=TILES)
    copy = pltpu.make_async_copy(result, out.at[:, x], sem)
    copy.start()
    return copy


def final_middle_kernel(nx, post2, bits, voxel, out, flow, table, result, field, sems):
    copies = []
    for i, x in enumerate(range(1, nx - 1)):
        read = lambda k, dx, tile, x=x: post2[k, x - dx, rows_of(tile), :]
        copies.append(final_layer(x, read, post2, bits, result.at[i], flow, out, sems.at[i]))

    def store(g, c, row):
        table[g, c : c + 1, :] = row

    found_flow(voxel, flow, list(range(1, nx - 1)), field, store)
    for copy in copies:
        copy.wait()


def final_outer_kernel(
    n, per, nx, out_in, flow_in, post2, bits, after, before, voxel, owner, part, out, flow, *refs
):
    outs, (halo, result, table, field, sems) = refs[:n], refs[n:]
    copies = []
    for i, (face, first) in enumerate(((after, False), (before, True))):
        x, near = (0, -1) if first else (nx - 1, nx)
        dirs, k_below, k_above = (CX_PLUS, 7, 9) if first else (CX_MINUS, 10, 8)
        for j in range(5):
            halo[i, j, 8:72, :] = face[j * ROWS : (j + 1) * ROWS, :]
        halo[i, dirs.index(k_below), 7:8, :] = face[320:321, :]
        halo[i, dirs.index(k_above), 72:73, :] = face[321:322, :]

        def read(k, dx, tile, i=i, x=x, near=near, dirs=dirs):
            if x - dx == near:
                return halo[i, dirs.index(k), rows_of(tile), :]
            return post2[k, x - dx, rows_of(tile), :]

        copies.append(final_layer(x, read, post2, bits, result.at[i], flow, out, sems.at[i]))

    def store(g, c, row):
        table[g, c : c + 1, :] = part[g, c : c + 1, :] + row

    found_flow(voxel, flow, [0, nx - 1], field, store)
    patches = voxel.shape[0]
    me = lax.axis_index("xs")
    rank = ranks(owner, patches)
    for d in range(n):
        target = me ^ d
        for r in range(per):
            found = jnp.int32(0)
            for g in range(patches):
                found = jnp.where((owner[g] == target) & (rank[g] == r), g, found)
            outs[d][r * 3 : r * 3 + 3, :] = table[found, 0:3, :]
    for copy in copies:
        copy.wait()


def pair_kernel(begin, end, pair_tiles, vel, rows, cols, left, right, noise, *refs):
    base, theta, along, acc = refs[-4:]
    tile = noise.shape[-1]
    count = cols.shape[2]
    pairs = noise.shape[1]
    patches = end - begin
    eye = lax.broadcasted_iota(I32, (tile, tile), 0) == lax.broadcasted_iota(I32, (tile, tile), 1)
    scale = jnp.where(eye, 15.0, 0.0).astype(BF16)
    acc[...] = jnp.zeros_like(acc)
    for g in range(patches):
        for p in range(pairs):
            theta[g * pairs + p] = lax.dot_general(
                scale, noise[begin + g, p], (((1,), (1,)), ((), ())), preferred_element_type=F32
            )
            first, second = pair_tiles[begin + g, 0, p], pair_tiles[begin + g, 1, p]
            along[g * pairs + p] = jnp.dot(
                left[begin + g, second], right[begin + g, first], preferred_element_type=F32
            )

    def one_pair(i, carry):
        g, p = i // pairs, i % pairs
        first = pair_tiles[begin + g, 0, p]
        second = pair_tiles[begin + g, 1, p]
        mine = [rows[begin + g, c, first] for c in range(3)]
        total = []
        for s in range(tile // 8):
            part = slice(8 * s, 8 * s + 8)
            dx, dy, dz = [mine[c] - cols[begin + g, c, second, part, :] for c in range(3)]
            square = (dx * dx + 0.01) + (dy * dy + dz * dz)
            close = jnp.maximum(lax.rsqrt(square) - 1.0, 0.0)
            force = close * ((theta[i, part, :] + 25.0) - close * along[i, part, :])
            here = [force * dx, force * dy, force * dz]
            total = here if not total else [a + b for a, b in zip(total, here)]
        for c in range(3):
            acc[g, first, c] += total[c]
        return carry

    lax.fori_loop(0, patches * pairs, one_pair, 0, unroll=4)
    for g in range(patches):
        for c in range(3):
            force = jnp.concatenate(
                [jnp.sum(acc[g, j, c], axis=0, keepdims=True) for j in range(count)], axis=1
            )
            speed = vel[c, begin + g : begin + g + 1, :]
            base[c, begin + g : begin + g + 1, :] = 0.5 * speed + 0.04 * force


def split(value):
    high = value.astype(BF16)
    return high, (value - high.astype(F32)).astype(BF16)


def ranks(owner, count):
    out = []
    for g in range(count):
        rank = jnp.int32(0)
        for h in range(g):
            rank = rank + (owner[h] == owner[g]).astype(I32)
        out.append(rank)
    return out


def one_hot(index, extent):
    want = index.astype(F32).astype(BF16)
    place = lax.broadcasted_iota(I32, (extent, index.shape[1]), 0).astype(F32).astype(BF16)
    return place == want


def scatter_kernel(n, per, owner, voxel, vel, *refs):
    sent, out, table = refs[: n - 1], refs[n - 1], refs[n]
    me = lax.axis_index("xs")
    beads = voxel.shape[1]
    for r in range(per):
        for c in range(3):
            table[me, r, c : c + 1, :] = vel[c, pl.ds(me * per + r, 1), :]
        for d in range(1, n):
            source = lax.rem(me + n - d, n)
            for c in range(3):
                table[source, r, c : c + 1, :] = sent_velocity(sent, n, d, r, c)
    out[...] = jnp.zeros_like(out)
    rank = ranks(owner, voxel.shape[0])
    one, zero = BF16(1), BF16(0)
    for g in range(voxel.shape[0]):
        index = voxel[g : g + 1, :]
        lanes = jnp.where(one_hot(index & 255, 256), one, zero)
        at_row = one_hot(index >> 8, out.shape[1])
        values = table[owner[g], rank[g]]
        lanes2 = jnp.concatenate([lanes, lanes], axis=1)
        for c in range(3):
            high, low = split(values[c : c + 1, :])
            left = jnp.concatenate(
                [jnp.where(at_row, high, zero), jnp.where(at_row, low, zero)], axis=1
            )
            out[c] += lax.dot_general(
                left, lanes2, (((1,), (1,)), ((), ())), preferred_element_type=F32
            )
        out[3] += lax.dot_general(
            jnp.where(at_row, one, zero), lanes, (((1,), (1,)), ((), ())), preferred_element_type=F32
        )


def found_flow(voxel, flow, layers, field, store):
    patches, beads = voxel.shape
    rows = len(layers) * ROWS
    for c in range(3):
        for i, x in enumerate(layers):
            high, low = split(flow[c, x])
            field[c, i * ROWS : (i + 1) * ROWS, 0:256] = high
            field[c, i * ROWS : (i + 1) * ROWS, 256:512] = low
    place = lax.broadcasted_iota(I32, (rows, beads), 0)
    step = (layers[1] - layers[0] - 1) * ROWS
    place = place + layers[0] * ROWS + jnp.where(place >= ROWS, step, 0)
    one, zero = BF16(1), BF16(0)
    for g in range(patches):
        index = voxel[g : g + 1, :]
        lanes = jnp.where(one_hot(index & 255, 256), one, zero)
        lanes2 = jnp.concatenate([lanes, lanes], axis=0)
        at_row = place == (index >> 8)
        for c in range(3):
            found = lax.dot_general(
                field[c], lanes2, (((1,), (0,)), ((), ())), preferred_element_type=F32
            )
            store(g, c, jnp.sum(jnp.where(at_row, found, 0.0), axis=0, keepdims=True))


def field_kernel(total, flow, field):
    for x in range(field.shape[1]):
        rows = slice(x * ROWS, (x + 1) * ROWS)
        number = 10.0 * total[3, rows, :]
        for c in range(3):
            field[c, x] = 0.5 * total[c, rows, :] - number * flow[c, x]


def final_kernel(n, per, pos, base, *refs):
    flows, new_pos, new_vel = refs[:n][::-1], refs[n], refs[n + 1]
    me = lax.axis_index("xs")
    for d in range(n):
        source = me ^ d
        for r in range(per):
            at = pl.ds(source * per + r, 1)
            for c in range(3):
                speed = base[c, at, :] + 10.0 * flows[d][r * 3 + c : r * 3 + c + 1, :]
                new_vel[c, at, :] = speed
                new_pos[c, at, :] = pos[c, at, :] + 0.04 * speed


def shift(value, axis, by):
    n = lax.axis_size(axis)
    return lax.ppermute(value, axis, [(i, (i + by) % n) for i in range(n)])


def swap(value, axis, by):
    n = lax.axis_size(axis)
    return lax.ppermute(value, axis, [(i, i ^ by) for i in range(n)])


def pair_call(begin, end, pair_tiles, vel, rows, cols, left, right, noise, given, after):
    tile = noise.shape[-1]
    return call(
        functools.partial(pair_kernel, begin, end),
        [pair_tiles, vel, rows, cols, left, right, noise] + given,
        jax.ShapeDtypeStruct(vel.shape, F32),
        "pair_forces",
        cost(1000, 1000),
        after=after,
        specs={0: SMEM_SPEC},
        out_specs=VMEM_SPEC,
        input_output_aliases={7: 0} if given else {},
        scratch_shapes=[
            pltpu.VMEM(((end - begin) * noise.shape[1], tile, tile), F32),
            pltpu.VMEM(((end - begin) * noise.shape[1], tile, tile), F32),
            pltpu.VMEM((end - begin, cols.shape[2], 3, 8, tile), F32),
        ],
    )


def per_device(
    populations, fluid_mask, patch_voxel, patch_owner, positions, velocities, pair_tiles, pair_noise
):
    n = lax.axis_size("xs")
    patches, beads = patch_voxel.shape
    per = patches // n
    nx = populations.shape[1]
    lanes = populations.shape[3]
    tiles = beads // 128
    arr = lambda *shape: jax.ShapeDtypeStruct(shape, F32)
    ints = lambda *shape: jax.ShapeDtypeStruct(shape, I32)
    vmem, dma = pltpu.VMEM, pltpu.SemaphoreType.DMA
    positions = jnp.transpose(positions, (1, 0, 2))
    velocities = jnp.transpose(velocities, (1, 0, 2))
    pair_tiles = jnp.transpose(pair_tiles, (0, 2, 1))

    post, fwd, bwd, up, down, *layouts = call(
        functools.partial(collide_kernel, n, per, nx),
        [in_hbm(value) for value in (populations, fluid_mask, positions, velocities)],
        [arr(19, nx, PAD, lanes), arr(384, lanes), arr(384, lanes)]
        + [arr(nx, 32, lanes)] * 2
        + [
            arr(patches, 3, tiles, 8, 128),
            arr(patches, 3, tiles, 128, 128),
            jax.ShapeDtypeStruct((patches, tiles, 128, 48), BF16),
            jax.ShapeDtypeStruct((patches, tiles, 48, 128), BF16),
        ]
        + [arr(16, lanes)] * (n - 3),
        "collide_first",
        cost(3_000_000_000, 11_000_000),
        specs={i: ANY_SPEC for i in range(4)},
        out_specs=[VMEM_SPEC] * (n + 6),
        scratch_shapes=[
            vmem((nx, 19, ROWS, lanes), F32),
            vmem((nx, ROWS, lanes), I32),
            vmem(positions.shape, F32),
            vmem(velocities.shape, F32),
            dma((2 * nx,)),
            dma((3,)),
        ],
    )
    before = shift(fwd, "ax", 1)
    after = shift(bwd, "ax", -1)
    layouts, others = layouts[:4], layouts[4:]
    below = shift(up, "xs", 1)
    above = shift(down, "xs", -1)
    sent = [below] + [shift(other, "xs", d + 2) for d, other in enumerate(others)] + [above]

    cuts = (patches * 5 // 8, patches * 7 // 8)
    bead_args = (pair_tiles, velocities, *layouts, pair_noise)
    base = pair_call(0, cuts[0], *bead_args, [], [down])

    post, edge_fwd, edge_bwd, flags = call(
        functools.partial(edges_kernel, n, nx),
        [post, fluid_mask, below, above],
        [arr(*post.shape), arr(16, lanes), arr(16, lanes), ints(nx, PAD, lanes)],
        "edges",
        cost(1000, 1000),
        after=[base],
        out_specs=[VMEM_SPEC] * 4,
        input_output_aliases={0: 0},
    )
    edge_before = shift(edge_fwd, "ax", 1)
    edge_after = shift(edge_bwd, "ax", -1)

    post2, bits = call(
        functools.partial(middle_kernel, nx),
        [post, flags],
        [arr(19, nx, PAD, lanes), ints(nx, 72, lanes)],
        "middle_layers",
        cost(1000, 1000),
        out_specs=[VMEM_SPEC] * 2,
    )
    def outer(first, face, edge, post2, bits, after):
        return call(
            functools.partial(outer_kernel, nx, first),
            [post, flags, face, edge, post2, bits],
            [arr(*post2.shape), ints(*bits.shape), arr(328, lanes)],
            "first_layer" if first else "last_layer",
            cost(1000, 1000),
            after=after,
            out_specs=[VMEM_SPEC] * 3,
            input_output_aliases={4: 0, 5: 1},
            scratch_shapes=[vmem((5, PAD, lanes), F32), vmem((PAD, lanes), I32)],
        )

    base = pair_call(cuts[0], cuts[1], *bead_args, [base], [flags])
    post2, bits, bwd2 = outer(True, before, edge_before, post2, bits, [base, after, edge_after] + sent[1:-1])
    after2 = shift(bwd2, "ax", -1)
    post2, bits, fwd2 = outer(False, after, edge_after, post2, bits, [])
    before2 = shift(fwd2, "ax", 1)

    base = pair_call(cuts[1], patches, *bead_args, [base], [fwd2])
    out, flow, part = call(
        functools.partial(final_middle_kernel, nx),
        [post2, bits, patch_voxel],
        [arr(*populations.shape), arr(3, nx, ROWS, lanes), arr(patches, 8, beads)],
        "final_middle",
        cost(1000, 1000),
        after=[fwd2],
        out_specs=[ANY_SPEC, VMEM_SPEC, VMEM_SPEC],
        scratch_shapes=[
            vmem((nx - 2, 19, ROWS, lanes), F32),
            vmem((3, (nx - 2) * ROWS, 2 * lanes), BF16),
            dma((nx - 2,)),
        ],
    )
    total = call(
        functools.partial(scatter_kernel, n, per),
        [patch_owner, patch_voxel, velocities] + sent,
        arr(4, nx * ROWS, lanes),
        "bead_sums",
        cost(1000, 1000),
        after=[fwd2],
        specs={0: SMEM_SPEC},
        out_specs=VMEM_SPEC,
        scratch_shapes=[vmem((n, per, 8, beads), F32)],
    )
    out, flow, *flows = call(
        functools.partial(final_outer_kernel, n, per, nx),
        [out, flow, post2, bits, after2, before2, patch_voxel, patch_owner, part],
        [arr(*populations.shape), arr(*flow.shape)] + [arr(8, beads)] * n,
        "final_outer",
        cost(1000, 1000),
        after=[total, base],
        specs={0: ANY_SPEC, 7: SMEM_SPEC},
        out_specs=[ANY_SPEC] + [VMEM_SPEC] * (n + 1),
        input_output_aliases={0: 0, 1: 1},
        scratch_shapes=[
            vmem((2, 5, PAD, lanes), F32),
            vmem((2, 19, ROWS, lanes), F32),
            vmem((patches, 8, beads), F32),
            vmem((3, 2 * ROWS, 2 * lanes), BF16),
            dma((2,)),
        ],
    )
    sent_flows = [flows[0]] + [swap(flows[d], "xs", d) for d in range(1, n)]
    field = call(
        field_kernel,
        [total, flow],
        arr(3, nx, ROWS, lanes),
        "drag_field",
        cost(1000, 1000),
        after=[flows[1]],
        out_specs=VMEM_SPEC,
    )
    new_pos, new_vel = call(
        functools.partial(final_kernel, n, per),
        [positions, base] + sent_flows[::-1],
        [arr(*positions.shape)] * 2,
        "bead_update",
        cost(1000, 1000),
        out_specs=[VMEM_SPEC] * 2,
    )
    return out, jnp.transpose(new_pos, (1, 0, 2)), jnp.transpose(new_vel, (1, 0, 2)), field


def solution(mesh):
    return jax.shard_map(
        per_device,
        mesh=mesh,
        in_specs=(
            P(None, "ax", "xs", None),
            P("ax", "xs", None),
            P(("ax", "xs"), None),
            P(("ax", "xs")),
            P(("ax", "xs"), None, None),
            P(("ax", "xs"), None, None),
            P(("ax", "xs"), None, None),
            P(("ax", "xs"), None, None, None),
        ),
        out_specs=(
            P(None, "ax", "xs", None),
            P(("ax", "xs"), None, None),
            P(("ax", "xs"), None, None),
            P(None, "ax", "xs", None),
        ),
        check_vma=False,
    )
```

```python
import functools

import jax
import jax.numpy as jnp
from jax import lax
from jax.experimental import pallas as pl
from jax.experimental.pallas import tpu as pltpu
from jax.sharding import PartitionSpec as P

DIRS = [
    (0, 0, 0),
    (1, 0, 0),
    (-1, 0, 0),
    (0, 1, 0),
    (0, -1, 0),
    (0, 0, 1),
    (0, 0, -1),
    (1, 1, 0),
    (-1, -1, 0),
    (1, -1, 0),
    (-1, 1, 0),
    (1, 0, 1),
    (-1, 0, -1),
    (1, 0, -1),
    (-1, 0, 1),
    (0, 1, 1),
    (0, -1, -1),
    (0, 1, -1),
    (0, -1, 1),
]
OPP = [0, 2, 1, 4, 3, 6, 5, 8, 7, 10, 9, 12, 11, 14, 13, 16, 15, 18, 17]
CX_PLUS = [k for k in range(19) if DIRS[k][0] == 1]
CX_MINUS = [k for k in range(19) if DIRS[k][0] == -1]
CY_PLUS = [k for k in range(19) if DIRS[k][1] == 1]
CY_MINUS = [k for k in range(19) if DIRS[k][1] == -1]
F32 = jnp.float32
BF16 = jnp.bfloat16
I32 = jnp.int32
VMEM_SPEC = pl.BlockSpec(memory_space=pltpu.VMEM)
SMEM_SPEC = pl.BlockSpec(memory_space=pltpu.SMEM)
ANY_SPEC = pl.BlockSpec(memory_space=pl.ANY)

ROWS = 64
PAD = 88
TILES = ROWS // 8


def params(mib=16):
    return pltpu.CompilerParams(vmem_limit_bytes=mib * 1024 * 1024)


def cost(flops, bytes_accessed):
    return pl.CostEstimate(flops=flops, bytes_accessed=bytes_accessed, transcendentals=0)


def call(kernel, ins, out_shape, name, estimate, after=(), specs=None, **kwargs):
    specs = specs or {}
    count, extra = len(ins), len(after)

    def body(*refs):
        kernel(*refs[:count], *refs[count + extra :])

    return pl.pallas_call(
        body,
        in_specs=[specs.get(i, VMEM_SPEC) for i in range(count)] + [ANY_SPEC] * extra,
        out_shape=out_shape,
        cost_estimate=estimate,
        name=name,
        **{"compiler_params": params(), **kwargs},
    )(*ins, *after)


def in_hbm(value):
    return pltpu.with_memory_space_constraint(value, pltpu.HBM)


def tree(values):
    while len(values) > 1:
        values = [
            values[i] + values[i + 1] if i + 1 < len(values) else values[i]
            for i in range(0, len(values), 2)
        ]
    return values[0]


def velocity_of(f):
    diff = [None] + [f[k] - f[k + 1] for k in range(1, 19, 2)]
    rho = tree([f[k] for k in range(1, 19)] + [f[0]])
    m1, m3, m5, m7, m9, m11, m13, m15, m17 = diff[1:]
    jx = m1 + ((m7 + m9) + (m11 + m13))
    jy = m3 + ((m7 - m9) + (m15 + m17))
    jz = m5 + ((m11 - m13) + (m15 - m17))
    inv = 1.0 / rho
    return rho, jx * inv, jy * inv, jz * inv


def collide(f):
    rho, ux, uy, uz = velocity_of(f)
    base = (1.25 * rho) * (1.0 - 1.5 * (ux * ux + uy * uy + uz * uz))
    ux, uy, uz = 1.5 * ux, 1.5 * uy, 1.5 * uz
    even1, even2 = base * (1.0 / 18.0), base * (1.0 / 36.0)
    odd1, odd2 = rho * (2.5 / 18.0), rho * (2.5 / 36.0)
    out = [None] * 19
    out[0] = base * (1.0 / 3.0) - 0.25 * f[0]
    for k in range(1, 19, 2):
        dx, dy, dz = DIRS[k]
        proj = None
        for sign, comp in ((dx, ux), (dy, uy), (dz, uz)):
            if sign == 0:
                continue
            if proj is None:
                proj = comp
            else:
                proj = proj + comp if sign > 0 else proj - comp
        even, odd = (even1, odd1) if k < 7 else (even2, odd2)
        odd = odd * proj
        even = even + odd * proj
        out[k] = (even + odd) - 0.25 * f[k]
        out[k + 1] = (even - odd) - 0.25 * f[k + 1]
    return out


def shifted(read, tile, dy, dz):
    here = read(tile)
    if dy != 0:
        sub = lax.broadcasted_iota(I32, here.shape, 0)
        if dy > 0:
            here = pltpu.roll(jnp.where(sub == 7, read(tile - 1), here), 1, 0)
        else:
            here = pltpu.roll(jnp.where(sub == 0, read(tile + 1), here), 7, 0)
    if dz != 0:
        here = pltpu.roll(here, 1 if dz > 0 else here.shape[1] - 1, 1)
    return here


def rows_of(tile):
    return pl.ds(pl.multiple_of(8 + 8 * tile, 8), 8)


def open_bits(read_mask, tile):
    bits = None
    cache = {}
    for k in range(1, 19):
        dx, dy, dz = DIRS[k]
        if (dx, dy) not in cache:
            cache[(dx, dy)] = shifted(functools.partial(read_mask, dx), tile, dy, 0)
        m = cache[(dx, dy)]
        if dz != 0:
            lane = lax.broadcasted_iota(I32, m.shape, 1)
            last = m.shape[1] - 1
            m = pltpu.roll(m, 1 if dz > 0 else last, 1)
            m = jnp.where(lane == (0 if dz > 0 else last), 0, m)
        m = m << k
        bits = m if bits is None else bits | m
    return bits


def stream(read, own, bits, tile):
    out = [own[0]]
    for k in range(1, 19):
        dx, dy, dz = DIRS[k]
        source = shifted(functools.partial(read, k, dx), tile, dy, dz)
        out.append(jnp.where((bits & (1 << k)) != 0, source, own[OPP[k]]))
    return out


def tile_rows(t):
    return pl.ds(pl.multiple_of(8 * t, 8), 8)


def three(value):
    high, rest = value.astype(BF16), value - value.astype(BF16).astype(F32)
    mid = rest.astype(BF16)
    return high.astype(F32), mid.astype(F32), (rest - mid.astype(F32)).astype(BF16).astype(F32)


def spread_beads(spots, speeds, rows, cols, left, right):
    patches, beads = spots.shape[1:]
    tile = cols.shape[-1]
    count = beads // tile
    place = lax.broadcasted_iota(I32, (48, 3 * tile), 0)
    comp = lax.broadcasted_iota(I32, (48, 3 * tile), 1) // tile
    part = ((place >> 3) == 0) | ((place >> 3) == 2) | ((place >> 3) == 5)
    spread = jnp.where(part & ((place & 7) == comp + 2), -1.0, 0.0).astype(BF16)
    stacks = []
    for g in range(patches):
        x = [spots[c, g : g + 1, :] for c in range(3)]
        w = [4.5 * speeds[c, g : g + 1, :] for c in range(3)]
        for c in range(3):
            for j in range(count):
                rows[g, c, j] = jnp.broadcast_to(x[c][:, j * tile : (j + 1) * tile], (8, tile))
        dot = x[0] * w[0] + (x[1] * w[1] + x[2] * w[2])
        one = jnp.ones_like(dot)
        high, mid, low = three(jnp.concatenate([dot, one] + w + x, axis=0))
        found = jnp.concatenate([high, mid, high, low, mid, high], axis=0).astype(BF16)
        for j in range(count):
            right[g, j] = found[:, j * tile : (j + 1) * tile]
        high, mid, low = three(jnp.concatenate([one, dot] + [-v for v in x + w], axis=0))
        stacks += [high, high, mid, high, mid, low]
    if -48 * patches % 128:
        stacks.append(jnp.zeros((-48 * patches % 128, beads), F32))
    turned = jnp.concatenate(stacks, axis=0).T.astype(BF16)
    for g in range(patches):
        for j in range(count):
            here = turned[j * tile : (j + 1) * tile, 48 * g : 48 * (g + 1)]
            left[g, j] = here
            wide = jnp.dot(here, spread, preferred_element_type=F32)
            for c in range(3):
                cols[g, c, j] = wide[:, c * tile : (c + 1) * tile]


def collide_kernel(n, per, nx, pop, mask, pos, vel, post, fwd, bwd, up, down, rows, cols, left, right, *rest):
    others, (here, flags, spots, speeds, sems, small) = rest[: n - 3], rest[n - 3 :]
    order = [(x, h) for x in [0, nx - 1] + list(range(1, nx - 1)) for h in range(1)]
    span = ROWS // 1
    copies = [
        pltpu.make_async_copy(
            pop.at[:, x, pl.ds(h * span, span)], here.at[x, :, pl.ds(h * span, span)], sems.at[i]
        )
        for i, (x, h) in enumerate(order)
    ]
    extra = [
        pltpu.make_async_copy(vel, speeds, small.at[0]),
        pltpu.make_async_copy(pos, spots, small.at[1]),
        pltpu.make_async_copy(mask, flags, small.at[2]),
    ]
    ahead = 3
    for copy in extra[:2] + copies[:ahead] + extra[2:]:
        copy.start()
    me = lax.axis_index("xs")
    extra[0].wait()
    for d in range(1, n):
        target = lax.rem(me + d, n)
        for r in range(per):
            for c in range(3):
                row = speeds[c, pl.ds(target * per + r, 1), :]
                for half in range(2):
                    i = (r * 3 + c) * 2 + half
                    piece = row[:, half * 256 : (half + 1) * 256]
                    if d in (1, n - 1):
                        ref = up if d == 1 else down
                        ref[i // 3, 26 + i % 3 : 27 + i % 3, :] = piece
                    else:
                        others[d - 2][i : i + 1, :] = piece
    extra[1].wait()
    spread_beads(spots, speeds, rows, cols, left, right)
    extra[2].wait()
    for i, (x, h) in enumerate(order):
        copies[i].wait()
        if i + ahead < len(copies):
            copies[i + ahead].start()

        def body(t, carry, x=x, h=h):
            t = t + h * (TILES // 1)
            out = collide([here[x, k, tile_rows(t), :] for k in range(19)])
            for k in range(19):
                post[k, x, rows_of(t), :] = out[k]
            return carry

        lax.fori_loop(0, TILES // 1, body, 0, unroll=TILES // 1)
        for ref, near, beyond, dirs in ((down, 0, 1, CY_MINUS), (up, ROWS - 1, ROWS - 2, CY_PLUS)):
            for k in range(19):
                ref[x, k : k + 1, :] = post[k, x, 8 + near : 9 + near, :]
            for j, k in enumerate(dirs):
                ref[x, 19 + j : 20 + j, :] = post[k, x, 8 + beyond : 9 + beyond, :]
            ref[x, 24:25, :] = flags[x, near : near + 1, :].astype(F32)
            ref[x, 25:26, :] = flags[x, beyond : beyond + 1, :].astype(F32)
    for x, ref, dirs in ((nx - 1, fwd, CX_PLUS), (0, bwd, CX_MINUS)):
        for j, k in enumerate(dirs):
            ref[j * ROWS : (j + 1) * ROWS, :] = post[k, x, 8:72, :]
        ref[5 * ROWS : 6 * ROWS, :] = flags[x].astype(F32)


def sent_velocity(refs, n, d, r, c):
    out = []
    for half in range(2):
        i = (r * 3 + c) * 2 + half
        if d in (1, n - 1):
            out.append(refs[d - 1][i // 3, 26 + i % 3 : 27 + i % 3, :])
        else:
            out.append(refs[d - 1][i : i + 1, :])
    return jnp.concatenate(out, axis=1)


def edges_kernel(n, nx, post_in, mask, below, above, post, fwd, bwd, flags):
    me = lax.axis_index("xs")
    has_below, has_above = (me > 0).astype(F32), (me < n - 1).astype(F32)
    for x in range(nx):
        for k in range(19):
            post[k, x, 79:80, :] = below[x, k : k + 1, :]
            post[k, x, 72:73, :] = above[x, k : k + 1, :]
        for j, k in enumerate(CY_PLUS):
            post[k, x, 7:8, :] = below[x, k : k + 1, :]
            post[k, x, 78:79, :] = below[x, 19 + j : 20 + j, :]
        for j, k in enumerate(CY_MINUS):
            post[k, x, 73:74, :] = above[x, 19 + j : 20 + j, :]
            post[k, x, 80:81, :] = post[k, x, 8:9, :]
        flags[x, 8:72, :] = mask[x]
        near = (below[x, 24:25, :] * has_below).astype(I32)
        flags[x, 79:80, :] = near
        flags[x, 7:8, :] = near
        flags[x, 78:79, :] = (below[x, 25:26, :] * has_below).astype(I32)
        flags[x, 72:73, :] = (above[x, 24:25, :] * has_above).astype(I32)
        flags[x, 73:74, :] = (above[x, 25:26, :] * has_above).astype(I32)
        flags[x, 80:81, :] = mask[x, 0:1, :]
    for rows, x, dirs, far_below, far_above in (
        (fwd, nx - 1, CX_PLUS, 7, 9),
        (bwd, 0, CX_MINUS, 10, 8),
    ):
        for j, k in enumerate(dirs):
            rows[j : j + 1, :] = below[x, k : k + 1, :]
            rows[8 + j : 9 + j, :] = above[x, k : k + 1, :]
        j = 19 + CY_PLUS.index(far_below)
        rows[5:6, :] = below[x, j : j + 1, :]
        j = 19 + CY_MINUS.index(far_above)
        rows[13:14, :] = above[x, j : j + 1, :]
        rows[6:8, :] = below[x, 24:26, :] * has_below
        rows[14:16, :] = above[x, 24:26, :] * has_above


def step_layer(x, read, read_mask, post, post2, bits_out):
    def body(t, carry):
        bits = open_bits(read_mask, t)
        own = [post[k, x, rows_of(t), :] for k in range(19)]
        out = collide(stream(read, own, bits, t))
        for k in range(19):
            post2[k, x, rows_of(t), :] = out[k]
        bits_out[x, tile_rows(t), :] = bits
        return carry

    lax.fori_loop(0, TILES + 1, body, 0, unroll=TILES + 1)
    for k in CY_PLUS:
        post2[k, x, 7:8, :] = post2[k, x, 79:80, :]


def middle_kernel(nx, post, flags, post2, bits_out):
    for x in range(1, nx - 1):
        step_layer(
            x,
            lambda k, dx, tile, x=x: post[k, x - dx, rows_of(tile), :],
            lambda dx, tile, x=x: flags[x - dx, rows_of(tile), :],
            post,
            post2,
            bits_out,
        )


def outer_kernel(
    nx, first, post, flags, face, edge, post2_in, bits_in, post2, bits_out, send, halo, halo_flags
):
    x, near = (0, -1) if first else (nx - 1, nx)
    dirs, k_below, k_above = (CX_PLUS, 7, 9) if first else (CX_MINUS, 10, 8)
    for j, k in enumerate(dirs):
        halo[j, 8:72, :] = face[j * ROWS : (j + 1) * ROWS, :]
        halo[j, 79:80, :] = edge[j : j + 1, :]
        halo[j, 72:73, :] = edge[8 + j : 9 + j, :]
        if k == k_below:
            halo[j, 7:8, :] = edge[j : j + 1, :]
            halo[j, 78:79, :] = edge[5:6, :]
        if k == k_above:
            halo[j, 73:74, :] = edge[13:14, :]
            halo[j, 80:81, :] = face[j * ROWS : j * ROWS + 1, :]
    halo_flags[8:72, :] = face[5 * ROWS : 6 * ROWS, :].astype(I32)
    halo_flags[79:80, :] = edge[6:7, :].astype(I32)
    halo_flags[7:8, :] = edge[6:7, :].astype(I32)
    halo_flags[78:79, :] = edge[7:8, :].astype(I32)
    halo_flags[72:73, :] = edge[14:15, :].astype(I32)
    halo_flags[73:74, :] = edge[15:16, :].astype(I32)
    halo_flags[80:81, :] = face[5 * ROWS : 5 * ROWS + 1, :].astype(I32)

    def read(k, dx, tile):
        if x - dx == near:
            return halo[dirs.index(k), rows_of(tile), :]
        return post[k, x - dx, rows_of(tile), :]

    def read_mask(dx, tile):
        if x - dx == near:
            return halo_flags[rows_of(tile), :]
        return flags[x - dx, rows_of(tile), :]

    step_layer(x, read, read_mask, post, post2, bits_out)
    dirs, k_below, k_above = (CX_MINUS, 10, 8) if first else (CX_PLUS, 7, 9)
    for j, k in enumerate(dirs):
        send[j * ROWS : (j + 1) * ROWS, :] = post2[k, x, 8:72, :]
    send[320:321, :] = post2[k_below, x, 79:80, :]
    send[321:322, :] = post2[k_above, x, 72:73, :]


def final_layer(x, read, post2, bits, result, flow, out, sem):
    def body(t, carry):
        rows = tile_rows(t)
        own = [post2[k, x, rows_of(t), :] for k in range(19)]
        f = stream(read, own, bits[x, rows, :], t)
        for k in range(19):
            result[k, rows, :] = f[k]
        rho, ux, uy, uz = velocity_of(f)
        flow[0, x, rows, :] = ux
        flow[1, x, rows, :] = uy
        flow[2, x, rows, :] = uz
        return carry

    lax.fori_loop(0, TILES, body, 0, unroll=TILES)
    copy = pltpu.make_async_copy(result, out.at[:, x], sem)
    copy.start()
    return copy


def final_middle_kernel(nx, post2, bits, voxel, out, flow, table, result, field, sems):
    copies = []
    for i, x in enumerate(range(1, nx - 1)):
        read = lambda k, dx, tile, x=x: post2[k, x - dx, rows_of(tile), :]
        copies.append(final_layer(x, read, post2, bits, result.at[i], flow, out, sems.at[i]))

    def store(g, c, row):
        table[g, c : c + 1, :] = row

    found_flow(voxel, flow, list(range(1, nx - 1)), field, store)
    for copy in copies:
        copy.wait()


def final_outer_kernel(
    n, per, nx, out_in, flow_in, post2, bits, after, before, voxel, owner, part, out, flow, *refs
):
    outs, (halo, result, table, field, sems) = refs[:n], refs[n:]
    copies = []
    for i, (face, first) in enumerate(((after, False), (before, True))):
        x, near = (0, -1) if first else (nx - 1, nx)
        dirs, k_below, k_above = (CX_PLUS, 7, 9) if first else (CX_MINUS, 10, 8)
        for j in range(5):
            halo[i, j, 8:72, :] = face[j * ROWS : (j + 1) * ROWS, :]
        halo[i, dirs.index(k_below), 7:8, :] = face[320:321, :]
        halo[i, dirs.index(k_above), 72:73, :] = face[321:322, :]

        def read(k, dx, tile, i=i, x=x, near=near, dirs=dirs):
            if x - dx == near:
                return halo[i, dirs.index(k), rows_of(tile), :]
            return post2[k, x - dx, rows_of(tile), :]

        copies.append(final_layer(x, read, post2, bits, result.at[i], flow, out, sems.at[i]))

    def store(g, c, row):
        table[g, c : c + 1, :] = part[g, c : c + 1, :] + row

    found_flow(voxel, flow, [0, nx - 1], field, store)
    patches = voxel.shape[0]
    me = lax.axis_index("xs")
    rank = ranks(owner, patches)
    for d in range(n):
        target = me ^ d
        for r in range(per):
            found = jnp.int32(0)
            for g in range(patches):
                found = jnp.where((owner[g] == target) & (rank[g] == r), g, found)
            outs[d][r * 3 : r * 3 + 3, :] = table[found, 0:3, :]
    for copy in copies:
        copy.wait()


def pair_kernel(begin, end, *refs):
    one_pair, steps, finish = pair_parts(begin, end, *refs)
    lax.fori_loop(0, steps, lambda i, carry: one_pair(i), None, unroll=4)
    finish()


def pair_parts(begin, end, pair_tiles, vel, rows, cols, left, right, noise, *refs):
    base, theta, along, acc = refs[-4:]
    tile = noise.shape[-1]
    count = cols.shape[2]
    pairs = noise.shape[1]
    patches = end - begin
    eye = lax.broadcasted_iota(I32, (tile, tile), 0) == lax.broadcasted_iota(I32, (tile, tile), 1)
    scale = jnp.where(eye, 15.0, 0.0).astype(BF16)
    acc[...] = jnp.zeros_like(acc)
    for g in range(patches):
        for p in range(pairs):
            theta[g * pairs + p] = lax.dot_general(
                scale, noise[begin + g, p], (((1,), (1,)), ((), ())), preferred_element_type=F32
            )
            first, second = pair_tiles[begin + g, 0, p], pair_tiles[begin + g, 1, p]
            along[g * pairs + p] = jnp.dot(
                left[begin + g, second], right[begin + g, first], preferred_element_type=F32
            )

    def one_pair(i):
        g, p = i // pairs, i % pairs
        first = pair_tiles[begin + g, 0, p]
        second = pair_tiles[begin + g, 1, p]
        mine = [rows[begin + g, c, first] for c in range(3)]
        total = []
        for s in range(tile // 8):
            part = slice(8 * s, 8 * s + 8)
            dx, dy, dz = [mine[c] - cols[begin + g, c, second, part, :] for c in range(3)]
            square = (dx * dx + 0.01) + (dy * dy + dz * dz)
            close = jnp.maximum(lax.rsqrt(square) - 1.0, 0.0)
            force = close * ((theta[i, part, :] + 25.0) - close * along[i, part, :])
            here = [force * dx, force * dy, force * dz]
            total = here if not total else [a + b for a, b in zip(total, here)]
        for c in range(3):
            acc[g, first, c] += total[c]

    def finish():
        for g in range(patches):
            for c in range(3):
                force = jnp.concatenate(
                    [jnp.sum(acc[g, j, c], axis=0, keepdims=True) for j in range(count)], axis=1
                )
                speed = vel[c, begin + g : begin + g + 1, :]
                base[c, begin + g : begin + g + 1, :] = 0.5 * speed + 0.04 * force

    return one_pair, patches * pairs, finish


def sums_and_pairs_kernel(n, per, begin, end, *refs):
    sums, rest = refs[: n + 2], refs[n + 2 :]
    pairs, (total, base, table, theta, along, acc) = rest[:7], rest[8:]
    one_pair, steps, finish = pair_parts(begin, end, *pairs, base, theta, along, acc)
    patches = sums[1].shape[0]

    def beside(g):
        for i in range(g * steps // patches, (g + 1) * steps // patches):
            one_pair(i)

    scatter_kernel(n, per, beside, *sums, total, table)
    finish()


def split(value):
    high = value.astype(BF16)
    return high, (value - high.astype(F32)).astype(BF16)


def ranks(owner, count):
    out = []
    for g in range(count):
        rank = jnp.int32(0)
        for h in range(g):
            rank = rank + (owner[h] == owner[g]).astype(I32)
        out.append(rank)
    return out


def one_hot(index, extent):
    want = index.astype(F32).astype(BF16)
    place = lax.broadcasted_iota(I32, (extent, index.shape[1]), 0).astype(F32).astype(BF16)
    return place == want


def scatter_kernel(n, per, beside, owner, voxel, vel, *refs):
    sent, out, table = refs[: n - 1], refs[n - 1], refs[n]
    me = lax.axis_index("xs")
    beads = voxel.shape[1]
    for r in range(per):
        for c in range(3):
            table[me, r, c : c + 1, :] = vel[c, pl.ds(me * per + r, 1), :]
        for d in range(1, n):
            source = lax.rem(me + n - d, n)
            for c in range(3):
                table[source, r, c : c + 1, :] = sent_velocity(sent, n, d, r, c)
    out[...] = jnp.zeros_like(out)
    rank = ranks(owner, voxel.shape[0])
    one, zero = BF16(1), BF16(0)
    for g in range(voxel.shape[0]):
        index = voxel[g : g + 1, :]
        lanes = jnp.where(one_hot(index & 255, 256), one, zero)
        at_row = one_hot(index >> 8, out.shape[1])
        values = table[owner[g], rank[g]]
        lanes2 = jnp.concatenate([lanes, lanes], axis=1)
        for c in range(3):
            high, low = split(values[c : c + 1, :])
            left = jnp.concatenate(
                [jnp.where(at_row, high, zero), jnp.where(at_row, low, zero)], axis=1
            )
            out[c] += lax.dot_general(
                left, lanes2, (((1,), (1,)), ((), ())), preferred_element_type=F32
            )
        out[3] += lax.dot_general(
            jnp.where(at_row, one, zero), lanes, (((1,), (1,)), ((), ())), preferred_element_type=F32
        )
        beside(g)


def found_flow(voxel, flow, layers, field, store):
    patches, beads = voxel.shape
    rows = len(layers) * ROWS
    for c in range(3):
        for i, x in enumerate(layers):
            high, low = split(flow[c, x])
            field[c * rows + i * ROWS : c * rows + (i + 1) * ROWS, 0:256] = high
            field[c * rows + i * ROWS : c * rows + (i + 1) * ROWS, 256:512] = low
    place = lax.broadcasted_iota(I32, (rows, beads), 0)
    step = (layers[1] - layers[0] - 1) * ROWS
    place = place + layers[0] * ROWS + jnp.where(place >= ROWS, step, 0)
    one, zero = BF16(1), BF16(0)
    for g in range(patches):
        index = voxel[g : g + 1, :]
        lanes = jnp.where(one_hot(index & 255, 256), one, zero)
        lanes2 = jnp.concatenate([lanes, lanes], axis=0)
        at_row = place == (index >> 8)
        found = jnp.dot(field[...], lanes2, preferred_element_type=F32)
        for c in range(3):
            part = jnp.where(at_row, found[c * rows : (c + 1) * rows], 0.0)
            store(g, c, jnp.sum(part, axis=0, keepdims=True))


def field_kernel(total, flow, field):
    for x in range(field.shape[1]):
        rows = slice(x * ROWS, (x + 1) * ROWS)
        number = 10.0 * total[3, rows, :]
        for c in range(3):
            field[c, x] = 0.5 * total[c, rows, :] - number * flow[c, x]


def final_kernel(n, per, pos, base, *refs):
    flows, new_pos, new_vel = refs[:n][::-1], refs[n], refs[n + 1]
    me = lax.axis_index("xs")
    for d in range(n):
        source = me ^ d
        for r in range(per):
            at = pl.ds(source * per + r, 1)
            for c in range(3):
                speed = base[c, at, :] + 10.0 * flows[d][r * 3 + c : r * 3 + c + 1, :]
                new_vel[c, at, :] = speed
                new_pos[c, at, :] = pos[c, at, :] + 0.04 * speed


def shift(value, axis, by):
    n = lax.axis_size(axis)
    return lax.ppermute(value, axis, [(i, (i + by) % n) for i in range(n)])


def swap(value, axis, by):
    n = lax.axis_size(axis)
    return lax.ppermute(value, axis, [(i, i ^ by) for i in range(n)])


def pair_call(begin, end, pair_tiles, vel, rows, cols, left, right, noise, given, after):
    tile = noise.shape[-1]
    return call(
        functools.partial(pair_kernel, begin, end),
        [pair_tiles, vel, rows, cols, left, right, noise] + given,
        jax.ShapeDtypeStruct(vel.shape, F32),
        "pair_forces",
        cost(1000, 1000),
        after=after,
        specs={0: SMEM_SPEC},
        out_specs=VMEM_SPEC,
        input_output_aliases={7: 0} if given else {},
        scratch_shapes=[
            pltpu.VMEM(((end - begin) * noise.shape[1], tile, tile), F32),
            pltpu.VMEM(((end - begin) * noise.shape[1], tile, tile), F32),
            pltpu.VMEM((end - begin, cols.shape[2], 3, 8, tile), F32),
        ],
    )


def per_device(
    populations, fluid_mask, patch_voxel, patch_owner, positions, velocities, pair_tiles, pair_noise
):
    n = lax.axis_size("xs")
    patches, beads = patch_voxel.shape
    per = patches // n
    nx = populations.shape[1]
    lanes = populations.shape[3]
    tiles = beads // 128
    arr = lambda *shape: jax.ShapeDtypeStruct(shape, F32)
    ints = lambda *shape: jax.ShapeDtypeStruct(shape, I32)
    vmem, dma = pltpu.VMEM, pltpu.SemaphoreType.DMA
    positions = jnp.transpose(positions, (1, 0, 2))
    velocities = jnp.transpose(velocities, (1, 0, 2))
    pair_tiles = jnp.transpose(pair_tiles, (0, 2, 1))

    post, fwd, bwd, up, down, *layouts = call(
        functools.partial(collide_kernel, n, per, nx),
        [in_hbm(value) for value in (populations, fluid_mask, positions, velocities)],
        [arr(19, nx, PAD, lanes), arr(384, lanes), arr(384, lanes)]
        + [arr(nx, 32, lanes)] * 2
        + [
            arr(patches, 3, tiles, 8, 128),
            arr(patches, 3, tiles, 128, 128),
            jax.ShapeDtypeStruct((patches, tiles, 128, 48), BF16),
            jax.ShapeDtypeStruct((patches, tiles, 48, 128), BF16),
        ]
        + [arr(16, lanes)] * (n - 3),
        "collide_first",
        cost(3_000_000_000, 11_000_000),
        specs={i: ANY_SPEC for i in range(4)},
        out_specs=[VMEM_SPEC] * (n + 6),
        scratch_shapes=[
            vmem((nx, 19, ROWS, lanes), F32),
            vmem((nx, ROWS, lanes), I32),
            vmem(positions.shape, F32),
            vmem(velocities.shape, F32),
            dma((2 * nx,)),
            dma((3,)),
        ],
    )
    before = shift(fwd, "ax", 1)
    after = shift(bwd, "ax", -1)
    layouts, others = layouts[:4], layouts[4:]
    below = shift(up, "xs", 1)
    above = shift(down, "xs", -1)
    sent = [below] + [shift(other, "xs", d + 2) for d, other in enumerate(others)] + [above]

    cuts = (patches * 5 // 8, patches * 7 // 8)
    bead_args = (pair_tiles, velocities, *layouts, pair_noise)
    base = pair_call(0, cuts[0], *bead_args, [], [down])

    post, edge_fwd, edge_bwd, flags = call(
        functools.partial(edges_kernel, n, nx),
        [post, fluid_mask, below, above],
        [arr(*post.shape), arr(16, lanes), arr(16, lanes), ints(nx, PAD, lanes)],
        "edges",
        cost(1000, 1000),
        after=[base],
        out_specs=[VMEM_SPEC] * 4,
        input_output_aliases={0: 0},
    )
    edge_before = shift(edge_fwd, "ax", 1)
    edge_after = shift(edge_bwd, "ax", -1)

    post2, bits = call(
        functools.partial(middle_kernel, nx),
        [post, flags],
        [arr(19, nx, PAD, lanes), ints(nx, 72, lanes)],
        "middle_layers",
        cost(1000, 1000),
        out_specs=[VMEM_SPEC] * 2,
    )
    def outer(first, face, edge, post2, bits, after):
        return call(
            functools.partial(outer_kernel, nx, first),
            [post, flags, face, edge, post2, bits],
            [arr(*post2.shape), ints(*bits.shape), arr(328, lanes)],
            "first_layer" if first else "last_layer",
            cost(1000, 1000),
            after=after,
            out_specs=[VMEM_SPEC] * 3,
            input_output_aliases={4: 0, 5: 1},
            scratch_shapes=[vmem((5, PAD, lanes), F32), vmem((PAD, lanes), I32)],
        )

    base = pair_call(cuts[0], cuts[1], *bead_args, [base], [flags])
    post2, bits, bwd2 = outer(True, before, edge_before, post2, bits, [base, after, edge_after] + sent[1:-1])
    after2 = shift(bwd2, "ax", -1)
    post2, bits, fwd2 = outer(False, after, edge_after, post2, bits, [])
    before2 = shift(fwd2, "ax", 1)

    out, flow, part = call(
        functools.partial(final_middle_kernel, nx),
        [post2, bits, patch_voxel],
        [arr(*populations.shape), arr(3, nx, ROWS, lanes), arr(patches, 8, beads)],
        "final_middle",
        cost(1000, 1000),
        after=[fwd2],
        out_specs=[ANY_SPEC, VMEM_SPEC, VMEM_SPEC],
        scratch_shapes=[
            vmem((nx - 2, 19, ROWS, lanes), F32),
            vmem((3 * (nx - 2) * ROWS, 2 * lanes), BF16),
            dma((nx - 2,)),
        ],
    )
    last_pairs = (patches - cuts[1]) * pair_noise.shape[1]
    total, base = call(
        functools.partial(sums_and_pairs_kernel, n, per, cuts[1], patches),
        [patch_owner, patch_voxel, velocities] + sent + list(bead_args) + [base],
        [arr(4, nx * ROWS, lanes), arr(*velocities.shape)],
        "bead_sums",
        cost(1000, 1000),
        after=[fwd2],
        specs={0: SMEM_SPEC, n + 2: SMEM_SPEC},
        out_specs=[VMEM_SPEC] * 2,
        input_output_aliases={n + 9: 1},
        scratch_shapes=[
            vmem((n, per, 8, beads), F32),
            vmem((last_pairs, 128, 128), F32),
            vmem((last_pairs, 128, 128), F32),
            vmem((patches - cuts[1], tiles, 3, 8, 128), F32),
        ],
    )
    out, flow, *flows = call(
        functools.partial(final_outer_kernel, n, per, nx),
        [out, flow, post2, bits, after2, before2, patch_voxel, patch_owner, part],
        [arr(*populations.shape), arr(*flow.shape)] + [arr(8, beads)] * n,
        "final_outer",
        cost(1000, 1000),
        after=[total, base],
        specs={0: ANY_SPEC, 7: SMEM_SPEC},
        out_specs=[ANY_SPEC] + [VMEM_SPEC] * (n + 1),
        input_output_aliases={0: 0, 1: 1},
        scratch_shapes=[
            vmem((2, 5, PAD, lanes), F32),
            vmem((2, 19, ROWS, lanes), F32),
            vmem((patches, 8, beads), F32),
            vmem((3 * 2 * ROWS, 2 * lanes), BF16),
            dma((2,)),
        ],
    )
    sent_flows = [flows[0]] + [swap(flows[d], "xs", d) for d in range(1, n)]
    field = call(
        field_kernel,
        [total, flow],
        arr(3, nx, ROWS, lanes),
        "drag_field",
        cost(1000, 1000),
        after=[flows[1]],
        out_specs=VMEM_SPEC,
    )
    new_pos, new_vel = call(
        functools.partial(final_kernel, n, per),
        [positions, base] + sent_flows[::-1],
        [arr(*positions.shape)] * 2,
        "bead_update",
        cost(1000, 1000),
        out_specs=[VMEM_SPEC] * 2,
    )
    return out, jnp.transpose(new_pos, (1, 0, 2)), jnp.transpose(new_vel, (1, 0, 2)), field


def solution(mesh):
    return jax.shard_map(
        per_device,
        mesh=mesh,
        in_specs=(
            P(None, "ax", "xs", None),
            P("ax", "xs", None),
            P(("ax", "xs"), None),
            P(("ax", "xs")),
            P(("ax", "xs"), None, None),
            P(("ax", "xs"), None, None),
            P(("ax", "xs"), None, None),
            P(("ax", "xs"), None, None, None),
        ),
        out_specs=(
            P(None, "ax", "xs", None),
            P(("ax", "xs"), None, None),
            P(("ax", "xs"), None, None),
            P(None, "ax", "xs", None),
        ),
        check_vma=False,
    )
```

```python
import functools

import jax
import jax.numpy as jnp
from jax import lax
from jax.experimental import pallas as pl
from jax.experimental.pallas import tpu as pltpu
from jax.sharding import PartitionSpec as P

DIRS = [
    (0, 0, 0),
    (1, 0, 0),
    (-1, 0, 0),
    (0, 1, 0),
    (0, -1, 0),
    (0, 0, 1),
    (0, 0, -1),
    (1, 1, 0),
    (-1, -1, 0),
    (1, -1, 0),
    (-1, 1, 0),
    (1, 0, 1),
    (-1, 0, -1),
    (1, 0, -1),
    (-1, 0, 1),
    (0, 1, 1),
    (0, -1, -1),
    (0, 1, -1),
    (0, -1, 1),
]
OPP = [0, 2, 1, 4, 3, 6, 5, 8, 7, 10, 9, 12, 11, 14, 13, 16, 15, 18, 17]
CX_PLUS = [k for k in range(19) if DIRS[k][0] == 1]
CX_MINUS = [k for k in range(19) if DIRS[k][0] == -1]
CY_PLUS = [k for k in range(19) if DIRS[k][1] == 1]
CY_MINUS = [k for k in range(19) if DIRS[k][1] == -1]
F32 = jnp.float32
BF16 = jnp.bfloat16
I32 = jnp.int32
VMEM_SPEC = pl.BlockSpec(memory_space=pltpu.VMEM)
SMEM_SPEC = pl.BlockSpec(memory_space=pltpu.SMEM)
ANY_SPEC = pl.BlockSpec(memory_space=pl.ANY)

ROWS = 64
PAD = 88
TILES = ROWS // 8


def params(mib=16):
    return pltpu.CompilerParams(vmem_limit_bytes=mib * 1024 * 1024)


def cost(flops, bytes_accessed):
    return pl.CostEstimate(flops=flops, bytes_accessed=bytes_accessed, transcendentals=0)


def call(kernel, ins, out_shape, name, estimate, after=(), specs=None, **kwargs):
    specs = specs or {}
    count, extra = len(ins), len(after)

    def body(*refs):
        kernel(*refs[:count], *refs[count + extra :])

    return pl.pallas_call(
        body,
        in_specs=[specs.get(i, VMEM_SPEC) for i in range(count)] + [ANY_SPEC] * extra,
        out_shape=out_shape,
        cost_estimate=estimate,
        name=name,
        **{"compiler_params": params(), **kwargs},
    )(*ins, *after)


def in_hbm(value):
    return pltpu.with_memory_space_constraint(value, pltpu.HBM)


def tree(values):
    while len(values) > 1:
        values = [
            values[i] + values[i + 1] if i + 1 < len(values) else values[i]
            for i in range(0, len(values), 2)
        ]
    return values[0]


def velocity_of(f):
    diff = [None] + [f[k] - f[k + 1] for k in range(1, 19, 2)]
    rho = tree([f[k] for k in range(1, 19)] + [f[0]])
    m1, m3, m5, m7, m9, m11, m13, m15, m17 = diff[1:]
    jx = m1 + ((m7 + m9) + (m11 + m13))
    jy = m3 + ((m7 - m9) + (m15 + m17))
    jz = m5 + ((m11 - m13) + (m15 - m17))
    inv = 1.0 / rho
    return rho, jx * inv, jy * inv, jz * inv


def collide(f):
    rho, ux, uy, uz = velocity_of(f)
    base = (1.25 * rho) * (1.0 - 1.5 * (ux * ux + uy * uy + uz * uz))
    ux, uy, uz = 1.5 * ux, 1.5 * uy, 1.5 * uz
    even1, even2 = base * (1.0 / 18.0), base * (1.0 / 36.0)
    odd1, odd2 = rho * (2.5 / 18.0), rho * (2.5 / 36.0)
    out = [None] * 19
    out[0] = base * (1.0 / 3.0) - 0.25 * f[0]
    for k in range(1, 19, 2):
        dx, dy, dz = DIRS[k]
        proj = None
        for sign, comp in ((dx, ux), (dy, uy), (dz, uz)):
            if sign == 0:
                continue
            if proj is None:
                proj = comp
            else:
                proj = proj + comp if sign > 0 else proj - comp
        even, odd = (even1, odd1) if k < 7 else (even2, odd2)
        odd = odd * proj
        even = even + odd * proj
        out[k] = (even + odd) - 0.25 * f[k]
        out[k + 1] = (even - odd) - 0.25 * f[k + 1]
    return out


def shifted(read, tile, dy, dz):
    here = read(tile)
    if dy != 0:
        sub = lax.broadcasted_iota(I32, here.shape, 0)
        if dy > 0:
            here = pltpu.roll(jnp.where(sub == 7, read(tile - 1), here), 1, 0)
        else:
            here = pltpu.roll(jnp.where(sub == 0, read(tile + 1), here), 7, 0)
    if dz != 0:
        here = pltpu.roll(here, 1 if dz > 0 else here.shape[1] - 1, 1)
    return here


def rows_of(tile):
    return pl.ds(pl.multiple_of(8 + 8 * tile, 8), 8)


def open_bits(read_mask, tile):
    bits = None
    cache = {}
    for k in range(1, 19):
        dx, dy, dz = DIRS[k]
        if (dx, dy) not in cache:
            cache[(dx, dy)] = shifted(functools.partial(read_mask, dx), tile, dy, 0)
        m = cache[(dx, dy)]
        if dz != 0:
            lane = lax.broadcasted_iota(I32, m.shape, 1)
            last = m.shape[1] - 1
            m = pltpu.roll(m, 1 if dz > 0 else last, 1)
            m = jnp.where(lane == (0 if dz > 0 else last), 0, m)
        m = m << k
        bits = m if bits is None else bits | m
    return bits


def stream(read, own, bits, tile):
    out = [own[0]]
    for k in range(1, 19):
        dx, dy, dz = DIRS[k]
        source = shifted(functools.partial(read, k, dx), tile, dy, dz)
        out.append(jnp.where((bits & (1 << k)) != 0, source, own[OPP[k]]))
    return out


def tile_rows(t):
    return pl.ds(pl.multiple_of(8 * t, 8), 8)


def three(value):
    high, rest = value.astype(BF16), value - value.astype(BF16).astype(F32)
    mid = rest.astype(BF16)
    return high.astype(F32), mid.astype(F32), (rest - mid.astype(F32)).astype(BF16).astype(F32)


def spread_beads(spots, speeds, rows, cols, left, right):
    patches, beads = spots.shape[1:]
    tile = cols.shape[-1]
    count = beads // tile
    place = lax.broadcasted_iota(I32, (48, 3 * tile), 0)
    comp = lax.broadcasted_iota(I32, (48, 3 * tile), 1) // tile
    part = ((place >> 3) == 0) | ((place >> 3) == 2) | ((place >> 3) == 5)
    spread = jnp.where(part & ((place & 7) == comp + 2), -1.0, 0.0).astype(BF16)
    stacks = []
    for g in range(patches):
        x = [spots[c, g : g + 1, :] for c in range(3)]
        w = [4.5 * speeds[c, g : g + 1, :] for c in range(3)]
        for c in range(3):
            for j in range(count):
                rows[g, c, j] = jnp.broadcast_to(x[c][:, j * tile : (j + 1) * tile], (8, tile))
        dot = x[0] * w[0] + (x[1] * w[1] + x[2] * w[2])
        one = jnp.ones_like(dot)
        high, mid, low = three(jnp.concatenate([dot, one] + w + x, axis=0))
        found = jnp.concatenate([high, mid, high, low, mid, high], axis=0).astype(BF16)
        for j in range(count):
            right[g, j] = found[:, j * tile : (j + 1) * tile]
        high, mid, low = three(jnp.concatenate([one, dot] + [-v for v in x + w], axis=0))
        stacks += [high, high, mid, high, mid, low]
    if -48 * patches % 128:
        stacks.append(jnp.zeros((-48 * patches % 128, beads), F32))
    turned = jnp.concatenate(stacks, axis=0).T.astype(BF16)
    for g in range(patches):
        for j in range(count):
            here = turned[j * tile : (j + 1) * tile, 48 * g : 48 * (g + 1)]
            left[g, j] = here
            wide = jnp.dot(here, spread, preferred_element_type=F32)
            for c in range(3):
                cols[g, c, j] = wide[:, c * tile : (c + 1) * tile]


def collide_kernel(n, per, nx, pop, mask, vel, post, fwd, bwd, up, down, *rest):
    others, (here, flags, speeds, sems, small) = rest[: n - 3], rest[n - 3 :]
    order = [(x, h) for x in [0, nx - 1] + list(range(1, nx - 1)) for h in range(1)]
    span = ROWS // 1
    copies = [
        pltpu.make_async_copy(
            pop.at[:, x, pl.ds(h * span, span)], here.at[x, :, pl.ds(h * span, span)], sems.at[i]
        )
        for i, (x, h) in enumerate(order)
    ]
    extra = [
        pltpu.make_async_copy(vel, speeds, small.at[0]),
        pltpu.make_async_copy(mask, flags, small.at[1]),
    ]
    ahead = 3
    for copy in copies[:ahead] + extra:
        copy.start()
    me = lax.axis_index("xs")
    extra[0].wait()
    for d in range(1, n):
        target = lax.rem(me + d, n)
        for r in range(per):
            for c in range(3):
                row = speeds[c, pl.ds(target * per + r, 1), :]
                for half in range(2):
                    i = (r * 3 + c) * 2 + half
                    piece = row[:, half * 256 : (half + 1) * 256]
                    if d in (1, n - 1):
                        ref = up if d == 1 else down
                        ref[i // 3, 26 + i % 3 : 27 + i % 3, :] = piece
                    else:
                        others[d - 2][i : i + 1, :] = piece
    extra[1].wait()
    for i, (x, h) in enumerate(order):
        copies[i].wait()
        if i + ahead < len(copies):
            copies[i + ahead].start()

        def body(t, carry, x=x, h=h):
            t = t + h * (TILES // 1)
            out = collide([here[x, k, tile_rows(t), :] for k in range(19)])
            for k in range(19):
                post[k, x, rows_of(t), :] = out[k]
            return carry

        lax.fori_loop(0, TILES // 1, body, 0, unroll=TILES // 1)
        for ref, near, beyond, dirs in ((down, 0, 1, CY_MINUS), (up, ROWS - 1, ROWS - 2, CY_PLUS)):
            for k in range(19):
                ref[x, k : k + 1, :] = post[k, x, 8 + near : 9 + near, :]
            for j, k in enumerate(dirs):
                ref[x, 19 + j : 20 + j, :] = post[k, x, 8 + beyond : 9 + beyond, :]
            ref[x, 24:25, :] = flags[x, near : near + 1, :].astype(F32)
            ref[x, 25:26, :] = flags[x, beyond : beyond + 1, :].astype(F32)
    for x, ref, dirs in ((nx - 1, fwd, CX_PLUS), (0, bwd, CX_MINUS)):
        for j, k in enumerate(dirs):
            ref[j * ROWS : (j + 1) * ROWS, :] = post[k, x, 8:72, :]
        ref[5 * ROWS : 6 * ROWS, :] = flags[x].astype(F32)


def sent_velocity(refs, n, d, r, c):
    out = []
    for half in range(2):
        i = (r * 3 + c) * 2 + half
        if d in (1, n - 1):
            out.append(refs[d - 1][i // 3, 26 + i % 3 : 27 + i % 3, :])
        else:
            out.append(refs[d - 1][i : i + 1, :])
    return jnp.concatenate(out, axis=1)


def edges_kernel(n, nx, post_in, mask, below, above, post, fwd, bwd, flags):
    me = lax.axis_index("xs")
    has_below, has_above = (me > 0).astype(F32), (me < n - 1).astype(F32)
    for x in range(nx):
        for k in range(19):
            post[k, x, 79:80, :] = below[x, k : k + 1, :]
            post[k, x, 72:73, :] = above[x, k : k + 1, :]
        for j, k in enumerate(CY_PLUS):
            post[k, x, 7:8, :] = below[x, k : k + 1, :]
            post[k, x, 78:79, :] = below[x, 19 + j : 20 + j, :]
        for j, k in enumerate(CY_MINUS):
            post[k, x, 73:74, :] = above[x, 19 + j : 20 + j, :]
            post[k, x, 80:81, :] = post[k, x, 8:9, :]
        flags[x, 8:72, :] = mask[x]
        near = (below[x, 24:25, :] * has_below).astype(I32)
        flags[x, 79:80, :] = near
        flags[x, 7:8, :] = near
        flags[x, 78:79, :] = (below[x, 25:26, :] * has_below).astype(I32)
        flags[x, 72:73, :] = (above[x, 24:25, :] * has_above).astype(I32)
        flags[x, 73:74, :] = (above[x, 25:26, :] * has_above).astype(I32)
        flags[x, 80:81, :] = mask[x, 0:1, :]
    for rows, x, dirs, far_below, far_above in (
        (fwd, nx - 1, CX_PLUS, 7, 9),
        (bwd, 0, CX_MINUS, 10, 8),
    ):
        for j, k in enumerate(dirs):
            rows[j : j + 1, :] = below[x, k : k + 1, :]
            rows[8 + j : 9 + j, :] = above[x, k : k + 1, :]
        j = 19 + CY_PLUS.index(far_below)
        rows[5:6, :] = below[x, j : j + 1, :]
        j = 19 + CY_MINUS.index(far_above)
        rows[13:14, :] = above[x, j : j + 1, :]
        rows[6:8, :] = below[x, 24:26, :] * has_below
        rows[14:16, :] = above[x, 24:26, :] * has_above


def step_layer(x, read, read_mask, post, post2, bits_out):
    def body(t, carry):
        bits = open_bits(read_mask, t)
        own = [post[k, x, rows_of(t), :] for k in range(19)]
        out = collide(stream(read, own, bits, t))
        for k in range(19):
            post2[k, x, rows_of(t), :] = out[k]
        bits_out[x, tile_rows(t), :] = bits
        return carry

    lax.fori_loop(0, TILES + 1, body, 0, unroll=TILES + 1)
    for k in CY_PLUS:
        post2[k, x, 7:8, :] = post2[k, x, 79:80, :]


def middle_kernel(nx, post, flags, post2, bits_out):
    for x in range(1, nx - 1):
        step_layer(
            x,
            lambda k, dx, tile, x=x: post[k, x - dx, rows_of(tile), :],
            lambda dx, tile, x=x: flags[x - dx, rows_of(tile), :],
            post,
            post2,
            bits_out,
        )


def outer_kernel(
    nx, first, post, flags, face, edge, post2_in, bits_in, post2, bits_out, send, halo, halo_flags
):
    x, near = (0, -1) if first else (nx - 1, nx)
    dirs, k_below, k_above = (CX_PLUS, 7, 9) if first else (CX_MINUS, 10, 8)
    for j, k in enumerate(dirs):
        halo[j, 8:72, :] = face[j * ROWS : (j + 1) * ROWS, :]
        halo[j, 79:80, :] = edge[j : j + 1, :]
        halo[j, 72:73, :] = edge[8 + j : 9 + j, :]
        if k == k_below:
            halo[j, 7:8, :] = edge[j : j + 1, :]
            halo[j, 78:79, :] = edge[5:6, :]
        if k == k_above:
            halo[j, 73:74, :] = edge[13:14, :]
            halo[j, 80:81, :] = face[j * ROWS : j * ROWS + 1, :]
    halo_flags[8:72, :] = face[5 * ROWS : 6 * ROWS, :].astype(I32)
    halo_flags[79:80, :] = edge[6:7, :].astype(I32)
    halo_flags[7:8, :] = edge[6:7, :].astype(I32)
    halo_flags[78:79, :] = edge[7:8, :].astype(I32)
    halo_flags[72:73, :] = edge[14:15, :].astype(I32)
    halo_flags[73:74, :] = edge[15:16, :].astype(I32)
    halo_flags[80:81, :] = face[5 * ROWS : 5 * ROWS + 1, :].astype(I32)

    def read(k, dx, tile):
        if x - dx == near:
            return halo[dirs.index(k), rows_of(tile), :]
        return post[k, x - dx, rows_of(tile), :]

    def read_mask(dx, tile):
        if x - dx == near:
            return halo_flags[rows_of(tile), :]
        return flags[x - dx, rows_of(tile), :]

    step_layer(x, read, read_mask, post, post2, bits_out)
    dirs, k_below, k_above = (CX_MINUS, 10, 8) if first else (CX_PLUS, 7, 9)
    for j, k in enumerate(dirs):
        send[j * ROWS : (j + 1) * ROWS, :] = post2[k, x, 8:72, :]
    send[320:321, :] = post2[k_below, x, 79:80, :]
    send[321:322, :] = post2[k_above, x, 72:73, :]


def final_layer(x, read, post2, bits, result, flow, out, sem):
    def body(t, carry):
        rows = tile_rows(t)
        own = [post2[k, x, rows_of(t), :] for k in range(19)]
        f = stream(read, own, bits[x, rows, :], t)
        for k in range(19):
            result[k, rows, :] = f[k]
        rho, ux, uy, uz = velocity_of(f)
        flow[0, x, rows, :] = ux
        flow[1, x, rows, :] = uy
        flow[2, x, rows, :] = uz
        return carry

    lax.fori_loop(0, TILES, body, 0, unroll=TILES)
    copy = pltpu.make_async_copy(result, out.at[:, x], sem)
    copy.start()
    return copy


def final_middle_kernel(nx, post2, bits, voxel, out, flow, table, result, field, sems):
    copies = []
    for i, x in enumerate(range(1, nx - 1)):
        read = lambda k, dx, tile, x=x: post2[k, x - dx, rows_of(tile), :]
        copies.append(final_layer(x, read, post2, bits, result.at[i], flow, out, sems.at[i]))

    def store(g, c, row):
        table[g, c : c + 1, :] = row

    found_flow(voxel, flow, list(range(1, nx - 1)), field, store)
    for copy in copies:
        copy.wait()


def final_outer_kernel(
    n, per, nx, out_in, flow_in, post2, bits, after, before, voxel, owner, part, out, flow, *refs
):
    outs, (halo, result, table, field, sems) = refs[:n], refs[n:]
    copies = []
    for i, (face, first) in enumerate(((after, False), (before, True))):
        x, near = (0, -1) if first else (nx - 1, nx)
        dirs, k_below, k_above = (CX_PLUS, 7, 9) if first else (CX_MINUS, 10, 8)
        for j in range(5):
            halo[i, j, 8:72, :] = face[j * ROWS : (j + 1) * ROWS, :]
        halo[i, dirs.index(k_below), 7:8, :] = face[320:321, :]
        halo[i, dirs.index(k_above), 72:73, :] = face[321:322, :]

        def read(k, dx, tile, i=i, x=x, near=near, dirs=dirs):
            if x - dx == near:
                return halo[i, dirs.index(k), rows_of(tile), :]
            return post2[k, x - dx, rows_of(tile), :]

        copies.append(final_layer(x, read, post2, bits, result.at[i], flow, out, sems.at[i]))

    def store(g, c, row):
        table[g, c : c + 1, :] = part[g, c : c + 1, :] + row

    found_flow(voxel, flow, [0, nx - 1], field, store)
    patches = voxel.shape[0]
    me = lax.axis_index("xs")
    rank = ranks(owner, patches)
    for d in range(n):
        target = me ^ d
        for r in range(per):
            found = jnp.int32(0)
            for g in range(patches):
                found = jnp.where((owner[g] == target) & (rank[g] == r), g, found)
            outs[d][r * 3 : r * 3 + 3, :] = table[found, 0:3, :]
    for copy in copies:
        copy.wait()


def pair_kernel(begin, end, *refs):
    prepare, one_pair, steps, finish = pair_parts(begin, end, *refs)
    ahead = steps // (end - begin)
    for i in range(-ahead, steps):
        if i + ahead < steps:
            prepare(i + ahead)
        if i >= 0:
            one_pair(i)
    finish()


def pair_parts(begin, end, pair_tiles, vel, rows, cols, left, right, noise, *refs):
    base, theta, along, acc = refs[-4:]
    tile = noise.shape[-1]
    count = cols.shape[2]
    pairs = noise.shape[1]
    patches = end - begin
    eye = lax.broadcasted_iota(I32, (tile, tile), 0) == lax.broadcasted_iota(I32, (tile, tile), 1)
    scale = jnp.where(eye, 15.0, 0.0).astype(BF16)
    acc[...] = jnp.zeros_like(acc)

    def prepare(i):
        g, p = i // pairs, i % pairs
        theta[i] = lax.dot_general(
            scale, noise[begin + g, p], (((1,), (1,)), ((), ())), preferred_element_type=F32
        )
        first, second = pair_tiles[begin + g, 0, p], pair_tiles[begin + g, 1, p]
        along[i] = jnp.dot(
            left[begin + g, second], right[begin + g, first], preferred_element_type=F32
        )

    def one_pair(i):
        g, p = i // pairs, i % pairs
        first = pair_tiles[begin + g, 0, p]
        second = pair_tiles[begin + g, 1, p]
        mine = [rows[begin + g, c, first] for c in range(3)]
        total = []
        for s in range(tile // 8):
            part = slice(8 * s, 8 * s + 8)
            dx, dy, dz = [mine[c] - cols[begin + g, c, second, part, :] for c in range(3)]
            square = (dx * dx + 0.01) + (dy * dy + dz * dz)
            close = jnp.maximum(lax.rsqrt(square) - 1.0, 0.0)
            force = close * ((theta[i, part, :] + 25.0) - close * along[i, part, :])
            here = [force * dx, force * dy, force * dz]
            total = here if not total else [a + b for a, b in zip(total, here)]
        for c in range(3):
            acc[g, first, c] += total[c]

    def finish():
        for g in range(patches):
            for c in range(3):
                force = jnp.concatenate(
                    [jnp.sum(acc[g, j, c], axis=0, keepdims=True) for j in range(count)], axis=1
                )
                speed = vel[c, begin + g : begin + g + 1, :]
                base[c, begin + g : begin + g + 1, :] = 0.5 * speed + 0.04 * force

    return prepare, one_pair, patches * pairs, finish


def sums_and_pairs_kernel(n, per, begin, end, *refs):
    sums, rest = refs[: n + 2], refs[n + 2 :]
    pairs, (total, base, table, theta, along, acc) = rest[:7], rest[8:]
    prepare, one_pair, steps, finish = pair_parts(begin, end, *pairs, base, theta, along, acc)
    for i in range(steps):
        prepare(i)
    patches = sums[1].shape[0]

    def beside(g):
        for i in range(g * steps // patches, (g + 1) * steps // patches):
            one_pair(i)

    scatter_kernel(n, per, beside, *sums, total, table)
    finish()


def split(value):
    high = value.astype(BF16)
    return high, (value - high.astype(F32)).astype(BF16)


def ranks(owner, count):
    out = []
    for g in range(count):
        rank = jnp.int32(0)
        for h in range(g):
            rank = rank + (owner[h] == owner[g]).astype(I32)
        out.append(rank)
    return out


def one_hot(index, extent):
    want = index.astype(F32).astype(BF16)
    place = lax.broadcasted_iota(I32, (extent, index.shape[1]), 0).astype(F32).astype(BF16)
    return place == want


def scatter_kernel(n, per, beside, owner, voxel, vel, *refs):
    sent, out, table = refs[: n - 1], refs[n - 1], refs[n]
    me = lax.axis_index("xs")
    beads = voxel.shape[1]
    for r in range(per):
        for c in range(3):
            table[me, r, c : c + 1, :] = vel[c, pl.ds(me * per + r, 1), :]
        for d in range(1, n):
            source = lax.rem(me + n - d, n)
            for c in range(3):
                table[source, r, c : c + 1, :] = sent_velocity(sent, n, d, r, c)
    out[...] = jnp.zeros_like(out)
    rank = ranks(owner, voxel.shape[0])
    one, zero = BF16(1), BF16(0)
    for g in range(voxel.shape[0]):
        index = voxel[g : g + 1, :]
        lanes = jnp.where(one_hot(index & 255, 256), one, zero)
        at_row = one_hot(index >> 8, out.shape[1])
        values = table[owner[g], rank[g]]
        lanes2 = jnp.concatenate([lanes, lanes], axis=1)
        for c in range(3):
            high, low = split(values[c : c + 1, :])
            left = jnp.concatenate(
                [jnp.where(at_row, high, zero), jnp.where(at_row, low, zero)], axis=1
            )
            out[c] += lax.dot_general(
                left, lanes2, (((1,), (1,)), ((), ())), preferred_element_type=F32
            )
        out[3] += lax.dot_general(
            jnp.where(at_row, one, zero), lanes, (((1,), (1,)), ((), ())), preferred_element_type=F32
        )
        beside(g)


def found_flow(voxel, flow, layers, field, store):
    patches, beads = voxel.shape
    rows = len(layers) * ROWS
    for c in range(3):
        for i, x in enumerate(layers):
            high, low = split(flow[c, x])
            field[c * rows + i * ROWS : c * rows + (i + 1) * ROWS, 0:256] = high
            field[c * rows + i * ROWS : c * rows + (i + 1) * ROWS, 256:512] = low
    place = lax.broadcasted_iota(I32, (rows, beads), 0)
    step = (layers[1] - layers[0] - 1) * ROWS
    place = place + layers[0] * ROWS + jnp.where(place >= ROWS, step, 0)
    one, zero = BF16(1), BF16(0)
    for g in range(patches):
        index = voxel[g : g + 1, :]
        lanes = jnp.where(one_hot(index & 255, 256), one, zero)
        lanes2 = jnp.concatenate([lanes, lanes], axis=0)
        at_row = place == (index >> 8)
        found = jnp.dot(field[...], lanes2, preferred_element_type=F32)
        for c in range(3):
            part = jnp.where(at_row, found[c * rows : (c + 1) * rows], 0.0)
            store(g, c, jnp.sum(part, axis=0, keepdims=True))


def field_kernel(total, flow, field):
    for x in range(field.shape[1]):
        rows = slice(x * ROWS, (x + 1) * ROWS)
        number = 10.0 * total[3, rows, :]
        for c in range(3):
            field[c, x] = 0.5 * total[c, rows, :] - number * flow[c, x]


def final_kernel(n, per, pos, base, *refs):
    flows, new_pos, new_vel = refs[:n][::-1], refs[n], refs[n + 1]
    me = lax.axis_index("xs")
    for d in range(n):
        source = me ^ d
        for r in range(per):
            at = pl.ds(source * per + r, 1)
            for c in range(3):
                speed = base[c, at, :] + 10.0 * flows[d][r * 3 + c : r * 3 + c + 1, :]
                new_vel[c, at, :] = speed
                new_pos[c, at, :] = pos[c, at, :] + 0.04 * speed


def shift(value, axis, by):
    n = lax.axis_size(axis)
    return lax.ppermute(value, axis, [(i, (i + by) % n) for i in range(n)])


def swap(value, axis, by):
    n = lax.axis_size(axis)
    return lax.ppermute(value, axis, [(i, i ^ by) for i in range(n)])


def pair_call(begin, end, pair_tiles, vel, rows, cols, left, right, noise, given, after):
    tile = noise.shape[-1]
    return call(
        functools.partial(pair_kernel, begin, end),
        [pair_tiles, vel, rows, cols, left, right, noise] + given,
        jax.ShapeDtypeStruct(vel.shape, F32),
        "pair_forces",
        cost(1000, 1000),
        after=after,
        specs={0: SMEM_SPEC},
        out_specs=VMEM_SPEC,
        input_output_aliases={7: 0} if given else {},
        scratch_shapes=[
            pltpu.VMEM(((end - begin) * noise.shape[1], tile, tile), F32),
            pltpu.VMEM(((end - begin) * noise.shape[1], tile, tile), F32),
            pltpu.VMEM((end - begin, cols.shape[2], 3, 8, tile), F32),
        ],
    )


def per_device(
    populations, fluid_mask, patch_voxel, patch_owner, positions, velocities, pair_tiles, pair_noise
):
    n = lax.axis_size("xs")
    patches, beads = patch_voxel.shape
    per = patches // n
    nx = populations.shape[1]
    lanes = populations.shape[3]
    tiles = beads // 128
    arr = lambda *shape: jax.ShapeDtypeStruct(shape, F32)
    ints = lambda *shape: jax.ShapeDtypeStruct(shape, I32)
    vmem, dma = pltpu.VMEM, pltpu.SemaphoreType.DMA
    positions = jnp.transpose(positions, (1, 0, 2))
    velocities = jnp.transpose(velocities, (1, 0, 2))
    pair_tiles = jnp.transpose(pair_tiles, (0, 2, 1))

    post, fwd, bwd, up, down, *others = call(
        functools.partial(collide_kernel, n, per, nx),
        [in_hbm(value) for value in (populations, fluid_mask, velocities)],
        [arr(19, nx, PAD, lanes), arr(384, lanes), arr(384, lanes)]
        + [arr(nx, 32, lanes)] * 2
        + [arr(16, lanes)] * (n - 3),
        "collide_first",
        cost(3_000_000_000, 11_000_000),
        specs={i: ANY_SPEC for i in range(3)},
        out_specs=[VMEM_SPEC] * (n + 2),
        scratch_shapes=[
            vmem((nx, 19, ROWS, lanes), F32),
            vmem((nx, ROWS, lanes), I32),
            vmem(velocities.shape, F32),
            dma((2 * nx,)),
            dma((2,)),
        ],
    )
    before = shift(fwd, "ax", 1)
    after = shift(bwd, "ax", -1)
    layouts = call(
        spread_beads,
        [positions, velocities],
        [
            arr(patches, 3, tiles, 8, 128),
            arr(patches, 3, tiles, 128, 128),
            jax.ShapeDtypeStruct((patches, tiles, 128, 48), BF16),
            jax.ShapeDtypeStruct((patches, tiles, 48, 128), BF16),
        ],
        "bead_layouts",
        cost(1000, 1000),
        after=[down],
        out_specs=[VMEM_SPEC] * 4,
    )
    below = shift(up, "xs", 1)
    above = shift(down, "xs", -1)
    sent = [below] + [shift(other, "xs", d + 2) for d, other in enumerate(others)] + [above]

    cuts = (patches * 5 // 8, patches * 6 // 8)
    bead_args = (pair_tiles, velocities, *layouts, pair_noise)
    base = pair_call(0, cuts[0], *bead_args, [], [down])

    post, edge_fwd, edge_bwd, flags = call(
        functools.partial(edges_kernel, n, nx),
        [post, fluid_mask, below, above],
        [arr(*post.shape), arr(16, lanes), arr(16, lanes), ints(nx, PAD, lanes)],
        "edges",
        cost(1000, 1000),
        after=[base],
        out_specs=[VMEM_SPEC] * 4,
        input_output_aliases={0: 0},
    )
    edge_before = shift(edge_fwd, "ax", 1)
    edge_after = shift(edge_bwd, "ax", -1)

    post2, bits = call(
        functools.partial(middle_kernel, nx),
        [post, flags],
        [arr(19, nx, PAD, lanes), ints(nx, 72, lanes)],
        "middle_layers",
        cost(1000, 1000),
        out_specs=[VMEM_SPEC] * 2,
    )
    def outer(first, face, edge, post2, bits, after):
        return call(
            functools.partial(outer_kernel, nx, first),
            [post, flags, face, edge, post2, bits],
            [arr(*post2.shape), ints(*bits.shape), arr(328, lanes)],
            "first_layer" if first else "last_layer",
            cost(1000, 1000),
            after=after,
            out_specs=[VMEM_SPEC] * 3,
            input_output_aliases={4: 0, 5: 1},
            scratch_shapes=[vmem((5, PAD, lanes), F32), vmem((PAD, lanes), I32)],
        )

    base = pair_call(cuts[0], cuts[1], *bead_args, [base], [flags])
    post2, bits, bwd2 = outer(True, before, edge_before, post2, bits, [base, after, edge_after] + sent[1:-1])
    after2 = shift(bwd2, "ax", -1)
    post2, bits, fwd2 = outer(False, after, edge_after, post2, bits, [])
    before2 = shift(fwd2, "ax", 1)

    out, flow, part = call(
        functools.partial(final_middle_kernel, nx),
        [post2, bits, patch_voxel],
        [arr(*populations.shape), arr(3, nx, ROWS, lanes), arr(patches, 8, beads)],
        "final_middle",
        cost(1000, 1000),
        after=[fwd2],
        out_specs=[ANY_SPEC, VMEM_SPEC, VMEM_SPEC],
        scratch_shapes=[
            vmem((nx - 2, 19, ROWS, lanes), F32),
            vmem((3 * (nx - 2) * ROWS, 2 * lanes), BF16),
            dma((nx - 2,)),
        ],
    )
    last_pairs = (patches - cuts[1]) * pair_noise.shape[1]
    total, base = call(
        functools.partial(sums_and_pairs_kernel, n, per, cuts[1], patches),
        [patch_owner, patch_voxel, velocities] + sent + list(bead_args) + [base],
        [arr(4, nx * ROWS, lanes), arr(*velocities.shape)],
        "bead_sums",
        cost(1000, 1000),
        after=[fwd2],
        specs={0: SMEM_SPEC, n + 2: SMEM_SPEC},
        out_specs=[VMEM_SPEC] * 2,
        input_output_aliases={n + 9: 1},
        scratch_shapes=[
            vmem((n, per, 8, beads), F32),
            vmem((last_pairs, 128, 128), F32),
            vmem((last_pairs, 128, 128), F32),
            vmem((patches - cuts[1], tiles, 3, 8, 128), F32),
        ],
    )
    out, flow, *flows = call(
        functools.partial(final_outer_kernel, n, per, nx),
        [out, flow, post2, bits, after2, before2, patch_voxel, patch_owner, part],
        [arr(*populations.shape), arr(*flow.shape)] + [arr(8, beads)] * n,
        "final_outer",
        cost(1000, 1000),
        after=[total, base],
        specs={0: ANY_SPEC, 7: SMEM_SPEC},
        out_specs=[ANY_SPEC] + [VMEM_SPEC] * (n + 1),
        input_output_aliases={0: 0, 1: 1},
        scratch_shapes=[
            vmem((2, 5, PAD, lanes), F32),
            vmem((2, 19, ROWS, lanes), F32),
            vmem((patches, 8, beads), F32),
            vmem((3 * 2 * ROWS, 2 * lanes), BF16),
            dma((2,)),
        ],
    )
    sent_flows = [flows[0]] + [swap(flows[d], "xs", d) for d in range(1, n)]
    field = call(
        field_kernel,
        [total, flow],
        arr(3, nx, ROWS, lanes),
        "drag_field",
        cost(1000, 1000),
        after=[flows[1]],
        out_specs=VMEM_SPEC,
    )
    new_pos, new_vel = call(
        functools.partial(final_kernel, n, per),
        [positions, base] + sent_flows[::-1],
        [arr(*positions.shape)] * 2,
        "bead_update",
        cost(1000, 1000),
        out_specs=[VMEM_SPEC] * 2,
    )
    return out, jnp.transpose(new_pos, (1, 0, 2)), jnp.transpose(new_vel, (1, 0, 2)), field


def solution(mesh):
    return jax.shard_map(
        per_device,
        mesh=mesh,
        in_specs=(
            P(None, "ax", "xs", None),
            P("ax", "xs", None),
            P(("ax", "xs"), None),
            P(("ax", "xs")),
            P(("ax", "xs"), None, None),
            P(("ax", "xs"), None, None),
            P(("ax", "xs"), None, None),
            P(("ax", "xs"), None, None, None),
        ),
        out_specs=(
            P(None, "ax", "xs", None),
            P(("ax", "xs"), None, None),
            P(("ax", "xs"), None, None),
            P(None, "ax", "xs", None),
        ),
        check_vma=False,
    )
```
